256 devices in a mesh: ens: 4 (over z_lo), space: 64 (over z_hi, x, y, core).
Axes of the slice: x: 4, y: 4, z: 8 (z_hi: 2, z_lo: 4; z = z_hi * 4 + z_lo), core: 2. Of those that a mesh axis runs over, the one named last changes fastest.
Arguments:
- latent: bfloat16 [8, 8192, 1024], P('ens', 'space'), may hold values from -6 to 6
- src_weight: bfloat16 [1024, 1024], replicated, may hold values from -0.1875 to 0.1875
- decoder_projection: bfloat16 [1024, 100], replicated, may hold values from -0.1875 to 0.1875
- verifying_truth: float32 [100, 16384], P(None, 'space'), may hold values from -3 to 3
- area_weight: float32 [16384], P('space'), may hold values from 0.5 to 4
- var_weight: float32 [100], replicated, may hold values from 0.5 to 4
- edge_src: int32 [128, 512], P('space'), may hold values from 0 to 383, as said below
- edge_dst: int32 [128, 512], P('space'), may hold values from 0 to 127
- edge_weight: float32 [128, 512], P('space'), may hold values from 0.2 to 1
- edge_count: int32 [128], P('space'), may hold values from 170 to 512, as said below
Outputs:
- score_field: float32 [100, 16384], P(None, 'space')
- grad_latent: bfloat16 [8, 8192, 1024], P('ens', 'space')
- grad_src: float32 [1024, 1024], P('space')
- grad_out: float32 [1024, 100], P('space')
The draws below stay inside these ranges and needn't reach their ends.
Inputs may be any that keep to these rules, and one draw needn't show every extreme that they name: `edge_src`: rows of a device's extended latent rows: first the last 128 nodes of the previous index of space (wrapping around), then its own 128, then the first 128 of the next. Block b of a device (b = t mod 2) reads rows b * 64 to b * 64 + 128 / 2 + 2 * 128 - 1. `edge_count`: slots from this count on are padding.
All inputs are finite; a program needn't handle non-finite values.
Results may differ from the reference program's by a relative error of at most 0.015.
The reference program's roundings to bfloat16 on the way count: a program that leaves them out, or rounds other values in their place, can miss the bound.
Values may be sent and summed in bfloat16 or wider, within the bound.
No kernel may reach another device: no remote copies, remote signals or barrier semaphores. Data moves between devices by JAX's collectives and lax.ppermute only.
A program may use at most 64 MiB of HBM per device.

```python
import math
import jax
import jax.numpy as jnp
from jax import lax

D = 1024
PREDICTED_VARS = 100
HID_DEV = 128
LOCATIONS_EACH = 256
HALO = 128
BLK = 128
SLOTS = 512
REALIZATIONS = 8
HIDDEN_SIZE = 8192
LOCATION_TALLY = 16384
NBLK = 2
TOTAL_BLK = 128
N_SPACE = 64


def draw_edge_src(key, part):
    key = jax.random.fold_in(key, 11)
    stride = HID_DEV // NBLK
    extent = stride + 2 * HALO
    offsets = jax.random.randint(key, (TOTAL_BLK, SLOTS), 0, extent)
    offsets = offsets.at[:, 0].set(0).at[:, 1].set(extent - 1)
    within = jnp.arange(TOTAL_BLK, dtype=jnp.int32) % NBLK
    return (within[:, None] * stride + offsets).astype(jnp.int32)


def draw_edge_count(key, part):
    key = jax.random.fold_in(key, 23)
    counts = jax.random.randint(key, (TOTAL_BLK,), SLOTS // 3, SLOTS + 1)
    return counts.at[0].set(SLOTS).at[1].set(SLOTS // 3).astype(jnp.int32)


def with_ends(entries, rng, low, high):
    shape = entries.shape
    spot = [jax.random.randint(jax.random.fold_in(rng, axis), (), 0, shape[axis]) for axis in range(len(shape))]
    entries = entries.at[tuple(spot)].set(low)
    longest = shape.index(max(shape))
    spot[longest] = (spot[longest] + 1) % shape[longest]
    return entries.at[tuple(spot)].set(high)


def steps_of(stream_key, shape, cuts, smallest, high):
    loudness = 1.0
    for axis_at, blocks in cuts:
        steps = jax.random.uniform(jax.random.fold_in(jax.random.fold_in(stream_key, 6), axis_at), (blocks,), jnp.float32, smallest / len(cuts), high / len(cuts))
        loudness = loudness * jnp.repeat(jnp.exp(steps), shape[axis_at] // blocks).reshape((-1,) + (1,) * (len(shape) - 1 - axis_at))
    return loudness


def scatter_about(stream_key, shape, width, bound, cuts=(), held_as=jnp.bfloat16):
    array = jax.random.normal(stream_key, shape, jnp.float32) * width
    if len(cuts) > 0:
        array = steps_of(stream_key, shape, cuts, -0.22, 0.18) * array
    return jnp.clip(array, min=-bound, max=bound).astype(held_as)


def setup_inputs(seed: int = 0) -> dict:
    splits = jax.random.split(jax.random.key(seed), 11)
    return {
        "latent": scatter_about(splits[0], (REALIZATIONS, HIDDEN_SIZE, D), 1.0, 6.0, ((0, 4), (1, 64))),
        "src_weight": scatter_about(splits[1], (D, D), D ** -0.5, 0.1875),
        "decoder_projection": scatter_about(splits[2], (D, PREDICTED_VARS), D ** -0.5, 0.1875),
        "verifying_truth": scatter_about(splits[3], (PREDICTED_VARS, LOCATION_TALLY), 0.5, 3.0, ((1, 64),), jnp.float32),
        "area_weight": jnp.clip(jnp.exp(math.log(4.0) - 2.0794415 * jax.random.uniform(splits[4], (LOCATION_TALLY,), jnp.float32) ** steps_of(splits[4], (LOCATION_TALLY,), ((0, 64),), -0.2, 0.2)), 0.5, 4.0),
        "var_weight": jnp.clip(jnp.exp(jax.random.uniform(splits[5], (PREDICTED_VARS,), jnp.float32, math.log(0.5), math.log(4.0))), 0.5, 4.0),
        "edge_src": draw_edge_src(jax.random.fold_in(splits[10], 71), 0),
        "edge_dst": with_ends(jax.random.randint(splits[7], (TOTAL_BLK, SLOTS), 0, BLK), jax.random.fold_in(splits[7], 1), 0, BLK - 1).astype(jnp.int32),
        "edge_weight": jnp.clip(jnp.exp(math.log(1.0) - 1.609438 * jax.random.uniform(splits[8], (TOTAL_BLK, SLOTS), jnp.float32) ** steps_of(splits[8], (TOTAL_BLK, SLOTS), ((0, 64),), -0.2, 0.2)), 0.2, 1.0),
        "edge_count": draw_edge_count(jax.random.fold_in(splits[10], 71), 0),
    }


ALPHA = 0.95
DELTA = 0.05

def smooth_abs(distance):
    return jnp.sqrt(distance * distance + DELTA * DELTA)

def smoothed_signum(distance):
    return distance / jnp.sqrt(distance * distance + DELTA * DELTA)

def edge_matrix(edge_dst, edge_weight, edge_count):
    slot_ids = jnp.arange(edge_dst.shape[-1], dtype=jnp.int32)
    is_valid = slot_ids[None, :] < edge_count[:, None]
    edge_coefs = jnp.where(is_valid, edge_weight, 0.0).astype(jnp.bfloat16)
    points = jnp.arange(BLK, dtype=jnp.int32)
    return jnp.where(edge_dst[:, None, :] == points[None, :, None], edge_coefs[:, None, :], jnp.zeros((), jnp.bfloat16))

def crps_score(collected_sequence, verifying_truth):
    realization_number = len(collected_sequence)
    fair_eps = (1.0 - ALPHA) / realization_number
    couple_factor = (1.0 - fair_eps) / (2.0 * realization_number * (realization_number - 1))
    skill_sum = smooth_abs(collected_sequence[0] - verifying_truth)
    for realization_position in range(1, realization_number):
        skill_sum = skill_sum + smooth_abs(collected_sequence[realization_position] - verifying_truth)
    spread = jnp.zeros_like(skill_sum)
    for realization_position in range(realization_number):
        for other_number in range(realization_position + 1, realization_number):
            spread = spread + smooth_abs(collected_sequence[realization_position] - collected_sequence[other_number])
    return skill_sum / realization_number - couple_factor * 2.0 * spread

def realization_adjoint(local_prediction, collected_sequence, verifying_truth, multiplier_array):
    realization_number = len(collected_sequence)
    fair_eps = (1.0 - ALPHA) / realization_number
    couple_factor = (1.0 - fair_eps) / (2.0 * realization_number * (realization_number - 1))
    mutual_difference_sum = jnp.zeros_like(local_prediction)
    for companion_realization in collected_sequence:
        mutual_difference_sum = mutual_difference_sum + smoothed_signum(local_prediction - companion_realization)
    return multiplier_array * (smoothed_signum(local_prediction - verifying_truth) / realization_number - 2.0 * couple_factor * mutual_difference_sum)

def reference(latent, src_weight, decoder_projection, verifying_truth, area_weight, var_weight, edge_src, edge_dst, edge_weight, edge_count):
    extent = HID_DEV + 2 * HALO
    project = jnp.einsum('mnd,de->mne', latent.astype(jnp.float32), src_weight.astype(jnp.float32)).astype(jnp.bfloat16)
    sources = edge_src.reshape(N_SPACE, NBLK, SLOTS)
    targets = edge_dst.reshape(N_SPACE, NBLK, SLOTS)
    coefs_all = edge_weight.reshape(N_SPACE, NBLK, SLOTS)
    counts = edge_count.reshape(N_SPACE, NBLK)

    def shard_hidden(partition_position):
        row_ids = (partition_position * HID_DEV - HALO + jnp.arange(extent, dtype=jnp.int32)) % HIDDEN_SIZE
        matrix = edge_matrix(targets[partition_position], coefs_all[partition_position], counts[partition_position])
        global_rows = row_ids[sources[partition_position]]
        picked = project[:, global_rows]
        summed = jnp.einsum('bps,mbsd->mbpd', matrix.astype(jnp.float32), picked.astype(jnp.float32))
        return (matrix, global_rows, summed.reshape(REALIZATIONS, LOCATIONS_EACH, D))

    def partitioned_prediction(partition_position):
        summed = shard_hidden(partition_position)[2]
        latent_activation = jax.nn.gelu(summed).astype(jnp.bfloat16)
        return jnp.einsum('uyf,fc->ucy', latent_activation.astype(jnp.float32), decoder_projection.astype(jnp.float32))
    prediction_array = lax.map(partitioned_prediction, jnp.arange(N_SPACE, dtype=jnp.int32))
    realization_prediction = prediction_array.transpose(1, 2, 0, 3).reshape(REALIZATIONS, PREDICTED_VARS, LOCATION_TALLY)
    multiplier_array = var_weight[:, None] * area_weight[None, :]
    collected_sequence = [realization_prediction[realization_position] for realization_position in range(REALIZATIONS)]
    score_field = crps_score(collected_sequence, verifying_truth)
    prediction_adjoint = jnp.stack([realization_adjoint(local_prediction, collected_sequence, verifying_truth, multiplier_array) for local_prediction in collected_sequence]).astype(jnp.bfloat16)

    def backward(partition_position, carry):
        accumulated, out_sum = carry
        matrix, global_rows, summed = shard_hidden(partition_position)
        latent_activation, gelu_back = jax.vjp(jax.nn.gelu, summed)
        latent_activation = latent_activation.astype(jnp.bfloat16)
        adjoint_piece = lax.dynamic_slice_in_dim(prediction_adjoint, partition_position * LOCATIONS_EACH, LOCATIONS_EACH, 2)
        out_sum = out_sum + jnp.einsum('rvs,rhv->sh', latent_activation.astype(jnp.float32), adjoint_piece.astype(jnp.float32))
        hidden_grad = jnp.einsum('bhr,fh->brf', adjoint_piece.astype(jnp.float32), decoder_projection.astype(jnp.float32))
        summed_grad = gelu_back(hidden_grad)[0].astype(jnp.bfloat16).reshape(REALIZATIONS, NBLK, BLK, D)
        row_grads = jnp.einsum('bps,mbpd->mbsd', matrix.astype(jnp.float32), summed_grad.astype(jnp.float32))
        accumulated = accumulated.at[:, global_rows].add(row_grads)
        return (accumulated, out_sum)
    initial = (jnp.zeros((REALIZATIONS, HIDDEN_SIZE, D), jnp.float32), jnp.zeros((D, PREDICTED_VARS), jnp.float32))
    accumulated, out_sum = lax.fori_loop(0, N_SPACE, backward, initial)
    project_grad = accumulated.astype(jnp.bfloat16)
    grad_latent = jnp.einsum('mne,de->mnd', project_grad.astype(jnp.float32), src_weight.astype(jnp.float32)).astype(jnp.bfloat16)
    scaling = 1.0 / math.sqrt(REALIZATIONS * LOCATION_TALLY)
    grad_src = jnp.einsum('mnd,mne->de', latent.astype(jnp.float32), project_grad.astype(jnp.float32)) * scaling
    grad_out = out_sum * scaling
    return (score_field, grad_latent, grad_src, grad_out)
```

```python
import math

import jax
import jax.numpy as jnp
from jax import lax
from jax.sharding import PartitionSpec as P

HALO = 128
BLK = 128
ALPHA = 0.95
DELTA = 0.05
SPACE = ("zhi", "x", "y", "core")
QMAX = 32000.0


def smooth_abs(distance):
    return jnp.sqrt(distance * distance + DELTA * DELTA)


def smoothed_signum(distance):
    return distance * lax.rsqrt(distance * distance + DELTA * DELTA)


def edge_matrix(edge_dst, edge_weight, edge_count):
    slot_ids = jnp.arange(edge_dst.shape[-1], dtype=jnp.int32)
    is_valid = slot_ids[None, :] < edge_count[:, None]
    edge_coefs = jnp.where(is_valid, edge_weight, 0.0).astype(jnp.bfloat16)
    points = jnp.arange(BLK, dtype=jnp.int32)
    return jnp.where(
        edge_dst[:, None, :] == points[None, :, None],
        edge_coefs[:, None, :],
        jnp.zeros((), jnp.bfloat16),
    )


def pair_factor(members):
    fair_eps = (1.0 - ALPHA) / members
    return (1.0 - fair_eps) / (2.0 * members * (members - 1))


def crps_score(collected, truth):
    members = len(collected)
    skill = sum(smooth_abs(f - truth) for f in collected)
    spread = jnp.zeros_like(skill)
    for m in range(members):
        for o in range(m + 1, members):
            spread = spread + smooth_abs(collected[m] - collected[o])
    return skill / members - pair_factor(members) * 2.0 * spread


def member_adjoint(own, collected, truth, multiplier):
    members = len(collected)
    mutual = sum(smoothed_signum(own - f) for f in collected)
    return multiplier * (
        smoothed_signum(own - truth) / members - 2.0 * pair_factor(members) * mutual
    )


def make_body(count):
    odd_pairs = [(i, (i + 1) % count if i % 2 else (i - 1) % count) for i in range(count)]
    far = [p for p in odd_pairs if abs(p[0] - p[1]) > 1 or p[0] // 32 != p[1] // 32]
    near = [p for p in odd_pairs if p not in far]
    swap = [(0, 1), (1, 0)]

    def body(
        latent, src_weight, decoder_projection, truth, area_weight, var_weight,
        edge_src, edge_dst, edge_weight, edge_count,
    ):
        local = latent.shape[0]
        rows = latent.shape[1]
        ens = lax.axis_size("ens")
        members = local * ens
        core = lax.axis_index("core")
        depth = latent.shape[2]
        nvar = decoder_projection.shape[1]
        points = truth.shape[1]
        grid_all = points * count

        odd_lat = lax.ppermute(latent, SPACE, odd_pairs)
        core_lat = lax.ppermute(latent, "core", swap)
        ext = jnp.concatenate([latent, core_lat, odd_lat], axis=1)
        window = ext.shape[1]

        side = edge_src // HALO
        left = jnp.where(core == 0, 2 * HALO, HALO)
        right = jnp.where(core == 0, HALO, 2 * HALO)
        place = jnp.where(side == 0, left, jnp.where(side == 1, 0, right))
        source = edge_src - side * HALO + place
        matrix = edge_matrix(edge_dst, edge_weight, edge_count)
        hot = (source[:, :, None] == jnp.arange(window, dtype=jnp.int32)).astype(jnp.bfloat16)
        coef = jnp.einsum("bps,bsr->bpr", matrix, hot, preferred_element_type=jnp.float32)
        coef = coef.reshape(points, window)
        high = coef.astype(jnp.bfloat16)
        low = (coef - high.astype(jnp.float32)).astype(jnp.bfloat16)

        def gather(values):
            return jnp.einsum(
                "pr,mrd->mpd", high, values, preferred_element_type=jnp.float32
            ) + jnp.einsum("pr,mrd->mpd", low, values, preferred_element_type=jnp.float32)

        project = jnp.einsum(
            "mnd,de->mne", ext, src_weight, preferred_element_type=jnp.float32
        ).astype(jnp.bfloat16)
        summed = gather(project)
        hidden, gelu_back = jax.vjp(jax.nn.gelu, summed)
        hidden = hidden.astype(jnp.bfloat16)
        forecast = jnp.einsum(
            "mpd,dv->mvp", hidden, decoder_projection, preferred_element_type=jnp.float32
        )
        largest = jnp.max(jnp.abs(forecast), axis=2, keepdims=True)
        power = jnp.ceil(jnp.log2(jnp.maximum(largest, 1e-30)) + 1e-3)
        coded = jnp.round(forecast * (jnp.exp2(-power) * QMAX)).astype(jnp.int16)
        power16 = jnp.broadcast_to(power, (local, nvar, 128)).astype(jnp.int16)
        coded = jnp.concatenate([coded, power16], axis=2)
        everyone = lax.all_gather(coded, "ens", axis=0, tiled=True)
        decoded = everyone[:, :, :points].astype(jnp.float32) * (
            jnp.exp2(everyone[:, :, points : points + 1].astype(jnp.float32)) * (1.0 / QMAX)
        )
        collected = [decoded[m] for m in range(members)]
        at = lax.axis_index("ens") * local
        own = lax.dynamic_slice_in_dim(decoded, at, local, 0)
        multiplier = var_weight[:, None] * area_weight[None, :]
        adjoint = jnp.stack(
            [member_adjoint(own[m], collected, truth, multiplier) for m in range(local)]
        ).astype(jnp.bfloat16)
        score = crps_score(collected, truth)

        agg = gather(ext).astype(jnp.bfloat16)
        out_sum = jnp.einsum("mpd,mvp->dv", hidden, adjoint, preferred_element_type=jnp.float32)
        hidden_grad = jnp.einsum(
            "mvp,dv->mpd", adjoint, decoder_projection, preferred_element_type=jnp.float32
        )
        summed_grad = gelu_back(hidden_grad)[0].astype(jnp.bfloat16)
        src_sum = jnp.einsum("mpd,mpe->de", agg, summed_grad, preferred_element_type=jnp.float32)

        partial = jnp.concatenate(
            [src_sum, jnp.pad(out_sum, ((0, 0), (0, 128 - nvar)))], axis=1
        ).astype(jnp.bfloat16)
        cols = partial.shape[1]
        per = depth // count
        partial = partial.reshape(2, 16, 2, per, cols)
        mine = lax.dynamic_index_in_dim(partial, core, 2, keepdims=False)
        theirs = lax.dynamic_index_in_dim(partial, 1 - core, 2, keepdims=False)
        theirs = lax.ppermute(theirs, "core", swap)

        row_grad = jnp.einsum(
            "pr,mpd->mrd", high, summed_grad, preferred_element_type=jnp.float32
        ) + jnp.einsum("pr,mpd->mrd", low, summed_grad, preferred_element_type=jnp.float32)
        send = row_grad[:, rows:].astype(jnp.bfloat16)
        far_grad = lax.ppermute(send[:, HALO:], SPACE, far)

        half = (mine.astype(jnp.float32) + theirs.astype(jnp.float32)).astype(jnp.bfloat16)
        half = half.transpose(1, 0, 2, 3)
        got = lax.all_to_all(half, ("x", "y"), 0, 0, tiled=True)
        plane = jnp.sum(got.astype(jnp.float32), axis=0).astype(jnp.bfloat16)
        near_grad = lax.ppermute(send[:, HALO:], SPACE, near)
        core_grad = lax.ppermute(send[:, :HALO], "core", swap)
        copies = jnp.broadcast_to(plane[:, None], (2, ens, per, cols)).reshape(2 * ens, per, cols)
        got = lax.all_to_all(copies, ("zhi", "ens"), 0, 0, tiled=True)
        total = jnp.sum(got.astype(jnp.float32), axis=0) * (1.0 / math.sqrt(members * grid_all))

        own_grad = (
            row_grad[:, :rows]
            + core_grad.astype(jnp.float32)
            + far_grad.astype(jnp.float32)
            + near_grad.astype(jnp.float32)
        ).astype(jnp.bfloat16)
        grad_latent = jnp.einsum(
            "mne,de->mnd", own_grad, src_weight, preferred_element_type=jnp.float32
        ).astype(jnp.bfloat16)
        return score, grad_latent, total[:, :depth], total[:, depth : depth + nvar]

    return body


def solution(mesh):
    fine = jax.sharding.Mesh(
        mesh.devices.reshape(mesh.devices.shape[0], 2, 4, 4, 2), ("ens",) + SPACE
    )
    return jax.shard_map(
        make_body(mesh.devices.shape[1]),
        mesh=fine,
        in_specs=(
            P("ens", SPACE, None), P(), P(), P(None, SPACE), P(SPACE), P(),
            P(SPACE, None), P(SPACE, None), P(SPACE, None), P(SPACE),
        ),
        out_specs=(P(None, SPACE), P("ens", SPACE, None), P(SPACE, None), P(SPACE, None)),
        check_vma=False,
    )
```

```python
import functools
import math

import jax
import jax.numpy as jnp
from jax import lax
from jax.experimental import pallas as pl
from jax.experimental.pallas import tpu as pltpu
from jax.sharding import PartitionSpec as P

HALO = 128
BLK = 128
ALPHA = 0.95
DELTA = 0.05
SPACE = ("zhi", "x", "y", "core")
QMAX = 32000.0
VPAD = 128
VROWS = 112
VUSE = 104
TILE = 256
GELU_C = math.sqrt(2.0 / math.pi)
MIB = 1 << 20
F32 = jnp.float32
BF16 = jnp.bfloat16


def dot(a, b):
    return jnp.dot(a, b, preferred_element_type=F32)


def dot_nt(a, b):
    return lax.dot_general(a, b, (((1,), (1,)), ((), ())), preferred_element_type=F32)


def vmem(count):
    return [pl.BlockSpec(memory_space=pltpu.VMEM)] * count


def smem(count):
    return [pl.BlockSpec(memory_space=pltpu.SMEM)] * count


def cost(flops, nbytes):
    return pl.CostEstimate(flops=flops, bytes_accessed=nbytes, transcendentals=0)


def params(mib):
    return pltpu.CompilerParams(vmem_limit_bytes=mib * MIB)


def pair_factor(members):
    fair_eps = (1.0 - ALPHA) / members
    return (1.0 - fair_eps) / (2.0 * members * (members - 1))


def smooth_abs(distance):
    return jnp.sqrt(distance * distance + DELTA * DELTA)


def signum(distance):
    return distance * lax.rsqrt(distance * distance + DELTA * DELTA)


def prepare_kernel(
    where_ref, count_ref, src_ref, dst_ref, wt_ref, lat_ref, clat_ref, w_ref,
    cf_ref, cfo_ref, cft_ref, part_ref, x_ref,
):
    core = where_ref[0]
    slots = src_ref.shape[1]
    window = cf_ref.shape[1] // 2
    points = cf_ref.shape[0]
    for b in range(src_ref.shape[0]):
        src = src_ref[b : b + 1, :]
        slot = lax.broadcasted_iota(jnp.int32, (1, slots), 1)
        wt = jnp.where(slot < count_ref[b], wt_ref[b : b + 1, :], 0.0)
        left = 2 * HALO - HALO * core
        right = HALO + HALO * core
        place = jnp.where(
            src < HALO,
            src + left,
            jnp.where(src < 2 * HALO, src - HALO, src - 2 * HALO + right),
        )
        rows = lax.broadcasted_iota(jnp.int32, (window, slots), 0)
        hot = jnp.where(rows == place, 1.0, 0.0).astype(BF16)
        pts = lax.broadcasted_iota(jnp.int32, (BLK, slots), 0)
        mat = jnp.where(pts == dst_ref[b : b + 1, :], wt, 0.0).astype(BF16)
        coef = dot_nt(mat, hot)
        high = coef.astype(BF16)
        low = (coef - high.astype(F32)).astype(BF16)
        at = slice(b * BLK, (b + 1) * BLK)
        cf_ref[at, :window] = high
        cf_ref[at, window:] = low
        cfo_ref[at, :HALO] = high[:, 2 * HALO :]
        cfo_ref[at, HALO:] = low[:, 2 * HALO :]
        coef_t = dot_nt(hot, mat)
        high_t = coef_t.astype(BF16)
        cft_ref[:, b * BLK : (b + 1) * BLK] = high_t
        cft_ref[:, points + b * BLK : points + (b + 1) * BLK] = (
            coef_t - high_t.astype(F32)
        ).astype(BF16)
    local = lat_ref.shape[0]
    for m in range(local):
        x_ref[2 * m * HALO : (2 * m + 1) * HALO, :] = lat_ref[m]
        x_ref[(2 * m + 1) * HALO : (2 * m + 2) * HALO, :] = clat_ref[m]
    x = x_ref[...]
    high = cf_ref[:, : 2 * HALO]
    low = cf_ref[:, window : window + 2 * HALO]
    for j in range(w_ref.shape[1] // TILE):
        at = slice(j * TILE, (j + 1) * TILE)
        p = dot(x, w_ref[:, at]).astype(BF16)
        for m in range(local):
            pm = p[2 * m * HALO : (2 * m + 2) * HALO]
            part_ref[m, :, at] = dot(high, pm) + dot(low, pm)


def forward_kernel(
    odd_ref, w_ref, cfo_ref, part_ref, dpt_ref, summed_ref, hidden_ref, coded_ref, f_ref
):
    j = pl.program_id(0)
    local = part_ref.shape[0]

    @pl.when(j == 0)
    def _():
        f_ref[...] = jnp.zeros_like(f_ref)

    p = dot(odd_ref[...], w_ref[...]).astype(BF16)
    for m in range(local):
        pm = p[m * HALO : (m + 1) * HALO]
        s = part_ref[m] + dot(cfo_ref[...], jnp.concatenate([pm, pm], axis=0))
        summed_ref[m] = s
        t = jnp.tanh(GELU_C * (s + 0.044715 * (s * s * s)))
        h = (0.5 * s * (1.0 + t)).astype(BF16)
        hidden_ref[m] = h
        f_ref[m] += dot_nt(dpt_ref[...], h)

    @pl.when(j == pl.num_programs(0) - 1)
    def _():
        for m in range(local):
            f = f_ref[m]
            largest = jnp.maximum(jnp.max(jnp.abs(f), axis=1, keepdims=True), 1e-30)
            power = jnp.ceil(jnp.log(largest) * (1.0 / math.log(2.0)) + 1e-3)
            power = jnp.broadcast_to(power, (VPAD, VPAD))
            q = f * (jnp.exp2(-power[:, :1]) * QMAX)
            q = jnp.where(q >= 0.0, q + 0.5, q - 0.5)
            row = jnp.concatenate([power.T[:8], jnp.zeros((8, f.shape[1] - VPAD), F32)], axis=1)
            row = jnp.where(row >= 0.0, row + 0.5, row - 0.5)
            code = jnp.concatenate([q[:VUSE], row], axis=0).astype(jnp.int32).astype(jnp.int16)
            for e in range(coded_ref.shape[0]):
                coded_ref[e, m] = code


def factors_kernel(
    where_ref, lat_ref, clat_ref, olat_ref, cf_ref, summed_ref, hidden_ref,
    aggt_ref, hidt_ref, slope_ref, x_ref,
):
    core = where_ref[0]
    window = cf_ref.shape[1] // 2
    depth = lat_ref.shape[2]
    local = lat_ref.shape[0]
    points = cf_ref.shape[0]
    high = cf_ref[:, :window]
    low = cf_ref[:, window:]
    for m in range(local):
        x_ref[:HALO] = lat_ref[m]
        x_ref[HALO : 2 * HALO] = clat_ref[m]
        x_ref[2 * HALO :] = olat_ref[m * HALO : (m + 1) * HALO]
        cols = slice(m * points, (m + 1) * points)
        for j in range(depth // TILE):
            at = slice(j * TILE, (j + 1) * TILE)
            x = x_ref[:, at]
            agg = (dot(high, x) + dot(low, x)).T.astype(BF16)
            hid = hidden_ref[m, :, at].astype(F32).T.astype(BF16)
            for k in range(TILE // 16):
                block = j * (TILE // 16) + k
                zhi, rest = divmod(block, 32)
                xy, c = divmod(rest, 2)
                to = lax.bitwise_xor(core, c) * (depth // 2) + (xy * 32 + zhi * 16)
                to = pl.ds(pl.multiple_of(to, 16), 16)
                aggt_ref[to, cols] = agg[k * 16 : (k + 1) * 16]
                hidt_ref[to, cols] = hid[k * 16 : (k + 1) * 16]
            s = summed_ref[m, :, at]
            t = jnp.tanh(GELU_C * (s + 0.044715 * (s * s * s)))
            slope_ref[m, :, at] = 0.5 * (1.0 + t) + (0.5 * GELU_C) * s * (1.0 - t * t) * (
                1.0 + 3.0 * 0.044715 * (s * s)
            )


def decode(code_ref, index):
    code = code_ref[index].astype(jnp.int32).astype(F32)
    power = jnp.broadcast_to(code[VUSE : VUSE + 1, :VPAD], (VPAD, VPAD)).T
    return code[:VUSE] * (jnp.exp2(power[:VUSE, :1]) * (1.0 / QMAX))


def score_kernel(code_ref, truth_ref, score_ref):
    members = code_ref.shape[0]
    nvar = truth_ref.shape[0]
    collected = [decode(code_ref, m)[:nvar] for m in range(members)]
    truth = truth_ref[...]
    skill = sum(smooth_abs(f - truth) for f in collected)
    spread = jnp.zeros_like(skill)
    for m in range(members):
        for o in range(m + 1, members):
            spread = spread + smooth_abs(collected[m] - collected[o])
    score_ref[...] = skill * (1.0 / members) - (pair_factor(members) * 2.0) * spread


def backward_kernel(
    where_ref, code_ref, truth_ref, var_ref, area_ref, dpt_ref, aggt_ref, hidt_ref, slope_ref,
    mine_ref, theirs_ref, sg_ref, f_ref, sgs_ref,
):
    members = code_ref.shape[0]
    local = slope_ref.shape[0]
    points = slope_ref.shape[1]
    depth = slope_ref.shape[2]
    half = depth // 2
    for m in range(members):
        f_ref[m] = decode(code_ref, m)
    first = where_ref[1] * local
    truth = truth_ref[...]
    multiplier = var_ref[...] * area_ref[...]
    grads = []
    for m in range(local):
        own = f_ref[first + m]
        mutual = sum(signum(own - f_ref[o]) for o in range(members))
        g = multiplier * (
            signum(own - truth) * (1.0 / members) - (2.0 * pair_factor(members)) * mutual
        )
        g = jnp.concatenate([g, jnp.zeros((VPAD - VUSE, points), F32)], axis=0)
        grads.append(g.T.astype(BF16))
    grad = jnp.concatenate(grads, axis=0)
    out = dot(hidt_ref[...], grad).astype(BF16)
    mine_ref[:, depth:] = out[:half]
    theirs_ref[:, depth:] = out[half:]
    aggt = aggt_ref[...]
    for j in range(depth // TILE):
        at = slice(j * TILE, (j + 1) * TILE)
        hg = dot(grad, dpt_ref[:, at])
        for m in range(local):
            s = (hg[m * points : (m + 1) * points] * slope_ref[m, :, at]).astype(BF16)
            sg_ref[m, :, at] = s
            sgs_ref[m * points : (m + 1) * points, :] = s
        part = dot(aggt, sgs_ref[...]).astype(BF16)
        mine_ref[:, at] = part[:half]
        theirs_ref[:, at] = part[half:]


def rows_kernel(cft_ref, sg_ref, own_ref, core_ref, odd_ref):
    points = sg_ref.shape[1]
    high = cft_ref[:, :points]
    low = cft_ref[:, points:]
    for m in range(sg_ref.shape[0]):
        for j in range(sg_ref.shape[2] // TILE):
            at = slice(j * TILE, (j + 1) * TILE)
            s = sg_ref[m, :, at]
            g = dot(high, s) + dot(low, s)
            own_ref[m, :, at] = g[:HALO]
            core_ref[m, :, at] = g[HALO : 2 * HALO].astype(BF16)
            odd_ref[m, :, at] = g[2 * HALO :].astype(BF16)


def plane_kernel(got_ref, out_ref):
    ens = out_ref.shape[1]
    per = out_ref.shape[2]
    total = got_ref[0].astype(F32)
    for k in range(1, got_ref.shape[0]):
        total = total + got_ref[k].astype(F32)
    total = total.astype(BF16)
    for z in range(out_ref.shape[0]):
        for e in range(ens):
            out_ref[z, e] = total[z * per : (z + 1) * per]


def final_kernel(got_ref, src_ref, out_ref, *, scaling):
    total = got_ref[0].astype(F32)
    for k in range(1, got_ref.shape[0]):
        total = total + got_ref[k].astype(F32)
    total = total * scaling
    depth = src_ref.shape[1]
    src_ref[...] = total[:, :depth]
    out_ref[...] = total[:, depth : depth + out_ref.shape[1]]


def latent_kernel(own_ref, core_ref, far_ref, near_ref, w_ref, out_ref, g_ref):
    local = own_ref.shape[0]
    for m in range(local):
        g = (
            own_ref[m]
            + core_ref[m].astype(F32)
            + far_ref[m].astype(F32)
            + near_ref[m].astype(F32)
        )
        g_ref[m * HALO : (m + 1) * HALO] = g.astype(BF16)
    for j in range(w_ref.shape[0] // TILE):
        at = slice(j * TILE, (j + 1) * TILE)
        r = dot_nt(g_ref[...], w_ref[at, :]).astype(BF16)
        for m in range(local):
            out_ref[m, :, at] = r[m * HALO : (m + 1) * HALO]


def shape(dims, dtype):
    return jax.ShapeDtypeStruct(dims, dtype)


def make_body(count):
    odd_pairs = [(i, (i + 1) % count if i % 2 else (i - 1) % count) for i in range(count)]
    far = [p for p in odd_pairs if abs(p[0] - p[1]) > 1 or p[0] // 32 != p[1] // 32]
    near = [p for p in odd_pairs if p not in far]
    swap = [(0, 1), (1, 0)]

    def body(
        latent, src_weight, decoder_projection, truth, area_weight, var_weight,
        edge_src, edge_dst, edge_weight, edge_count,
    ):
        local, rows, depth = latent.shape
        ens = lax.axis_size("ens")
        members = local * ens
        nvar = decoder_projection.shape[1]
        points = truth.shape[1]
        window = rows + 2 * HALO
        per = depth // count
        cols = depth + VPAD
        where = jnp.stack([lax.axis_index("core"), lax.axis_index("ens")]).astype(jnp.int32)

        odd_lat = lax.ppermute(latent, SPACE, odd_pairs).reshape(local * rows, depth)
        core_lat = lax.ppermute(latent, "core", swap)
        dpt = jnp.pad(decoder_projection.T, ((0, VPAD - nvar), (0, 0)))

        cf, cfo, cft, part = pl.pallas_call(
            prepare_kernel,
            out_shape=(
                shape((points, 2 * window), BF16),
                shape((points, 2 * HALO), BF16),
                shape((window, 2 * points), BF16),
                shape((local, points, depth), F32),
            ),
            in_specs=smem(2) + vmem(6),
            out_specs=tuple(vmem(4)),
            scratch_shapes=[pltpu.VMEM((local * 2 * HALO, depth), BF16)],
            compiler_params=params(24),
            cost_estimate=cost(3 * 10**9, 6 * 10**6),
            name="prepare",
        )(where, edge_count, edge_src, edge_dst, edge_weight, latent, core_lat, src_weight)

        steps = depth // TILE
        summed, hidden, coded = pl.pallas_call(
            forward_kernel,
            grid=(steps,),
            out_shape=(
                shape((local, points, depth), F32),
                shape((local, points, depth), BF16),
                shape((ens, local, VROWS, points), jnp.int16),
            ),
            in_specs=[
                pl.BlockSpec((local * rows, depth), lambda j: (0, 0)),
                pl.BlockSpec((depth, TILE), lambda j: (0, j)),
                pl.BlockSpec((points, 2 * HALO), lambda j: (0, 0)),
                pl.BlockSpec((local, points, TILE), lambda j: (0, 0, j)),
                pl.BlockSpec((VPAD, TILE), lambda j: (0, j)),
            ],
            out_specs=(
                pl.BlockSpec((local, points, TILE), lambda j: (0, 0, j)),
                pl.BlockSpec((local, points, TILE), lambda j: (0, 0, j)),
                pl.BlockSpec((ens, local, VROWS, points), lambda j: (0, 0, 0, 0)),
            ),
            scratch_shapes=[pltpu.VMEM((local, VPAD, points), F32)],
            compiler_params=params(24),
            cost_estimate=cost(2 * 10**9, 8 * 10**6),
            name="forward",
        )(odd_lat, src_weight, cfo, part, dpt)

        everyone = lax.all_to_all(coded, "ens", 0, 0, tiled=True)
        everyone = everyone.reshape(members, VROWS, points)

        aggt, hidt, slope = pl.pallas_call(
            factors_kernel,
            out_shape=(
                shape((depth, local * points), BF16),
                shape((depth, local * points), BF16),
                shape((local, points, depth), F32),
            ),
            in_specs=smem(1) + vmem(6),
            out_specs=tuple(vmem(3)),
            scratch_shapes=[pltpu.VMEM((window, depth), BF16)],
            compiler_params=params(24),
            cost_estimate=cost(3 * 10**9, 10 * 10**6),
            name="factors",
        )(where, latent, core_lat, odd_lat, cf, summed, hidden)

        tall = jnp.pad(truth, ((0, VUSE - nvar), (0, 0)))
        var_col = jnp.pad(var_weight, (0, VUSE - nvar)).reshape(VUSE, 1)
        mine, theirs, summed_grad = pl.pallas_call(
            backward_kernel,
            out_shape=(
                shape((depth // 2, cols), BF16),
                shape((depth // 2, cols), BF16),
                shape((local, points, depth), BF16),
            ),
            in_specs=smem(1) + vmem(8),
            out_specs=tuple(vmem(3)),
            scratch_shapes=[
                pltpu.VMEM((members, VUSE, points), F32),
                pltpu.VMEM((local * points, TILE), BF16),
            ],
            compiler_params=params(24),
            cost_estimate=cost(2 * 10**9, 8 * 10**6),
            name="backward",
        )(
            where, everyone, tall, var_col, area_weight.reshape(1, points), dpt,
            aggt, hidt, slope,
        )

        theirs = lax.ppermute(theirs, "core", swap)
        own_rows, core_send, odd_send = pl.pallas_call(
            rows_kernel,
            out_shape=(
                shape((local, rows, depth), F32),
                shape((local, HALO, depth), BF16),
                shape((local, HALO, depth), BF16),
            ),
            in_specs=vmem(2),
            out_specs=tuple(vmem(3)),
            compiler_params=params(16),
            cost_estimate=cost(10**9, 4 * 10**6),
            name="rows",
        )(cft, summed_grad)
        far_grad = lax.ppermute(odd_send, SPACE, far)

        half = (mine.astype(F32) + theirs.astype(F32)).astype(BF16).reshape(16, 2 * per, cols)
        got = lax.all_to_all(half, ("x", "y"), 0, 0, tiled=True)
        near_grad = lax.ppermute(odd_send, SPACE, near)
        core_grad = lax.ppermute(core_send, "core", swap)
        plane = pl.pallas_call(
            plane_kernel,
            out_shape=shape((2, ens, per, cols), BF16),
            in_specs=vmem(1),
            out_specs=vmem(1)[0],
            compiler_params=params(16),
            cost_estimate=cost(10**6, 2 * 10**6),
            name="plane",
        )(got)
        got = lax.all_to_all(plane.reshape(2 * ens, per, cols), ("zhi", "ens"), 0, 0, tiled=True)

        score = pl.pallas_call(
            score_kernel,
            out_shape=shape(truth.shape, F32),
            in_specs=vmem(2),
            out_specs=vmem(1)[0],
            compiler_params=params(16),
            cost_estimate=cost(10**7, 10**6),
            name="score",
        )(everyone, truth)
        grad_latent = pl.pallas_call(
            latent_kernel,
            out_shape=shape(latent.shape, BF16),
            in_specs=vmem(5),
            out_specs=vmem(1)[0],
            scratch_shapes=[pltpu.VMEM((local * rows, depth), BF16)],
            compiler_params=params(16),
            cost_estimate=cost(10**9, 5 * 10**6),
            name="latent",
        )(own_rows, core_grad, far_grad, near_grad, src_weight)

        grad_src, grad_out = pl.pallas_call(
            functools.partial(
                final_kernel, scaling=1.0 / math.sqrt(members * points * count)
            ),
            out_shape=(shape((per, depth), F32), shape((per, nvar), F32)),
            in_specs=vmem(1),
            out_specs=tuple(vmem(2)),
            compiler_params=params(16),
            cost_estimate=cost(10**5, 4 * 10**5),
            name="final",
        )(got)
        return score, grad_latent, grad_src, grad_out

    return body


def solution(mesh):
    fine = jax.sharding.Mesh(
        mesh.devices.reshape(mesh.devices.shape[0], 2, 4, 4, 2), ("ens",) + SPACE
    )
    return jax.shard_map(
        make_body(mesh.devices.shape[1]),
        mesh=fine,
        in_specs=(
            P("ens", SPACE, None), P(), P(), P(None, SPACE), P(SPACE), P(),
            P(SPACE, None), P(SPACE, None), P(SPACE, None), P(SPACE),
        ),
        out_specs=(P(None, SPACE), P("ens", SPACE, None), P(SPACE, None), P(SPACE, None)),
        check_vma=False,
    )
```

```python
import functools
import math

import jax
import jax.numpy as jnp
from jax import lax
from jax.experimental import pallas as pl
from jax.experimental.pallas import tpu as pltpu
from jax.sharding import PartitionSpec as P

HALO = 128
BLK = 128
ALPHA = 0.95
DELTA = 0.05
SPACE = ("zhi", "x", "y", "core")
QMAX = 32000.0
VPAD = 128
VROWS = 112
VUSE = 104
TILE = 256
GELU_C = math.sqrt(2.0 / math.pi)
MIB = 1 << 20
BIG = 56
MID = 24
F32 = jnp.float32
BF16 = jnp.bfloat16


def dot(a, b):
    return jnp.dot(a, b, preferred_element_type=F32)


def dot_nt(a, b):
    return lax.dot_general(a, b, (((1,), (1,)), ((), ())), preferred_element_type=F32)


def smem(count):
    return [pl.BlockSpec(memory_space=pltpu.SMEM)] * count


def cost(flops, nbytes):
    return pl.CostEstimate(flops=flops, bytes_accessed=nbytes, transcendentals=0)


def params(mib):
    return pltpu.CompilerParams(vmem_limit_bytes=mib * MIB)


def whole(*arrays):
    return [
        pl.BlockSpec(a.shape, functools.partial(lambda n, j: (0,) * n, len(a.shape)))
        for a in arrays
    ]


def hbm(count):
    return [pl.BlockSpec(memory_space=pltpu.HBM)] * count


def vmem(count):
    return [pl.BlockSpec(memory_space=pltpu.VMEM)] * count


def start_copy(src, dst, sem):
    copy = pltpu.make_async_copy(src, dst, sem)
    copy.start()
    return copy


def pair_factor(members):
    fair_eps = (1.0 - ALPHA) / members
    return (1.0 - fair_eps) / (2.0 * members * (members - 1))


def smooth_abs(distance):
    square = distance * distance + DELTA * DELTA
    return square * lax.rsqrt(square)


def signum(distance):
    return distance * lax.rsqrt(distance * distance + DELTA * DELTA)


def prepare_kernel(
    where_ref, count_hbm, src_hbm, dst_hbm, wt_hbm, lat_hbm, clat_hbm, w_hbm,
    cf_hbm, cft_hbm, cfo_ref, part_ref,
    count_ref, src_ref, dst_ref, wt_ref, x_ref, w_ref, cf_ref, cft_ref, in_sem, out_sem,
):
    edges = [
        start_copy(src, dst, in_sem.at[k])
        for k, (src, dst) in enumerate(
            ((count_hbm, count_ref), (src_hbm, src_ref), (dst_hbm, dst_ref), (wt_hbm, wt_ref))
        )
    ]
    local = lat_hbm.shape[0]
    inputs = []
    for m in range(local):
        for k, ref in enumerate((lat_hbm, clat_hbm)):
            inputs.append(
                start_copy(
                    ref.at[m],
                    x_ref.at[pl.ds((2 * m + k) * HALO, HALO)],
                    in_sem.at[4 + 2 * m + k],
                )
            )
    inputs.append(start_copy(w_hbm, w_ref, in_sem.at[4 + 2 * local]))
    core = where_ref[0]
    slots = src_ref.shape[1]
    window = cf_ref.shape[1] // 2
    points = cf_ref.shape[0]
    for copy in edges:
        copy.wait()
    for b in range(src_ref.shape[0]):
        src = src_ref[b : b + 1, :]
        slot = lax.broadcasted_iota(jnp.int32, (1, slots), 1)
        wt = jnp.where(slot < count_ref[b], wt_ref[b : b + 1, :], 0.0)
        left = 2 * HALO - HALO * core
        right = HALO + HALO * core
        place = jnp.where(
            src < HALO,
            src + left,
            jnp.where(src < 2 * HALO, src - HALO, src - 2 * HALO + right),
        )
        rows = lax.broadcasted_iota(jnp.int32, (window, slots), 0)
        hot = jnp.where(rows == place, 1.0, 0.0).astype(BF16)
        pts = lax.broadcasted_iota(jnp.int32, (BLK, slots), 0)
        mat = jnp.where(pts == dst_ref[b : b + 1, :], wt, 0.0).astype(BF16)
        coef = dot_nt(mat, hot)
        high = coef.astype(BF16)
        low = (coef - high.astype(F32)).astype(BF16)
        at = slice(b * BLK, (b + 1) * BLK)
        cf_ref[at, :window] = high
        cf_ref[at, window:] = low
        cfo_ref[at, :HALO] = high[:, 2 * HALO :]
        cfo_ref[at, HALO:] = low[:, 2 * HALO :]
        coef_t = dot_nt(hot, mat)
        high_t = coef_t.astype(BF16)
        cft_ref[:, b * BLK : (b + 1) * BLK] = high_t
        cft_ref[:, points + b * BLK : points + (b + 1) * BLK] = (
            coef_t - high_t.astype(F32)
        ).astype(BF16)
    outs = [
        start_copy(cf_ref, cf_hbm, out_sem.at[0]),
        start_copy(cft_ref, cft_hbm, out_sem.at[1]),
    ]
    for copy in inputs:
        copy.wait()
    x = x_ref[...]
    high = cf_ref[:, : 2 * HALO]
    low = cf_ref[:, window : window + 2 * HALO]
    for j in range(w_ref.shape[1] // TILE):
        at = slice(j * TILE, (j + 1) * TILE)
        p = dot(x, w_ref[:, at]).astype(BF16)
        for m in range(local):
            pm = p[2 * m * HALO : (2 * m + 2) * HALO]
            part_ref[m, :, at] = dot(high, pm) + dot(low, pm)
    for copy in outs:
        copy.wait()


def forward_kernel(
    odd_ref, w_ref, cfo_ref, part_ref, dpt_ref, summed_hbm, hidden_hbm, coded_hbm,
    summed_ref, hidden_ref, code_ref, out_sem,
):
    local, points, depth = part_ref.shape
    steps = depth // TILE
    forecast = [jnp.zeros((VPAD, points), F32) for _ in range(local)]
    outs = []
    for j in range(steps):
        at = slice(j * TILE, (j + 1) * TILE)
        p = dot(odd_ref[...], w_ref[:, at]).astype(BF16)
        for m in range(local):
            pm = p[m * HALO : (m + 1) * HALO]
            s = part_ref[m, :, at] + dot(cfo_ref[...], jnp.concatenate([pm, pm], axis=0))
            summed_ref[m, :, at] = s
            t = jnp.tanh(GELU_C * (s + 0.044715 * (s * s * s)))
            h = (0.5 * s * (1.0 + t)).astype(BF16)
            hidden_ref[m, :, at] = h
            forecast[m] = forecast[m] + dot_nt(dpt_ref[:, at], h)
        cols = pl.ds(j * TILE, TILE)
        for k, (src, dst) in enumerate(((summed_ref, summed_hbm), (hidden_ref, hidden_hbm))):
            outs.append(
                start_copy(src.at[:, :, cols], dst.at[:, :, cols], out_sem.at[k, j])
            )
    for m in range(local):
        f = forecast[m]
        largest = jnp.maximum(jnp.max(jnp.abs(f), axis=1, keepdims=True), 1e-30)
        power = jnp.ceil(jnp.log(largest) * (1.0 / math.log(2.0)) + 1e-3)
        power = jnp.broadcast_to(power, (VPAD, VPAD))
        q = f * (jnp.exp2(-power[:, :1]) * QMAX)
        q = jnp.where(q >= 0.0, q + 0.5, q - 0.5)
        row = jnp.concatenate([power.T[:8], jnp.zeros((8, points - VPAD), F32)], axis=1)
        row = jnp.where(row >= 0.0, row + 0.5, row - 0.5)
        code = jnp.concatenate([q[:VUSE], row], axis=0)
        code_ref[m] = code.astype(jnp.int32).astype(jnp.int16)
    for e in range(coded_hbm.shape[0]):
        outs.append(start_copy(code_ref, coded_hbm.at[e], out_sem.at[2, e]))
    for copy in outs:
        copy.wait()


def factors_kernel(
    where_ref, lat_ref, clat_ref, olat_ref, cf_ref, summed_ref, hidden_ref,
    aggt_ref, hidt_ref, slope_ref, x_ref,
):
    core = where_ref[0]
    j = pl.program_id(0)
    window = cf_ref.shape[1] // 2
    half = aggt_ref.shape[0] // 2
    local = lat_ref.shape[0]
    points = cf_ref.shape[0]
    high = cf_ref[:, :window]
    low = cf_ref[:, window:]
    for m in range(local):
        x_ref[:HALO] = lat_ref[m]
        x_ref[HALO : 2 * HALO] = clat_ref[m]
        x_ref[2 * HALO :] = olat_ref[m * HALO : (m + 1) * HALO]
        cols = slice(m * points, (m + 1) * points)
        x = x_ref[...]
        agg = (dot(high, x) + dot(low, x)).T.astype(BF16)
        hid = hidden_ref[m].astype(F32).T.astype(BF16)
        for k in range(TILE // 16):
            xy = lax.rem(j, 2) * (TILE // 32) + k // 2
            to = lax.bitwise_xor(core, k % 2) * half + xy * 32 + lax.div(j, 2) * 16
            to = pl.ds(pl.multiple_of(to, 16), 16)
            aggt_ref[to, cols] = agg[k * 16 : (k + 1) * 16]
            hidt_ref[to, cols] = hid[k * 16 : (k + 1) * 16]
        s = summed_ref[m]
        t = jnp.tanh(GELU_C * (s + 0.044715 * (s * s * s)))
        slope_ref[m] = 0.5 * (1.0 + t) + (0.5 * GELU_C) * s * (1.0 - t * t) * (
            1.0 + 3.0 * 0.044715 * (s * s)
        )


def decode(code_ref, index):
    code = code_ref[index].astype(jnp.int32).astype(F32)
    power = jnp.broadcast_to(code[VUSE : VUSE + 1, :VPAD], (VPAD, VPAD)).T
    return code[:VUSE] * (jnp.exp2(power[:VUSE, :1]) * (1.0 / QMAX))


def score_kernel(code_ref, truth_ref, score_ref):
    members = code_ref.shape[0]
    nvar = truth_ref.shape[0]
    collected = [decode(code_ref, m)[:nvar] for m in range(members)]
    truth = truth_ref[...]
    skill = sum(smooth_abs(f - truth) for f in collected)
    spread = jnp.zeros_like(skill)
    for m in range(members):
        for o in range(m + 1, members):
            spread = spread + smooth_abs(collected[m] - collected[o])
    score_ref[...] = skill * (1.0 / members) - (pair_factor(members) * 2.0) * spread


def backward_kernel(
    where_ref, code_hbm, truth_hbm, var_hbm, area_hbm, dpt_hbm, aggt_hbm, hidt_hbm, slope_hbm,
    mine_hbm, theirs_hbm, sg_hbm,
    code_ref, truth_ref, var_ref, area_ref, dpt_ref, aggt_ref, hidt_ref, slope_ref,
    f_ref, part_ref, out_ref, sg_ref, in_sem, out_sem,
):
    members = code_ref.shape[0]
    local, points, depth = slope_ref.shape
    half = depth // 2
    steps = depth // TILE
    pairs = (
        (code_hbm, code_ref), (truth_hbm, truth_ref), (var_hbm, var_ref), (area_hbm, area_ref),
        (dpt_hbm, dpt_ref), (hidt_hbm, hidt_ref), (slope_hbm, slope_ref), (aggt_hbm, aggt_ref),
    )
    copies = [start_copy(src, dst, in_sem.at[k]) for k, (src, dst) in enumerate(pairs)]
    for copy in copies[:5]:
        copy.wait()
    for m in range(members):
        f_ref[m] = decode(code_ref, m)
    first = where_ref[1] * local
    truth = truth_ref[...]
    multiplier = var_ref[...] * area_ref[...]
    grads = []
    for m in range(local):
        own = f_ref[first + m]
        mutual = sum(signum(own - f_ref[o]) for o in range(members))
        g = multiplier * (
            signum(own - truth) * (1.0 / members) - (2.0 * pair_factor(members)) * mutual
        )
        g = jnp.concatenate([g, jnp.zeros((VPAD - VUSE, points), F32)], axis=0)
        grads.append(g.T.astype(BF16))
    grad = jnp.concatenate(grads, axis=0)
    outs = []
    copies[5].wait()
    out_ref[...] = dot(hidt_ref[...], grad).astype(BF16)
    cols = pl.ds(depth, VPAD)
    for k, hbm_ref in enumerate((mine_hbm, theirs_hbm)):
        src = out_ref.at[pl.ds(k * half, half)]
        outs.append(start_copy(src, hbm_ref.at[:, cols], out_sem.at[k, steps]))
    copies[6].wait()
    copies[7].wait()
    for j in range(steps):
        at = slice(j * TILE, (j + 1) * TILE)
        cols = pl.ds(j * TILE, TILE)
        hg = dot(grad, dpt_ref[:, at])
        for m in range(local):
            rows = slice(m * points, (m + 1) * points)
            sg_ref[j, rows, :] = (hg[rows] * slope_ref[m, :, at]).astype(BF16)
        part_ref[j] = dot(aggt_ref[...], sg_ref[j]).astype(BF16)
        outs.append(start_copy(sg_ref.at[j], sg_hbm.at[:, cols], out_sem.at[2, j]))
        for k, hbm_ref in enumerate((mine_hbm, theirs_hbm)):
            src = part_ref.at[j, pl.ds(k * half, half)]
            outs.append(start_copy(src, hbm_ref.at[:, cols], out_sem.at[k, j]))
    for copy in outs:
        copy.wait()


def merge_kernel(mine_ref, theirs_ref, out_hbm, out_ref, out_sem):
    rows = mine_ref.shape[0] // 4
    outs = []
    for k in range(4):
        at = slice(k * rows, (k + 1) * rows)
        out_ref[at] = (mine_ref[at].astype(F32) + theirs_ref[at].astype(F32)).astype(BF16)
        cut = pl.ds(k * rows, rows)
        outs.append(start_copy(out_ref.at[cut], out_hbm.at[cut], out_sem.at[k]))
    for copy in outs:
        copy.wait()


def rows_kernel(
    cft_hbm, sg_hbm, core_hbm, odd_hbm, cft_ref, sg_ref, core_ref, odd_ref, in_sem, out_sem
):
    local = core_ref.shape[0]
    points = cft_ref.shape[1] // 2
    cft_copy = start_copy(cft_hbm.at[pl.ds(HALO, 2 * HALO)], cft_ref, in_sem.at[local])
    copies = [
        start_copy(sg_hbm.at[pl.ds(m * points, points)], sg_ref.at[m], in_sem.at[m])
        for m in range(local)
    ]
    cft_copy.wait()
    high = cft_ref[:, :points]
    low = cft_ref[:, points:]
    outs = []
    for m in range(local):
        copies[m].wait()
        for j in range(sg_ref.shape[2] // TILE):
            at = slice(j * TILE, (j + 1) * TILE)
            s = sg_ref[m, :, at]
            g = (dot(high, s) + dot(low, s)).astype(BF16)
            core_ref[m, :, at] = g[:HALO]
            odd_ref[m, :, at] = g[HALO:]
        outs.append(start_copy(odd_ref.at[m], odd_hbm.at[m], out_sem.at[0, m]))
        outs.append(start_copy(core_ref.at[m], core_hbm.at[m], out_sem.at[1, m]))
    for copy in outs:
        copy.wait()


def plane_kernel(got_ref, out_hbm, out_ref, out_sem):
    per = out_hbm.shape[2]
    outs = []
    for z in range(out_hbm.shape[0]):
        at = slice(z * per, (z + 1) * per)
        total = got_ref[0, at].astype(F32)
        for k in range(1, got_ref.shape[0]):
            total = total + got_ref[k, at].astype(F32)
        out_ref[z] = total.astype(BF16)
        for e in range(out_hbm.shape[1]):
            outs.append(start_copy(out_ref.at[z], out_hbm.at[z, e], out_sem.at[z, e]))
    for copy in outs:
        copy.wait()


def final_kernel(got_ref, src_ref, out_ref, *, scaling):
    total = got_ref[0].astype(F32)
    for k in range(1, got_ref.shape[0]):
        total = total + got_ref[k].astype(F32)
    total = total * scaling
    depth = src_ref.shape[1]
    src_ref[...] = total[:, :depth]
    out_ref[...] = total[:, depth : depth + out_ref.shape[1]]


def latent_kernel(cft_ref, sg_ref, core_ref, odd_ref, w_ref, out_ref, g_ref):
    local = core_ref.shape[0]
    points = cft_ref.shape[1] // 2

    @pl.when(pl.program_id(0) == 0)
    def _():
        high = cft_ref[:, :points]
        low = cft_ref[:, points:]
        for m in range(local):
            s = sg_ref[m * points : (m + 1) * points]
            g = dot(high, s) + dot(low, s)
            g = g + core_ref[m].astype(F32) + odd_ref[m].astype(F32)
            g_ref[m * HALO : (m + 1) * HALO] = g.astype(BF16)

    r = dot_nt(g_ref[...], w_ref[...]).astype(BF16)
    for m in range(local):
        out_ref[m] = r[m * HALO : (m + 1) * HALO]


def shape(dims, dtype):
    return jax.ShapeDtypeStruct(dims, dtype)


def call_prepare(where, edge_count, edge_src, edge_dst, edge_weight, latent, core_lat, weight):
    local, rows, depth = latent.shape
    window = rows + 2 * HALO
    points = edge_src.shape[0] * BLK
    edges = edge_src.shape
    return pl.pallas_call(
        prepare_kernel,
        out_shape=(
            shape((points, 2 * window), BF16),
            shape((window, 2 * points), BF16),
            shape((points, 2 * HALO), BF16),
            shape((local, points, depth), F32),
        ),
        in_specs=smem(1) + hbm(7),
        out_specs=tuple(hbm(2) + vmem(2)),
        scratch_shapes=[
            pltpu.SMEM(edge_count.shape, jnp.int32),
            pltpu.VMEM(edges, jnp.int32),
            pltpu.VMEM(edges, jnp.int32),
            pltpu.VMEM(edges, F32),
            pltpu.VMEM((local * 2 * HALO, depth), BF16),
            pltpu.VMEM(weight.shape, BF16),
            pltpu.VMEM((points, 2 * window), BF16),
            pltpu.VMEM((window, 2 * points), BF16),
            pltpu.SemaphoreType.DMA((5 + 2 * local,)),
            pltpu.SemaphoreType.DMA((2,)),
        ],
        compiler_params=params(BIG),
        cost_estimate=cost(3 * 10**9, 6 * 10**6),
        name="prepare",
    )(where, edge_count, edge_src, edge_dst, edge_weight, latent, core_lat, weight)


def call_forward(odd_lat, weight, cfo, part, dpt, ens):
    local, points, depth = part.shape
    steps = depth // TILE
    return pl.pallas_call(
        forward_kernel,
        out_shape=(
            shape((local, points, depth), F32),
            shape((local, points, depth), BF16),
            shape((ens, local, VROWS, points), jnp.int16),
        ),
        in_specs=vmem(5),
        out_specs=tuple(hbm(3)),
        scratch_shapes=[
            pltpu.VMEM((local, points, depth), F32),
            pltpu.VMEM((local, points, depth), BF16),
            pltpu.VMEM((local, VROWS, points), jnp.int16),
            pltpu.SemaphoreType.DMA((3, max(steps, ens))),
        ],
        compiler_params=params(BIG),
        cost_estimate=cost(2 * 10**9, 8 * 10**6),
        name="forward",
    )(odd_lat, weight, cfo, part, dpt)


def call_factors(where, latent, core_lat, odd_lat, cf, summed, hidden):
    local, points, depth = summed.shape
    rows = latent.shape[1]
    lat_spec = pl.BlockSpec((local, rows, TILE), lambda j: (0, 0, j))
    sliced = pl.BlockSpec((local, points, TILE), lambda j: (0, 0, j))
    out_shape = (
        shape((depth, local * points), BF16),
        shape((depth, local * points), BF16),
        shape((local, points, depth), F32),
    )
    return pl.pallas_call(
        factors_kernel,
        grid=(depth // TILE,),
        out_shape=out_shape,
        in_specs=smem(1)
        + [
            lat_spec,
            lat_spec,
            pl.BlockSpec((local * rows, TILE), lambda j: (0, j)),
            *whole(cf),
            sliced,
            sliced,
        ],
        out_specs=(*whole(*out_shape[:2]), sliced),
        scratch_shapes=[pltpu.VMEM((cf.shape[1] // 2, TILE), BF16)],
        compiler_params=params(BIG),
        cost_estimate=cost(3 * 10**9, 10 * 10**6),
        name="factors",
    )(where, latent, core_lat, odd_lat, cf, summed, hidden)


def call_backward(where, everyone, truth, var_col, area, dpt, aggt, hidt, slope):
    members = everyone.shape[0]
    local, points, depth = slope.shape
    cols = depth + VPAD
    steps = depth // TILE
    operands = (everyone, truth, var_col, area, dpt, aggt, hidt, slope)
    return pl.pallas_call(
        backward_kernel,
        out_shape=(
            shape((depth // 2, cols), BF16),
            shape((depth // 2, cols), BF16),
            shape((local * points, depth), BF16),
        ),
        in_specs=smem(1) + hbm(len(operands)),
        out_specs=tuple(hbm(3)),
        scratch_shapes=[pltpu.VMEM(a.shape, a.dtype) for a in operands]
        + [
            pltpu.VMEM((members, VUSE, points), F32),
            pltpu.VMEM((steps, depth, TILE), BF16),
            pltpu.VMEM((depth, VPAD), BF16),
            pltpu.VMEM((steps, local * points, TILE), BF16),
            pltpu.SemaphoreType.DMA((len(operands),)),
            pltpu.SemaphoreType.DMA((3, steps + 1)),
        ],
        compiler_params=params(BIG),
        cost_estimate=cost(2 * 10**9, 8 * 10**6),
        name="backward",
    )(where, *operands)


def call_merge(mine, theirs):
    return pl.pallas_call(
        merge_kernel,
        out_shape=shape(mine.shape, BF16),
        in_specs=vmem(2),
        out_specs=hbm(1)[0],
        scratch_shapes=[pltpu.VMEM(mine.shape, BF16), pltpu.SemaphoreType.DMA((4,))],
        compiler_params=params(MID),
        cost_estimate=cost(10**6, 4 * 10**6),
        name="merge",
    )(mine, theirs)


def call_rows(cft, summed_grad, local):
    depth = summed_grad.shape[1]
    points = summed_grad.shape[0] // local
    send = shape((local, HALO, depth), BF16)
    return pl.pallas_call(
        rows_kernel,
        out_shape=(send, send),
        in_specs=hbm(2),
        out_specs=tuple(hbm(2)),
        scratch_shapes=[
            pltpu.VMEM((2 * HALO, cft.shape[1]), BF16),
            pltpu.VMEM((local, points, depth), BF16),
            pltpu.VMEM(send.shape, BF16),
            pltpu.VMEM(send.shape, BF16),
            pltpu.SemaphoreType.DMA((local + 1,)),
            pltpu.SemaphoreType.DMA((2, local)),
        ],
        compiler_params=params(BIG),
        cost_estimate=cost(10**9, 4 * 10**6),
        name="rows",
    )(cft, summed_grad)


def call_plane(got, ens):
    out_shape = shape((2, ens, got.shape[1] // 2, got.shape[2]), BF16)
    return pl.pallas_call(
        plane_kernel,
        out_shape=out_shape,
        in_specs=vmem(1),
        out_specs=hbm(1)[0],
        scratch_shapes=[
            pltpu.VMEM((2,) + out_shape.shape[2:], BF16),
            pltpu.SemaphoreType.DMA((2, ens)),
        ],
        compiler_params=params(MID),
        cost_estimate=cost(10**6, 2 * 10**6),
        name="plane",
    )(got)


def call_score(everyone, truth):
    return pl.pallas_call(
        score_kernel,
        grid=(1,),
        out_shape=shape(truth.shape, F32),
        in_specs=whole(everyone, truth),
        out_specs=whole(truth)[0],
        compiler_params=params(MID),
        cost_estimate=cost(10**7, 10**6),
        name="score",
    )(everyone, truth)


def call_latent(cft, summed_grad, core_grad, odd_grad, weight):
    local, rows, depth = core_grad.shape
    return pl.pallas_call(
        latent_kernel,
        grid=(depth // TILE,),
        out_shape=shape(core_grad.shape, BF16),
        in_specs=[
            pl.BlockSpec((HALO, cft.shape[1]), lambda j: (0, 0)),
            *whole(summed_grad, core_grad, odd_grad),
            pl.BlockSpec((TILE, depth), lambda j: (j, 0)),
        ],
        out_specs=pl.BlockSpec((local, rows, TILE), lambda j: (0, 0, j)),
        scratch_shapes=[pltpu.VMEM((local * rows, depth), BF16)],
        compiler_params=params(BIG),
        cost_estimate=cost(10**9, 5 * 10**6),
        name="latent",
    )(cft, summed_grad, core_grad, odd_grad, weight)


def call_final(got, nvar, scaling):
    per = got.shape[1]
    return pl.pallas_call(
        functools.partial(final_kernel, scaling=scaling),
        out_shape=(shape((per, got.shape[2] - VPAD), F32), shape((per, nvar), F32)),
        in_specs=vmem(1),
        out_specs=tuple(vmem(2)),
        compiler_params=params(MID),
        cost_estimate=cost(10**5, 4 * 10**5),
        name="final",
    )(got)


def make_body(count):
    odd_pairs = [(i, (i + 1) % count if i % 2 else (i - 1) % count) for i in range(count)]
    swap = [(0, 1), (1, 0)]

    def body(
        latent, src_weight, decoder_projection, truth, area_weight, var_weight,
        edge_src, edge_dst, edge_weight, edge_count,
    ):
        local, rows, depth = latent.shape
        ens = lax.axis_size("ens")
        members = local * ens
        nvar = decoder_projection.shape[1]
        points = truth.shape[1]
        per = depth // count
        cols = depth + VPAD
        where = jnp.stack([lax.axis_index("core"), lax.axis_index("ens")]).astype(jnp.int32)

        odd_lat = lax.ppermute(latent, SPACE, odd_pairs).reshape(local * rows, depth)
        core_lat = lax.ppermute(latent, "core", swap)
        dpt = jnp.pad(decoder_projection.T, ((0, VPAD - nvar), (0, 0)))
        cf, cft, cfo, part = call_prepare(
            where, edge_count, edge_src, edge_dst, edge_weight, latent, core_lat, src_weight
        )
        summed, hidden, coded = call_forward(odd_lat, src_weight, cfo, part, dpt, ens)
        everyone = lax.all_to_all(coded, "ens", 0, 0, tiled=True)
        everyone = everyone.reshape(members, VROWS, points)
        aggt, hidt, slope = call_factors(
            where, latent, core_lat, odd_lat, cf, summed, hidden
        )
        tall = jnp.pad(truth, ((0, VUSE - nvar), (0, 0)))
        var_col = jnp.pad(var_weight, (0, VUSE - nvar)).reshape(VUSE, 1)
        mine, theirs, summed_grad = call_backward(
            where, everyone, tall, var_col, area_weight.reshape(1, points), dpt,
            aggt, hidt, slope,
        )

        theirs = lax.ppermute(theirs, "core", swap)
        half = call_merge(mine, theirs).reshape(16, 2 * per, cols)
        got = lax.all_to_all(half, ("x", "y"), 0, 0, tiled=True)
        core_send, odd_send = call_rows(cft, summed_grad, local)
        odd_grad = lax.ppermute(odd_send, SPACE, odd_pairs)
        core_grad = lax.ppermute(core_send, "core", swap)
        plane = call_plane(got, ens)
        got = lax.all_to_all(plane.reshape(2 * ens, per, cols), ("zhi", "ens"), 0, 0, tiled=True)
        score = call_score(everyone, truth)
        grad_latent = call_latent(cft, summed_grad, core_grad, odd_grad, src_weight)
        grad_src, grad_out = call_final(got, nvar, 1.0 / math.sqrt(members * points * count))
        return score, grad_latent, grad_src, grad_out

    return body


def solution(mesh):
    fine = jax.sharding.Mesh(
        mesh.devices.reshape(mesh.devices.shape[0], 2, 4, 4, 2), ("ens",) + SPACE
    )
    return jax.shard_map(
        make_body(mesh.devices.shape[1]),
        mesh=fine,
        in_specs=(
            P("ens", SPACE, None), P(), P(), P(None, SPACE), P(SPACE), P(),
            P(SPACE, None), P(SPACE, None), P(SPACE, None), P(SPACE),
        ),
        out_specs=(P(None, SPACE), P("ens", SPACE, None), P(SPACE, None), P(SPACE, None)),
        check_vma=False,
    )
```

```python
import functools
import math

import jax
import jax.numpy as jnp
from jax import lax
from jax.experimental import pallas as pl
from jax.experimental.pallas import tpu as pltpu
from jax.sharding import PartitionSpec as P

HALO = 128
BLK = 128
ALPHA = 0.95
DELTA = 0.05
SPACE = ("zhi", "x", "y", "core")
QMAX = 32000.0
VPAD = 128
VROWS = 112
VUSE = 104
TILE = 256
GELU_C = math.sqrt(2.0 / math.pi)
MIB = 1 << 20
LIMIT = 24
PREP = 53
F32 = jnp.float32
BF16 = jnp.bfloat16


def dot(a, b):
    return jnp.dot(a, b, preferred_element_type=F32)


def dot_nt(a, b):
    return lax.dot_general(a, b, (((1,), (1,)), ((), ())), preferred_element_type=F32)


def smem(count):
    return [pl.BlockSpec(memory_space=pltpu.SMEM)] * count


def cost(flops, nbytes):
    return pl.CostEstimate(flops=flops, bytes_accessed=nbytes, transcendentals=0)


def params(mib):
    return pltpu.CompilerParams(vmem_limit_bytes=mib * MIB)


def hbm(count):
    return [pl.BlockSpec(memory_space=pltpu.HBM)] * count


def vmem(count):
    return [pl.BlockSpec(memory_space=pltpu.VMEM)] * count


def anywhere(count):
    return [pl.BlockSpec(memory_space=pl.ANY)] * count


def start_copy(src, dst, sem):
    copy = pltpu.make_async_copy(src, dst, sem)
    copy.start()
    return copy


def pair_factor(members):
    fair_eps = (1.0 - ALPHA) / members
    return (1.0 - fair_eps) / (2.0 * members * (members - 1))


def smooth_abs(distance):
    square = distance * distance + DELTA * DELTA
    return square * lax.rsqrt(square)


def signum(distance):
    return distance * lax.rsqrt(distance * distance + DELTA * DELTA)


def prepare_kernel(
    where_ref, count_hbm, src_hbm, dst_hbm, wt_hbm, lat_hbm, clat_hbm, w_hbm,
    cf_ref, cft_hbm, cfo_ref, part_ref,
    count_ref, src_ref, dst_ref, wt_ref, x_ref, w_ref, cft_ref, in_sem, out_sem,
):
    edges = [
        start_copy(src, dst, in_sem.at[k])
        for k, (src, dst) in enumerate(
            ((count_hbm, count_ref), (src_hbm, src_ref), (dst_hbm, dst_ref), (wt_hbm, wt_ref))
        )
    ]
    local = lat_hbm.shape[0]
    inputs = []
    for m in range(local):
        for k, ref in enumerate((lat_hbm, clat_hbm)):
            inputs.append(
                start_copy(
                    ref.at[m],
                    x_ref.at[pl.ds((2 * m + k) * HALO, HALO)],
                    in_sem.at[4 + 2 * m + k],
                )
            )
    inputs.append(start_copy(w_hbm, w_ref, in_sem.at[4 + 2 * local]))
    core = where_ref[0]
    slots = src_ref.shape[1]
    window = cf_ref.shape[1] // 2
    points = cf_ref.shape[0]
    for copy in edges:
        copy.wait()
    for b in range(src_ref.shape[0]):
        src = src_ref[b : b + 1, :]
        slot = lax.broadcasted_iota(jnp.int32, (1, slots), 1)
        wt = jnp.where(slot < count_ref[b], wt_ref[b : b + 1, :], 0.0)
        left = 2 * HALO - HALO * core
        right = HALO + HALO * core
        place = jnp.where(
            src < HALO,
            src + left,
            jnp.where(src < 2 * HALO, src - HALO, src - 2 * HALO + right),
        )
        rows = lax.broadcasted_iota(jnp.int32, (window, slots), 0)
        hot = jnp.where(rows == place, 1.0, 0.0).astype(BF16)
        pts = lax.broadcasted_iota(jnp.int32, (BLK, slots), 0)
        mat = jnp.where(pts == dst_ref[b : b + 1, :], wt, 0.0).astype(BF16)
        coef = dot_nt(mat, hot)
        high = coef.astype(BF16)
        low = (coef - high.astype(F32)).astype(BF16)
        at = slice(b * BLK, (b + 1) * BLK)
        cf_ref[at, :window] = high
        cf_ref[at, window:] = low
        cfo_ref[at, :HALO] = high[:, 2 * HALO :]
        cfo_ref[at, HALO:] = low[:, 2 * HALO :]
        coef_t = dot_nt(hot, mat)
        high_t = coef_t.astype(BF16)
        cft_ref[:, b * BLK : (b + 1) * BLK] = high_t
        cft_ref[:, points + b * BLK : points + (b + 1) * BLK] = (
            coef_t - high_t.astype(F32)
        ).astype(BF16)
    out = start_copy(cft_ref, cft_hbm, out_sem)
    for copy in inputs:
        copy.wait()
    x = x_ref[...]
    high = cf_ref[:, : 2 * HALO]
    low = cf_ref[:, window : window + 2 * HALO]
    for j in range(w_ref.shape[1] // TILE):
        at = slice(j * TILE, (j + 1) * TILE)
        p = dot(x, w_ref[:, at]).astype(BF16)
        for m in range(local):
            pm = p[2 * m * HALO : (2 * m + 2) * HALO]
            part_ref[m, :, at] = dot(high, pm) + dot(low, pm)
    out.wait()


def forward_kernel(
    odd_ref, w_ref, cfo_ref, part_ref, dpt_ref, summed_ref, hidden_ref, code_ref
):
    local, points, depth = part_ref.shape
    forecast = [jnp.zeros((VPAD, points), F32) for _ in range(local)]
    for j in range(depth // TILE):
        at = slice(j * TILE, (j + 1) * TILE)
        p = dot(odd_ref[...], w_ref[:, at]).astype(BF16)
        for m in range(local):
            pm = p[m * HALO : (m + 1) * HALO]
            s = part_ref[m, :, at] + dot(cfo_ref[...], jnp.concatenate([pm, pm], axis=0))
            summed_ref[m, :, at] = s
            t = jnp.tanh(s * (GELU_C + (GELU_C * 0.044715) * (s * s)))
            h = (0.5 * s * (1.0 + t)).astype(BF16)
            hidden_ref[m, :, at] = h
            forecast[m] = forecast[m] + dot_nt(dpt_ref[:, at], h)
    for m in range(local):
        f = forecast[m]
        largest = jnp.maximum(jnp.max(jnp.abs(f), axis=1, keepdims=True), 1e-30)
        power = jnp.ceil(jnp.log(largest) * (1.0 / math.log(2.0)) + 1e-3)
        power = jnp.broadcast_to(power, (VPAD, VPAD))
        q = f * (jnp.exp2(-power[:, :1]) * QMAX)
        q = jnp.where(q >= 0.0, q + 0.5, q - 0.5)
        row = jnp.concatenate([power.T[:8], jnp.zeros((8, points - VPAD), F32)], axis=1)
        row = jnp.where(row >= 0.0, row + 0.5, row - 0.5)
        code = jnp.concatenate([q[:VUSE], row], axis=0)
        code_ref[m] = code.astype(jnp.int32).astype(jnp.int16)


def factors_kernel(
    where_ref, lat_ref, clat_ref, olat_ref, cf_ref, summed_ref, hidden_ref,
    aggt_ref, hidt_ref, slope_ref, x_ref,
):
    core = where_ref[0]
    window = cf_ref.shape[1] // 2
    local, points, depth = summed_ref.shape
    high = cf_ref[:, :window]
    low = cf_ref[:, window:]
    for m in range(local):
        x_ref[:HALO] = lat_ref[m]
        x_ref[HALO : 2 * HALO] = clat_ref[m]
        x_ref[2 * HALO :] = olat_ref[m * HALO : (m + 1) * HALO]
        cols = slice(m * points, (m + 1) * points)
        for j in range(depth // TILE):
            at = slice(j * TILE, (j + 1) * TILE)
            x = x_ref[:, at]
            agg = (dot(high, x) + dot(low, x)).T.astype(BF16)
            hid = hidden_ref[m, :, at].astype(F32).T.astype(BF16)
            for k in range(TILE // 16):
                block = j * (TILE // 16) + k
                zhi, rest = divmod(block, 32)
                xy, c = divmod(rest, 2)
                to = lax.bitwise_xor(core, c) * (depth // 2) + (xy * 32 + zhi * 16)
                to = pl.ds(pl.multiple_of(to, 16), 16)
                aggt_ref[to, cols] = agg[k * 16 : (k + 1) * 16]
                hidt_ref[to, cols] = hid[k * 16 : (k + 1) * 16]
            s = summed_ref[m, :, at]
            t = jnp.tanh(s * (GELU_C + (GELU_C * 0.044715) * (s * s)))
            slope_ref[m, :, at] = 0.5 * (1.0 + t) + (0.5 * GELU_C) * s * (1.0 - t * t) * (
                1.0 + 3.0 * 0.044715 * (s * s)
            )


def decode(where_ref, code_refs, f_ref):
    local = code_refs[0].shape[0]
    rows = [
        ref[m, VROWS - 8 :, :].astype(jnp.int32).astype(F32)[:1, :VPAD]
        for ref in code_refs
        for m in range(local)
    ]
    rows.append(jnp.zeros((VPAD - len(rows), VPAD), F32))
    power = (jnp.exp2(jnp.concatenate(rows, axis=0)) * (1.0 / QMAX)).T
    for k, ref in enumerate(code_refs):
        first = lax.bitwise_xor(where_ref[1], k) * local
        for m in range(local):
            code = ref[m].astype(jnp.int32).astype(F32)[:VUSE]
            at = k * local + m
            f_ref[first + m] = code * power[:VUSE, at : at + 1]


def score_kernel(where_ref, c0_ref, c1_ref, c2_ref, c3_ref, truth_ref, score_ref, f_ref):
    members = f_ref.shape[0]
    nvar = truth_ref.shape[0]
    decode(where_ref, (c0_ref, c1_ref, c2_ref, c3_ref), f_ref)
    collected = [f_ref[m][:nvar] for m in range(members)]
    truth = truth_ref[...]
    skill = sum(smooth_abs(f - truth) for f in collected)
    spread = jnp.zeros_like(skill)
    for m in range(members):
        for o in range(m + 1, members):
            spread = spread + smooth_abs(collected[m] - collected[o])
    score_ref[...] = skill * (1.0 / members) - (pair_factor(members) * 2.0) * spread


def backward_kernel(
    where_ref, c0_ref, c1_ref, c2_ref, c3_ref, truth_ref, var_ref, area_ref, dpt_ref,
    aggt_ref, hidt_ref, slope_ref, mine_ref, theirs_ref, sg_ref, f_ref, g_ref,
):
    members = f_ref.shape[0]
    nvar = truth_ref.shape[0]
    local, points, depth = slope_ref.shape
    half = depth // 2
    decode(where_ref, (c0_ref, c1_ref, c2_ref, c3_ref), f_ref)
    first = where_ref[1] * local
    truth = truth_ref[...]
    g_ref[96:] = jnp.zeros((VPAD - 96, points), F32)
    grads = []
    for m in range(local):
        own = f_ref[first + m][:nvar]
        mutual = sum(signum(own - f_ref[o][:nvar]) for o in range(members))
        g_ref[:nvar] = area_ref[...] * (
            signum(own - truth) * (1.0 / members) - (2.0 * pair_factor(members)) * mutual
        )
        grads.append((g_ref[...].T * var_ref[...]).astype(BF16))
    grad = jnp.concatenate(grads, axis=0)
    out = dot(hidt_ref[...], grad).astype(BF16)
    mine_ref[:, depth:] = out[:half]
    theirs_ref[:, depth:] = out[half:]
    for j in range(depth // TILE):
        at = slice(j * TILE, (j + 1) * TILE)
        hg = dot(grad, dpt_ref[:, at])
        for m in range(local):
            rows = slice(m * points, (m + 1) * points)
            sg_ref[rows, at] = (hg[rows] * slope_ref[m, :, at]).astype(BF16)
        part = dot(aggt_ref[...], sg_ref[:, at]).astype(BF16)
        mine_ref[:, at] = part[:half]
        theirs_ref[:, at] = part[half:]


def merge_kernel(mine_ref, theirs_ref, out_hbm, out_ref, out_sem):
    rows = mine_ref.shape[0] // 4
    outs = []
    for k in range(4):
        at = slice(k * rows, (k + 1) * rows)
        out_ref[at] = (mine_ref[at].astype(F32) + theirs_ref[at].astype(F32)).astype(BF16)
        cut = pl.ds(k * rows, rows)
        outs.append(start_copy(out_ref.at[cut], out_hbm.at[cut], out_sem.at[k]))
    for copy in outs:
        copy.wait()


def rows_kernel(cft_ref, sg_ref, core_hbm, odd_hbm, core_ref, odd_ref, out_sem):
    local, _, depth = core_ref.shape
    points = cft_ref.shape[1] // 2
    high = cft_ref[HALO:, :points]
    low = cft_ref[HALO:, points:]
    outs = []
    for m in range(local):
        for j in range(depth // TILE):
            at = slice(j * TILE, (j + 1) * TILE)
            s = sg_ref[m * points : (m + 1) * points, at]
            g = (dot(high, s) + dot(low, s)).astype(BF16)
            core_ref[m, :, at] = g[:HALO]
            odd_ref[m, :, at] = g[HALO:]
        outs.append(start_copy(odd_ref.at[m], odd_hbm.at[m], out_sem.at[0, m]))
        outs.append(start_copy(core_ref.at[m], core_hbm.at[m], out_sem.at[1, m]))
    for copy in outs:
        copy.wait()


def plane_kernel(got_ref, out_hbm, out_ref, out_sem):
    per = out_hbm.shape[2]
    outs = []
    for z in range(out_hbm.shape[0]):
        at = slice(z * per, (z + 1) * per)
        total = got_ref[0, at].astype(F32)
        for k in range(1, got_ref.shape[0]):
            total = total + got_ref[k, at].astype(F32)
        out_ref[z] = total.astype(BF16)
        for e in range(out_hbm.shape[1]):
            outs.append(start_copy(out_ref.at[z], out_hbm.at[z, e], out_sem.at[z, e]))
    for copy in outs:
        copy.wait()


def final_kernel(got_ref, src_ref, out_ref, *, scaling):
    total = got_ref[0].astype(F32)
    for k in range(1, got_ref.shape[0]):
        total = total + got_ref[k].astype(F32)
    total = total * scaling
    depth = src_ref.shape[1]
    src_ref[...] = total[:, :depth]
    out_ref[...] = total[:, depth : depth + out_ref.shape[1]]


def latent_kernel(
    cft_ref, sg_ref, w_ref, core_ref, odd_ref, out_hbm, g_ref, out_ref, out_sem
):
    local, rows, depth = core_ref.shape
    points = cft_ref.shape[1] // 2
    steps = depth // TILE
    high = cft_ref[:HALO, :points]
    low = cft_ref[:HALO, points:]
    for m in range(local):
        for j in range(steps):
            at = slice(j * TILE, (j + 1) * TILE)
            s = sg_ref[m * points : (m + 1) * points, at]
            g = dot(high, s) + dot(low, s)
            g = g + core_ref[m, :, at].astype(F32) + odd_ref[m, :, at].astype(F32)
            g_ref[m * HALO : (m + 1) * HALO, at] = g.astype(BF16)
    outs = []
    for j in range(steps):
        at = slice(j * TILE, (j + 1) * TILE)
        r = dot_nt(g_ref[...], w_ref[at, :]).astype(BF16)
        for m in range(local):
            out_ref[m, :, at] = r[m * HALO : (m + 1) * HALO]
        cols = pl.ds(j * TILE, TILE)
        outs.append(start_copy(out_ref.at[:, :, cols], out_hbm.at[:, :, cols], out_sem.at[j]))
    for copy in outs:
        copy.wait()


def shape(dims, dtype):
    return jax.ShapeDtypeStruct(dims, dtype)


def scratch(*arrays):
    return [pltpu.VMEM(a.shape, a.dtype) for a in arrays]


def sems(*dims):
    return pltpu.SemaphoreType.DMA(dims)


def call(
    kernel, name, out_shape, in_specs, out_specs, scratch_shapes, work, operands, limit=LIMIT
):
    return pl.pallas_call(
        kernel,
        out_shape=out_shape,
        in_specs=in_specs,
        out_specs=out_specs,
        scratch_shapes=scratch_shapes,
        compiler_params=params(limit),
        cost_estimate=cost(*work),
        name=name,
    )(*operands)


def call_prepare(where, edge_count, edge_src, edge_dst, edge_weight, latent, core_lat, weight):
    local, rows, depth = latent.shape
    window = rows + 2 * HALO
    points = edge_src.shape[0] * BLK
    cf = shape((points, 2 * window), BF16)
    cft = shape((window, 2 * points), BF16)
    return call(
        prepare_kernel,
        "prepare",
        (cf, cft, shape((points, 2 * HALO), BF16), shape((local, points, depth), F32)),
        smem(1) + hbm(5) + anywhere(1) + hbm(1),
        tuple(vmem(1) + hbm(1) + vmem(2)),
        [pltpu.SMEM(edge_count.shape, jnp.int32)]
        + scratch(edge_src, edge_dst, edge_weight)
        + [pltpu.VMEM((local * 2 * HALO, depth), BF16)]
        + scratch(weight, cft)
        + [sems(5 + 2 * local), pltpu.SemaphoreType.DMA],
        (3 * 10**9, 6 * 10**6),
        (where, edge_count, edge_src, edge_dst, edge_weight, latent, core_lat, weight),
        PREP,
    )


def call_forward(odd_lat, weight, cfo, part, dpt):
    local, points, depth = part.shape
    return call(
        forward_kernel,
        "forward",
        (
            shape(part.shape, F32),
            shape(part.shape, BF16),
            shape((local, VROWS, points), jnp.int16),
        ),
        vmem(5),
        tuple(vmem(3)),
        [],
        (2 * 10**9, 8 * 10**6),
        (odd_lat, weight, cfo, part, dpt),
    )


def call_factors(where, latent, core_lat, odd_lat, cf, summed, hidden):
    local, points, depth = summed.shape
    left = shape((depth, local * points), BF16)
    return call(
        factors_kernel,
        "factors",
        (left, left, shape(summed.shape, F32)),
        smem(1) + vmem(6),
        tuple(vmem(3)),
        [pltpu.VMEM((cf.shape[1] // 2, depth), BF16)],
        (3 * 10**9, 10 * 10**6),
        (where, latent, core_lat, odd_lat, cf, summed, hidden),
    )


def call_backward(where, codes, truth, var_row, area_row, dpt, aggt, hidt, slope):
    local, points, depth = slope.shape
    part = shape((depth // 2, depth + VPAD), BF16)
    return call(
        backward_kernel,
        "backward",
        (part, part, shape((local * points, depth), BF16)),
        smem(1) + vmem(len(codes) + 7),
        tuple(vmem(3)),
        [
            pltpu.VMEM((local * len(codes), VUSE, points), F32),
            pltpu.VMEM((VPAD, points), F32),
        ],
        (2 * 10**9, 5 * 10**6),
        (where, *codes, truth, var_row, area_row, dpt, aggt, hidt, slope),
    )


def call_merge(mine, theirs):
    return call(
        merge_kernel,
        "merge",
        shape(mine.shape, BF16),
        vmem(2),
        hbm(1)[0],
        scratch(mine) + [sems(4)],
        (10**6, 4 * 10**6),
        (mine, theirs),
    )


def call_rows(cft, summed_grad, local):
    send = shape((local, HALO, summed_grad.shape[1]), BF16)
    return call(
        rows_kernel,
        "rows",
        (send, send),
        vmem(2),
        tuple(hbm(2)),
        scratch(send, send) + [sems(2, local)],
        (10**9, 3 * 10**6),
        (cft, summed_grad),
    )


def call_plane(got, ens):
    out_shape = shape((2, ens, got.shape[1] // 2, got.shape[2]), BF16)
    return call(
        plane_kernel,
        "plane",
        out_shape,
        vmem(1),
        hbm(1)[0],
        [pltpu.VMEM((2,) + out_shape.shape[2:], BF16), sems(2, ens)],
        (10**6, 10**6),
        (got,),
    )


def call_score(where, codes, truth):
    local, _, points = codes[0].shape
    return call(
        score_kernel,
        "score",
        shape(truth.shape, F32),
        smem(1) + vmem(len(codes) + 1),
        vmem(1)[0],
        [pltpu.VMEM((local * len(codes), VUSE, points), F32)],
        (10**7, 10**6),
        (where, *codes, truth),
    )


def call_latent(cft, summed_grad, weight, core_grad, odd_grad):
    local, rows, depth = core_grad.shape
    return call(
        latent_kernel,
        "latent",
        shape(core_grad.shape, BF16),
        vmem(5),
        hbm(1)[0],
        [pltpu.VMEM((local * rows, depth), BF16)]
        + scratch(core_grad)
        + [sems(depth // TILE)],
        (10**9, 5 * 10**6),
        (cft, summed_grad, weight, core_grad, odd_grad),
    )


def call_final(got, nvar, scaling):
    per = got.shape[1]
    return call(
        functools.partial(final_kernel, scaling=scaling),
        "final",
        (shape((per, got.shape[2] - VPAD), F32), shape((per, nvar), F32)),
        vmem(1),
        tuple(vmem(2)),
        [],
        (10**5, 4 * 10**5),
        (got,),
    )


def make_body(count):
    odd_pairs = [(i, (i + 1) % count if i % 2 else (i - 1) % count) for i in range(count)]
    swap = [(0, 1), (1, 0)]

    def body(
        latent, src_weight, decoder_projection, truth, area_weight, var_weight,
        edge_src, edge_dst, edge_weight, edge_count,
    ):
        local, rows, depth = latent.shape
        ens = lax.axis_size("ens")
        members = local * ens
        nvar = decoder_projection.shape[1]
        points = truth.shape[1]
        per = depth // count
        where = jnp.stack([lax.axis_index("core"), lax.axis_index("ens")]).astype(jnp.int32)

        odd_lat = lax.ppermute(latent, SPACE, odd_pairs).reshape(local * rows, depth)
        core_lat = lax.ppermute(latent, "core", swap)
        dpt = jnp.pad(decoder_projection.T, ((0, VPAD - nvar), (0, 0)))
        cf, cft, cfo, part = call_prepare(
            where, edge_count, edge_src, edge_dst, edge_weight, latent, core_lat, src_weight
        )
        var_row = jnp.pad(var_weight, (0, VPAD - nvar)).reshape(1, VPAD)
        area_row = area_weight.reshape(1, points)
        summed, hidden, coded = call_forward(odd_lat, src_weight, cfo, part, dpt)
        codes = [coded] + [
            lax.ppermute(coded, "ens", [(e, e ^ k) for e in range(ens)]) for k in range(1, ens)
        ]
        aggt, hidt, slope = call_factors(
            where, latent, core_lat, odd_lat, cf, summed, hidden
        )
        mine, theirs, summed_grad = call_backward(
            where, codes, truth, var_row, area_row, dpt, aggt, hidt, slope
        )
        theirs = lax.ppermute(theirs, "core", swap)
        part = call_merge(mine, theirs)
        core_send, odd_send = call_rows(cft, summed_grad, local)
        part = part.reshape(16, 2 * per, part.shape[1])
        got = lax.all_to_all(part, ("x", "y"), 0, 0, tiled=True)
        odd_grad = lax.ppermute(odd_send, SPACE, odd_pairs)
        core_grad = lax.ppermute(core_send, "core", swap)
        plane = call_plane(got, ens).reshape(2 * ens, per, got.shape[2])
        got = lax.all_to_all(plane, ("zhi", "ens"), 0, 0, tiled=True)
        score = call_score(where, codes, truth)
        grad_latent = call_latent(cft, summed_grad, src_weight, core_grad, odd_grad)
        scaling = 1.0 / math.sqrt(members * points * count)
        grad_src, grad_out = call_final(got, nvar, scaling)
        return score, grad_latent, grad_src, grad_out

    return body


def solution(mesh):
    fine = jax.sharding.Mesh(
        mesh.devices.reshape(mesh.devices.shape[0], 2, 4, 4, 2), ("ens",) + SPACE
    )
    return jax.shard_map(
        make_body(mesh.devices.shape[1]),
        mesh=fine,
        in_specs=(
            P("ens", SPACE, None), P(), P(), P(None, SPACE), P(SPACE), P(),
            P(SPACE, None), P(SPACE, None), P(SPACE, None), P(SPACE),
        ),
        out_specs=(P(None, SPACE), P("ens", SPACE, None), P(SPACE, None), P(SPACE, None)),
        check_vma=False,
    )
```

```python
import functools
import math

import jax
import jax.numpy as jnp
from jax import lax
from jax.experimental import pallas as pl
from jax.experimental.pallas import tpu as pltpu
from jax.sharding import PartitionSpec as P

HALO = 128
BLK = 128
ALPHA = 0.95
DELTA = 0.05
SPACE = ("zhi", "x", "y", "core")
QMAX = 32000.0
VPAD = 128
VROWS = 112
VUSE = 104
TILE = 256
GELU_C = math.sqrt(2.0 / math.pi)
MIB = 1 << 20
LIMIT = 24
PREP = 50
LARGE = 56
F32 = jnp.float32
BF16 = jnp.bfloat16


def dot(a, b):
    return jnp.dot(a, b, preferred_element_type=F32)


def dot_nt(a, b):
    return lax.dot_general(a, b, (((1,), (1,)), ((), ())), preferred_element_type=F32)


def smem(count):
    return [pl.BlockSpec(memory_space=pltpu.SMEM)] * count


def cost(flops, nbytes):
    return pl.CostEstimate(flops=flops, bytes_accessed=nbytes, transcendentals=0)


def params(mib):
    return pltpu.CompilerParams(vmem_limit_bytes=mib * MIB)


def hbm(count):
    return [pl.BlockSpec(memory_space=pltpu.HBM)] * count


def vmem(count):
    return [pl.BlockSpec(memory_space=pltpu.VMEM)] * count


def anywhere(count):
    return [pl.BlockSpec(memory_space=pl.ANY)] * count


def start_copy(src, dst, sem):
    copy = pltpu.make_async_copy(src, dst, sem)
    copy.start()
    return copy


def pair_factor(members):
    fair_eps = (1.0 - ALPHA) / members
    return (1.0 - fair_eps) / (2.0 * members * (members - 1))


def smooth_abs(distance):
    square = distance * distance + DELTA * DELTA
    return square * lax.rsqrt(square)


def signum(distance):
    return distance * lax.rsqrt(distance * distance + DELTA * DELTA)


def prepare_kernel(
    where_ref, count_hbm, src_hbm, dst_hbm, wt_hbm, lat_hbm, clat_hbm, w_hbm,
    cf_ref, cft_hbm, cfo_ref, part_ref,
    count_ref, src_ref, dst_ref, wt_ref, x_ref, w_ref, cft_ref, in_sem, out_sem,
):
    edges = [
        start_copy(src, dst, in_sem.at[k])
        for k, (src, dst) in enumerate(
            ((count_hbm, count_ref), (src_hbm, src_ref), (dst_hbm, dst_ref), (wt_hbm, wt_ref))
        )
    ]
    local = lat_hbm.shape[0]
    inputs = []
    for m in range(local):
        for k, ref in enumerate((lat_hbm, clat_hbm)):
            inputs.append(
                start_copy(
                    ref.at[m],
                    x_ref.at[pl.ds((2 * m + k) * HALO, HALO)],
                    in_sem.at[4 + 2 * m + k],
                )
            )
    inputs.append(start_copy(w_hbm, w_ref, in_sem.at[4 + 2 * local]))
    core = where_ref[0]
    slots = src_ref.shape[1]
    window = cf_ref.shape[1] // 2
    points = cf_ref.shape[0]
    for copy in edges:
        copy.wait()
    for b in range(src_ref.shape[0]):
        src = src_ref[b : b + 1, :]
        slot = lax.broadcasted_iota(jnp.int32, (1, slots), 1)
        wt = jnp.where(slot < count_ref[b], wt_ref[b : b + 1, :], 0.0)
        left = 2 * HALO - HALO * core
        right = HALO + HALO * core
        place = jnp.where(
            src < HALO,
            src + left,
            jnp.where(src < 2 * HALO, src - HALO, src - 2 * HALO + right),
        )
        rows = lax.broadcasted_iota(jnp.int32, (window, slots), 0)
        hot = jnp.where(rows == place, 1.0, 0.0).astype(BF16)
        pts = lax.broadcasted_iota(jnp.int32, (BLK, slots), 0)
        mat = jnp.where(pts == dst_ref[b : b + 1, :], wt, 0.0).astype(BF16)
        coef = dot_nt(mat, hot)
        high = coef.astype(BF16)
        low = (coef - high.astype(F32)).astype(BF16)
        at = slice(b * BLK, (b + 1) * BLK)
        cf_ref[at, :window] = high
        cf_ref[at, window:] = low
        cfo_ref[at, :HALO] = high[:, 2 * HALO :]
        cfo_ref[at, HALO:] = low[:, 2 * HALO :]
        coef_t = dot_nt(hot, mat)
        high_t = coef_t.astype(BF16)
        cft_ref[:, b * BLK : (b + 1) * BLK] = high_t
        cft_ref[:, points + b * BLK : points + (b + 1) * BLK] = (
            coef_t - high_t.astype(F32)
        ).astype(BF16)
    out = start_copy(cft_ref, cft_hbm, out_sem)
    for copy in inputs:
        copy.wait()
    x = x_ref[...]
    high = cf_ref[:, : 2 * HALO]
    low = cf_ref[:, window : window + 2 * HALO]
    for j in range(w_ref.shape[1] // TILE):
        at = slice(j * TILE, (j + 1) * TILE)
        p = dot(x, w_ref[:, at]).astype(BF16)
        for m in range(local):
            pm = p[2 * m * HALO : (2 * m + 2) * HALO]
            part_ref[m, :, at] = dot(high, pm) + dot(low, pm)
    out.wait()


def forward_kernel(
    odd_ref, w_ref, cfo_ref, part_ref, dpt_ref, summed_ref, hidden_ref, code_ref
):
    local, points, depth = part_ref.shape
    forecast = [jnp.zeros((VPAD, points), F32) for _ in range(local)]
    for j in range(depth // TILE):
        at = slice(j * TILE, (j + 1) * TILE)
        p = dot(odd_ref[...], w_ref[:, at]).astype(BF16)
        for m in range(local):
            pm = p[m * HALO : (m + 1) * HALO]
            s = part_ref[m, :, at] + dot(cfo_ref[...], jnp.concatenate([pm, pm], axis=0))
            summed_ref[m, :, at] = s
            t = jnp.tanh(s * (GELU_C + (GELU_C * 0.044715) * (s * s)))
            h = (0.5 * s * (1.0 + t)).astype(BF16)
            hidden_ref[m, :, at] = h
            forecast[m] = forecast[m] + dot_nt(dpt_ref[:, at], h)
    for m in range(local):
        f = forecast[m]
        largest = jnp.maximum(jnp.max(jnp.abs(f), axis=1, keepdims=True), 1e-30)
        power = jnp.ceil(jnp.log(largest) * (1.0 / math.log(2.0)) + 1e-3)
        power = jnp.broadcast_to(power, (VPAD, VPAD))
        q = f * (jnp.exp2(-power[:, :1]) * QMAX)
        q = jnp.where(q >= 0.0, q + 0.5, q - 0.5)
        row = jnp.concatenate([power.T[:8], jnp.zeros((8, points - VPAD), F32)], axis=1)
        row = jnp.where(row >= 0.0, row + 0.5, row - 0.5)
        code = jnp.concatenate([q[:VUSE], row], axis=0)
        code_ref[m] = code.astype(jnp.int32).astype(jnp.int16)


def factors_kernel(
    where_ref, lat_ref, clat_ref, olat_ref, cf_ref, summed_ref, hidden_ref,
    aggt_ref, hidt_ref, slope_ref, x_ref,
):
    core = where_ref[0]
    window = cf_ref.shape[1] // 2
    local, points, depth = summed_ref.shape
    high = cf_ref[:, :window]
    low = cf_ref[:, window:]
    for m in range(local):
        x_ref[:HALO] = lat_ref[m]
        x_ref[HALO : 2 * HALO] = clat_ref[m]
        x_ref[2 * HALO :] = olat_ref[m * HALO : (m + 1) * HALO]
        cols = slice(m * points, (m + 1) * points)
        for j in range(depth // TILE):
            at = slice(j * TILE, (j + 1) * TILE)
            x = x_ref[:, at]
            agg = (dot(high, x) + dot(low, x)).T.astype(BF16)
            hid = hidden_ref[m, :, at].astype(F32).T.astype(BF16)
            for k in range(TILE // 16):
                block = j * (TILE // 16) + k
                zhi, rest = divmod(block, 32)
                xy, c = divmod(rest, 2)
                to = lax.bitwise_xor(core, c) * (depth // 2) + (xy * 32 + zhi * 16)
                to = pl.ds(pl.multiple_of(to, 16), 16)
                aggt_ref[to, cols] = agg[k * 16 : (k + 1) * 16]
                hidt_ref[to, cols] = hid[k * 16 : (k + 1) * 16]
            s = summed_ref[m, :, at]
            t = jnp.tanh(s * (GELU_C + (GELU_C * 0.044715) * (s * s)))
            slope_ref[m, :, at] = 0.5 * (1.0 + t) + (0.5 * GELU_C) * s * (1.0 - t * t) * (
                1.0 + 3.0 * 0.044715 * (s * s)
            )


def decode(where_ref, code_refs, f_ref):
    local = code_refs[0].shape[0]
    rows = [
        ref[m, VROWS - 8 :, :].astype(jnp.int32).astype(F32)[:1, :VPAD]
        for ref in code_refs
        for m in range(local)
    ]
    rows.append(jnp.zeros((VPAD - len(rows), VPAD), F32))
    power = (jnp.exp2(jnp.concatenate(rows, axis=0)) * (1.0 / QMAX)).T
    for k, ref in enumerate(code_refs):
        first = lax.bitwise_xor(where_ref[1], k) * local
        for m in range(local):
            code = ref[m].astype(jnp.int32).astype(F32)[:VUSE]
            at = k * local + m
            f_ref[first + m] = code * power[:VUSE, at : at + 1]


def score_kernel(
    where_ref, c0_any, c1_any, c2_any, c3_any, truth_hbm, score_ref,
    c_ref, truth_ref, f_ref, in_sem,
):
    members = f_ref.shape[0]
    nvar = truth_ref.shape[0]
    codes = [c_ref.at[k] for k in range(4)]
    pairs = list(zip((c0_any, c1_any, c2_any, c3_any), codes)) + [(truth_hbm, truth_ref)]
    copies = [start_copy(src, dst, in_sem.at[k]) for k, (src, dst) in enumerate(pairs)]
    for copy in copies:
        copy.wait()
    decode(where_ref, codes, f_ref)
    collected = [f_ref[m][:nvar] for m in range(members)]
    truth = truth_ref[...]
    skill = sum(smooth_abs(f - truth) for f in collected)
    spread = jnp.zeros_like(skill)
    for m in range(members):
        for o in range(m + 1, members):
            spread = spread + smooth_abs(collected[m] - collected[o])
    score_ref[...] = skill * (1.0 / members) - (pair_factor(members) * 2.0) * spread


def backward_kernel(
    where_ref, c0_ref, c1_ref, c2_ref, c3_ref, truth_ref, var_ref, area_ref, dpt_ref,
    aggt_ref, hidt_ref, slope_ref, mine_ref, theirs_ref, sg_ref, f_ref, g_ref,
):
    members = f_ref.shape[0]
    nvar = truth_ref.shape[0]
    local, points, depth = slope_ref.shape
    half = depth // 2
    decode(where_ref, (c0_ref, c1_ref, c2_ref, c3_ref), f_ref)
    first = where_ref[1] * local
    truth = truth_ref[...]
    g_ref[96:] = jnp.zeros((VPAD - 96, points), F32)
    grads = []
    for m in range(local):
        own = f_ref[first + m][:nvar]
        mutual = sum(signum(own - f_ref[o][:nvar]) for o in range(members))
        g_ref[:nvar] = area_ref[...] * (
            signum(own - truth) * (1.0 / members) - (2.0 * pair_factor(members)) * mutual
        )
        grads.append((g_ref[...].T * var_ref[...]).astype(BF16))
    grad = jnp.concatenate(grads, axis=0)
    out = dot(hidt_ref[...], grad).astype(BF16)
    mine_ref[:, depth:] = out[:half]
    theirs_ref[:, depth:] = out[half:]
    for j in range(depth // TILE):
        at = slice(j * TILE, (j + 1) * TILE)
        hg = dot(grad, dpt_ref[:, at])
        for m in range(local):
            rows = slice(m * points, (m + 1) * points)
            sg_ref[rows, at] = (hg[rows] * slope_ref[m, :, at]).astype(BF16)
        part = dot(aggt_ref[...], sg_ref[:, at]).astype(BF16)
        mine_ref[:, at] = part[:half]
        theirs_ref[:, at] = part[half:]


def merge_kernel(mine_ref, theirs_ref, after_any, out_hbm, out_ref, out_sem):
    rows = mine_ref.shape[0] // 4
    outs = []
    for k in range(4):
        at = slice(k * rows, (k + 1) * rows)
        out_ref[at] = (mine_ref[at].astype(F32) + theirs_ref[at].astype(F32)).astype(BF16)
        cut = pl.ds(k * rows, rows)
        outs.append(start_copy(out_ref.at[cut], out_hbm.at[cut], out_sem.at[k]))
    for copy in outs:
        copy.wait()


def rows_kernel(cft_ref, sg_ref, core_hbm, odd_hbm, core_ref, odd_ref, out_sem):
    local, _, depth = core_ref.shape
    points = cft_ref.shape[1] // 2
    high = cft_ref[HALO:, :points]
    low = cft_ref[HALO:, points:]
    outs = []
    for m in range(local):
        for j in range(depth // TILE):
            at = slice(j * TILE, (j + 1) * TILE)
            s = sg_ref[m * points : (m + 1) * points, at]
            g = (dot(high, s) + dot(low, s)).astype(BF16)
            core_ref[m, :, at] = g[:HALO]
            odd_ref[m, :, at] = g[HALO:]
        outs.append(start_copy(odd_ref.at[m], odd_hbm.at[m], out_sem.at[0, m]))
        outs.append(start_copy(core_ref.at[m], core_hbm.at[m], out_sem.at[1, m]))
    for copy in outs:
        copy.wait()


def plane_kernel(got_ref, out_hbm, out_ref, out_sem):
    per = out_hbm.shape[2]
    outs = []
    for z in range(out_hbm.shape[0]):
        at = slice(z * per, (z + 1) * per)
        total = got_ref[0, at].astype(F32)
        for k in range(1, got_ref.shape[0]):
            total = total + got_ref[k, at].astype(F32)
        out_ref[z] = total.astype(BF16)
        for e in range(out_hbm.shape[1]):
            outs.append(start_copy(out_ref.at[z], out_hbm.at[z, e], out_sem.at[z, e]))
    for copy in outs:
        copy.wait()


def final_kernel(got_ref, src_ref, out_ref, *, scaling):
    total = got_ref[0].astype(F32)
    for k in range(1, got_ref.shape[0]):
        total = total + got_ref[k].astype(F32)
    total = total * scaling
    depth = src_ref.shape[1]
    src_ref[...] = total[:, :depth]
    out_ref[...] = total[:, depth : depth + out_ref.shape[1]]


def latent_kernel(
    cft_hbm, sg_hbm, w_hbm, core_any, far_any, near_any, out_hbm,
    cft_ref, sg_ref, w_ref, core_ref, far_ref, near_ref, g_ref, out_ref, in_sem, out_sem,
):
    local, rows, depth = core_ref.shape
    points = cft_ref.shape[1] // 2
    steps = depth // TILE
    pairs = (
        (cft_hbm.at[pl.ds(0, HALO)], cft_ref), (sg_hbm, sg_ref), (core_any, core_ref),
        (far_any, far_ref), (near_any, near_ref), (w_hbm, w_ref),
    )
    copies = [start_copy(src, dst, in_sem.at[k]) for k, (src, dst) in enumerate(pairs)]
    for copy in copies[:5]:
        copy.wait()
    high = cft_ref[:, :points]
    low = cft_ref[:, points:]
    for m in range(local):
        for j in range(steps):
            at = slice(j * TILE, (j + 1) * TILE)
            s = sg_ref[m * points : (m + 1) * points, at]
            g = dot(high, s) + dot(low, s)
            for ref in (core_ref, far_ref, near_ref):
                g = g + ref[m, :, at].astype(F32)
            g_ref[m * HALO : (m + 1) * HALO, at] = g.astype(BF16)
    copies[5].wait()
    outs = []
    for j in range(steps):
        at = slice(j * TILE, (j + 1) * TILE)
        r = dot_nt(g_ref[...], w_ref[at, :]).astype(BF16)
        for m in range(local):
            out_ref[m, :, at] = r[m * HALO : (m + 1) * HALO]
        cols = pl.ds(j * TILE, TILE)
        outs.append(start_copy(out_ref.at[:, :, cols], out_hbm.at[:, :, cols], out_sem.at[j]))
    for copy in outs:
        copy.wait()


def shape(dims, dtype):
    return jax.ShapeDtypeStruct(dims, dtype)


def scratch(*arrays):
    return [pltpu.VMEM(a.shape, a.dtype) for a in arrays]


def sems(*dims):
    return pltpu.SemaphoreType.DMA(dims)


def call(
    kernel, name, out_shape, in_specs, out_specs, scratch_shapes, work, operands, limit=LIMIT
):
    return pl.pallas_call(
        kernel,
        out_shape=out_shape,
        in_specs=in_specs,
        out_specs=out_specs,
        scratch_shapes=scratch_shapes,
        compiler_params=params(limit),
        cost_estimate=cost(*work),
        name=name,
    )(*operands)


def call_prepare(where, edge_count, edge_src, edge_dst, edge_weight, latent, core_lat, weight):
    local, rows, depth = latent.shape
    window = rows + 2 * HALO
    points = edge_src.shape[0] * BLK
    cf = shape((points, 2 * window), BF16)
    cft = shape((window, 2 * points), BF16)
    return call(
        prepare_kernel,
        "prepare",
        (cf, cft, shape((points, 2 * HALO), BF16), shape((local, points, depth), F32)),
        smem(1) + hbm(5) + anywhere(1) + hbm(1),
        tuple(vmem(1) + hbm(1) + vmem(2)),
        [pltpu.SMEM(edge_count.shape, jnp.int32)]
        + scratch(edge_src, edge_dst, edge_weight)
        + [pltpu.VMEM((local * 2 * HALO, depth), BF16)]
        + scratch(weight, cft)
        + [sems(5 + 2 * local), pltpu.SemaphoreType.DMA],
        (3 * 10**9, 6 * 10**6),
        (where, edge_count, edge_src, edge_dst, edge_weight, latent, core_lat, weight),
        PREP,
    )


def call_forward(odd_lat, weight, cfo, part, dpt):
    local, points, depth = part.shape
    return call(
        forward_kernel,
        "forward",
        (
            shape(part.shape, F32),
            shape(part.shape, BF16),
            shape((local, VROWS, points), jnp.int16),
        ),
        vmem(5),
        tuple(vmem(3)),
        [],
        (2 * 10**9, 8 * 10**6),
        (odd_lat, weight, cfo, part, dpt),
    )


def call_factors(where, latent, core_lat, odd_lat, cf, summed, hidden):
    local, points, depth = summed.shape
    left = shape((depth, local * points), BF16)
    return call(
        factors_kernel,
        "factors",
        (left, left, shape(summed.shape, F32)),
        smem(1) + vmem(6),
        tuple(vmem(3)),
        [pltpu.VMEM((cf.shape[1] // 2, depth), BF16)],
        (3 * 10**9, 10 * 10**6),
        (where, latent, core_lat, odd_lat, cf, summed, hidden),
    )


def call_backward(where, codes, truth, var_row, area_row, dpt, aggt, hidt, slope):
    local, points, depth = slope.shape
    part = shape((depth // 2, depth + VPAD), BF16)
    return call(
        backward_kernel,
        "backward",
        (part, part, shape((local * points, depth), BF16)),
        smem(1) + vmem(len(codes) + 7),
        tuple(vmem(3)),
        [
            pltpu.VMEM((local * len(codes), VUSE, points), F32),
            pltpu.VMEM((VPAD, points), F32),
        ],
        (2 * 10**9, 5 * 10**6),
        (where, *codes, truth, var_row, area_row, dpt, aggt, hidt, slope),
    )


def call_merge(mine, theirs, after):
    return call(
        merge_kernel,
        "merge",
        shape(mine.shape, BF16),
        vmem(2) + anywhere(1),
        hbm(1)[0],
        scratch(mine) + [sems(4)],
        (10**6, 4 * 10**6),
        (mine, theirs, after),
    )


def call_rows(cft, summed_grad, local):
    send = shape((local, HALO, summed_grad.shape[1]), BF16)
    return call(
        rows_kernel,
        "rows",
        (send, send),
        vmem(2),
        tuple(hbm(2)),
        scratch(send, send) + [sems(2, local)],
        (10**9, 3 * 10**6),
        (cft, summed_grad),
    )


def call_plane(got, ens):
    out_shape = shape((2, ens, got.shape[1] // 2, got.shape[2]), BF16)
    return call(
        plane_kernel,
        "plane",
        out_shape,
        vmem(1),
        hbm(1)[0],
        [pltpu.VMEM((2,) + out_shape.shape[2:], BF16), sems(2, ens)],
        (10**6, 10**6),
        (got,),
    )


def call_score(where, codes, truth):
    local, _, points = codes[0].shape
    return call(
        score_kernel,
        "score",
        shape(truth.shape, F32),
        smem(1) + anywhere(len(codes)) + hbm(1),
        vmem(1)[0],
        [pltpu.VMEM((len(codes),) + codes[0].shape, jnp.int16)]
        + scratch(truth)
        + [pltpu.VMEM((local * len(codes), VUSE, points), F32), sems(len(codes) + 1)],
        (10**7, 10**6),
        (where, *codes, truth),
        LARGE,
    )


def call_latent(cft, summed_grad, weight, core_grad, far_grad, near_grad):
    local, rows, depth = core_grad.shape
    return call(
        latent_kernel,
        "latent",
        shape(core_grad.shape, BF16),
        hbm(3) + anywhere(3),
        hbm(1)[0],
        [pltpu.VMEM((HALO, cft.shape[1]), BF16)]
        + scratch(summed_grad, weight, core_grad, far_grad, near_grad)
        + [pltpu.VMEM((local * rows, depth), BF16)]
        + scratch(core_grad)
        + [sems(6), sems(depth // TILE)],
        (10**9, 5 * 10**6),
        (cft, summed_grad, weight, core_grad, far_grad, near_grad),
        LARGE,
    )


def call_final(got, nvar, scaling):
    per = got.shape[1]
    return call(
        functools.partial(final_kernel, scaling=scaling),
        "final",
        (shape((per, got.shape[2] - VPAD), F32), shape((per, nvar), F32)),
        vmem(1),
        tuple(vmem(2)),
        [],
        (10**5, 4 * 10**5),
        (got,),
    )


def make_body(count):
    odd_pairs = [(i, (i + 1) % count if i % 2 else (i - 1) % count) for i in range(count)]
    far = [p for p in odd_pairs if abs(p[0] - p[1]) > 1 or p[0] // 32 != p[1] // 32]
    near = [p for p in odd_pairs if p not in far]
    swap = [(0, 1), (1, 0)]

    def body(
        latent, src_weight, decoder_projection, truth, area_weight, var_weight,
        edge_src, edge_dst, edge_weight, edge_count,
    ):
        local, rows, depth = latent.shape
        ens = lax.axis_size("ens")
        members = local * ens
        nvar = decoder_projection.shape[1]
        points = truth.shape[1]
        per = depth // count
        where = jnp.stack([lax.axis_index("core"), lax.axis_index("ens")]).astype(jnp.int32)

        odd_lat = lax.ppermute(latent, SPACE, odd_pairs).reshape(local * rows, depth)
        core_lat = lax.ppermute(latent, "core", swap)
        dpt = jnp.pad(decoder_projection.T, ((0, VPAD - nvar), (0, 0)))
        cf, cft, cfo, part = call_prepare(
            where, edge_count, edge_src, edge_dst, edge_weight, latent, core_lat, src_weight
        )
        var_row = jnp.pad(var_weight, (0, VPAD - nvar)).reshape(1, VPAD)
        area_row = area_weight.reshape(1, points)
        summed, hidden, coded = call_forward(odd_lat, src_weight, cfo, part, dpt)
        codes = [coded] + [
            lax.ppermute(coded, "ens", [(e, e ^ k) for e in range(ens)]) for k in range(1, ens)
        ]
        aggt, hidt, slope = call_factors(
            where, latent, core_lat, odd_lat, cf, summed, hidden
        )
        mine, theirs, summed_grad = call_backward(
            where, codes, truth, var_row, area_row, dpt, aggt, hidt, slope
        )
        theirs = lax.ppermute(theirs, "core", swap)
        core_send, odd_send = call_rows(cft, summed_grad, local)
        near_grad = lax.ppermute(odd_send, SPACE, near)
        part = call_merge(mine, theirs, odd_send)
        part, odd_send, core_send = lax.optimization_barrier((part, odd_send, core_send))
        part = part.reshape(16, 2 * per, part.shape[1])
        got = lax.all_to_all(part, ("x", "y"), 0, 0, tiled=True)
        far_grad = lax.ppermute(odd_send, SPACE, far)
        core_grad = lax.ppermute(core_send, "core", swap)
        plane = call_plane(got, ens).reshape(2 * ens, per, got.shape[2])
        got = lax.all_to_all(plane, ("zhi", "ens"), 0, 0, tiled=True)
        score = call_score(where, codes, truth)
        grad_latent = call_latent(cft, summed_grad, src_weight, core_grad, far_grad, near_grad)
        scaling = 1.0 / math.sqrt(members * points * count)
        grad_src, grad_out = call_final(got, nvar, scaling)
        return score, grad_latent, grad_src, grad_out

    return body


def solution(mesh):
    fine = jax.sharding.Mesh(
        mesh.devices.reshape(mesh.devices.shape[0], 2, 4, 4, 2), ("ens",) + SPACE
    )
    return jax.shard_map(
        make_body(mesh.devices.shape[1]),
        mesh=fine,
        in_specs=(
            P("ens", SPACE, None), P(), P(), P(None, SPACE), P(SPACE), P(),
            P(SPACE, None), P(SPACE, None), P(SPACE, None), P(SPACE),
        ),
        out_specs=(P(None, SPACE), P("ens", SPACE, None), P(SPACE, None), P(SPACE, None)),
        check_vma=False,
    )
```

```python
import functools
import math

import jax
import jax.numpy as jnp
from jax import lax
from jax.experimental import pallas as pl
from jax.experimental.pallas import tpu as pltpu
from jax.sharding import PartitionSpec as P

HALO = 128
BLK = 128
ALPHA = 0.95
DELTA = 0.05
SPACE = ("zhi", "x", "y", "core")
QMAX = 32000.0
VPAD = 128
VROWS = 112
VUSE = 104
TILE = 256
GELU_C = math.sqrt(2.0 / math.pi)
MIB = 1 << 20
LIMIT = 24
PREP = 50
LARGE = 56
F32 = jnp.float32
BF16 = jnp.bfloat16


def dot(a, b):
    return jnp.dot(a, b, preferred_element_type=F32)


def dot_nt(a, b):
    return lax.dot_general(a, b, (((1,), (1,)), ((), ())), preferred_element_type=F32)


def smem(count):
    return [pl.BlockSpec(memory_space=pltpu.SMEM)] * count


def cost(flops, nbytes):
    return pl.CostEstimate(flops=flops, bytes_accessed=nbytes, transcendentals=0)


def params(mib):
    return pltpu.CompilerParams(vmem_limit_bytes=mib * MIB)


def hbm(count):
    return [pl.BlockSpec(memory_space=pltpu.HBM)] * count


def vmem(count):
    return [pl.BlockSpec(memory_space=pltpu.VMEM)] * count


def anywhere(count):
    return [pl.BlockSpec(memory_space=pl.ANY)] * count


def start_copy(src, dst, sem):
    copy = pltpu.make_async_copy(src, dst, sem)
    copy.start()
    return copy


def pair_factor(members):
    fair_eps = (1.0 - ALPHA) / members
    return (1.0 - fair_eps) / (2.0 * members * (members - 1))


def smooth_abs(distance):
    square = distance * distance + DELTA * DELTA
    return square * lax.rsqrt(square)


def signum(distance):
    return distance * lax.rsqrt(distance * distance + DELTA * DELTA)


def prepare_kernel(
    where_ref, count_hbm, src_hbm, dst_hbm, wt_hbm, lat_hbm, clat_hbm, w_hbm,
    cf_ref, cft_hbm, cfo_ref, part_ref,
    count_ref, src_ref, dst_ref, wt_ref, x_ref, w_ref, cft_ref, in_sem, out_sem,
):
    edges = [
        start_copy(src, dst, in_sem.at[k])
        for k, (src, dst) in enumerate(
            ((count_hbm, count_ref), (src_hbm, src_ref), (dst_hbm, dst_ref), (wt_hbm, wt_ref))
        )
    ]
    local = lat_hbm.shape[0]
    inputs = []
    for m in range(local):
        for k, ref in enumerate((lat_hbm, clat_hbm)):
            inputs.append(
                start_copy(
                    ref.at[m],
                    x_ref.at[pl.ds((2 * m + k) * HALO, HALO)],
                    in_sem.at[4 + 2 * m + k],
                )
            )
    inputs.append(start_copy(w_hbm, w_ref, in_sem.at[4 + 2 * local]))
    core = where_ref[0]
    slots = src_ref.shape[1]
    window = cf_ref.shape[1] // 2
    points = cf_ref.shape[0]
    for copy in edges:
        copy.wait()
    for b in range(src_ref.shape[0]):
        src = src_ref[b : b + 1, :]
        slot = lax.broadcasted_iota(jnp.int32, (1, slots), 1)
        wt = jnp.where(slot < count_ref[b], wt_ref[b : b + 1, :], 0.0)
        left = 2 * HALO - HALO * core
        right = HALO + HALO * core
        place = jnp.where(
            src < HALO,
            src + left,
            jnp.where(src < 2 * HALO, src - HALO, src - 2 * HALO + right),
        )
        rows = lax.broadcasted_iota(jnp.int32, (window, slots), 0)
        hot = jnp.where(rows == place, 1.0, 0.0).astype(BF16)
        pts = lax.broadcasted_iota(jnp.int32, (BLK, slots), 0)
        mat = jnp.where(pts == dst_ref[b : b + 1, :], wt, 0.0).astype(BF16)
        coef = dot_nt(mat, hot)
        high = coef.astype(BF16)
        low = (coef - high.astype(F32)).astype(BF16)
        at = slice(b * BLK, (b + 1) * BLK)
        cf_ref[at, :window] = high
        cf_ref[at, window:] = low
        cfo_ref[at, :HALO] = high[:, 2 * HALO :]
        cfo_ref[at, HALO:] = low[:, 2 * HALO :]
        coef_t = dot_nt(hot, mat)
        high_t = coef_t.astype(BF16)
        cft_ref[:, b * BLK : (b + 1) * BLK] = high_t
        cft_ref[:, points + b * BLK : points + (b + 1) * BLK] = (
            coef_t - high_t.astype(F32)
        ).astype(BF16)
    out = start_copy(cft_ref, cft_hbm, out_sem)
    for copy in inputs:
        copy.wait()
    x = x_ref[...]
    high = cf_ref[:, : 2 * HALO]
    low = cf_ref[:, window : window + 2 * HALO]
    for j in range(w_ref.shape[1] // TILE):
        at = slice(j * TILE, (j + 1) * TILE)
        p = dot(x, w_ref[:, at]).astype(BF16)
        for m in range(local):
            pm = p[2 * m * HALO : (2 * m + 2) * HALO]
            part_ref[m, :, at] = dot(high, pm) + dot(low, pm)
    out.wait()


def forward_kernel(
    odd_ref, w_ref, cfo_ref, part_ref, dpt_ref, summed_ref, hidden_ref, code_ref
):
    local, points, depth = part_ref.shape
    forecast = [jnp.zeros((VPAD, points), F32) for _ in range(local)]
    for j in range(depth // TILE):
        at = slice(j * TILE, (j + 1) * TILE)
        p = dot(odd_ref[...], w_ref[:, at]).astype(BF16)
        for m in range(local):
            pm = p[m * HALO : (m + 1) * HALO]
            s = part_ref[m, :, at] + dot(cfo_ref[...], jnp.concatenate([pm, pm], axis=0))
            summed_ref[m, :, at] = s
            t = jnp.tanh(s * (GELU_C + (GELU_C * 0.044715) * (s * s)))
            h = (0.5 * s * (1.0 + t)).astype(BF16)
            hidden_ref[m, :, at] = h
            forecast[m] = forecast[m] + dot_nt(dpt_ref[:, at], h)
    for m in range(local):
        f = forecast[m]
        largest = jnp.maximum(jnp.max(jnp.abs(f), axis=1, keepdims=True), 1e-30)
        power = jnp.ceil(jnp.log(largest) * (1.0 / math.log(2.0)) + 1e-3)
        power = jnp.broadcast_to(power, (VPAD, VPAD))
        q = f * (jnp.exp2(-power[:, :1]) * QMAX)
        q = jnp.where(q >= 0.0, q + 0.5, q - 0.5)
        row = jnp.concatenate([power.T[:8], jnp.zeros((8, points - VPAD), F32)], axis=1)
        row = jnp.where(row >= 0.0, row + 0.5, row - 0.5)
        code = jnp.concatenate([q[:VUSE], row], axis=0)
        code_ref[m] = code.astype(jnp.int32).astype(jnp.int16)


def factors_kernel(
    where_ref, lat_ref, clat_ref, olat_ref, cf_ref, summed_ref, hidden_ref,
    aggt_ref, hidt_ref, slope_ref, x_ref,
):
    core = where_ref[0]
    window = cf_ref.shape[1] // 2
    local, points, depth = summed_ref.shape
    high = cf_ref[:, :window]
    low = cf_ref[:, window:]
    for m in range(local):
        x_ref[:HALO] = lat_ref[m]
        x_ref[HALO : 2 * HALO] = clat_ref[m]
        x_ref[2 * HALO :] = olat_ref[m * HALO : (m + 1) * HALO]
        cols = slice(m * points, (m + 1) * points)
        for j in range(depth // TILE):
            at = slice(j * TILE, (j + 1) * TILE)
            x = x_ref[:, at]
            agg = (dot(high, x) + dot(low, x)).T.astype(BF16)
            hid = hidden_ref[m, :, at].astype(F32).T.astype(BF16)
            for k in range(TILE // 16):
                block = j * (TILE // 16) + k
                zhi, rest = divmod(block, 32)
                xy, c = divmod(rest, 2)
                to = lax.bitwise_xor(core, c) * (depth // 2) + (xy * 32 + zhi * 16)
                to = pl.ds(pl.multiple_of(to, 16), 16)
                aggt_ref[to, cols] = agg[k * 16 : (k + 1) * 16]
                hidt_ref[to, cols] = hid[k * 16 : (k + 1) * 16]
            s = summed_ref[m, :, at]
            t = jnp.tanh(s * (GELU_C + (GELU_C * 0.044715) * (s * s)))
            slope_ref[m, :, at] = 0.5 * (1.0 + t) + (0.5 * GELU_C) * s * (1.0 - t * t) * (
                1.0 + 3.0 * 0.044715 * (s * s)
            )


def decode(where_ref, code_refs, f_ref):
    local = code_refs[0].shape[0]
    rows = [
        ref[m, VROWS - 8 :, :].astype(jnp.int32).astype(F32)[:1, :VPAD]
        for ref in code_refs
        for m in range(local)
    ]
    rows.append(jnp.zeros((VPAD - len(rows), VPAD), F32))
    power = (jnp.exp2(jnp.concatenate(rows, axis=0)) * (1.0 / QMAX)).T
    for k, ref in enumerate(code_refs):
        first = lax.bitwise_xor(where_ref[1], k) * local
        for m in range(local):
            code = ref[m].astype(jnp.int32).astype(F32)[:VUSE]
            at = k * local + m
            f_ref[first + m] = code * power[:VUSE, at : at + 1]


def score_kernel(
    where_ref, c0_any, c1_any, c2_any, c3_any, truth_hbm, score_ref,
    c_ref, truth_ref, f_ref, in_sem,
):
    members = f_ref.shape[0]
    nvar = truth_ref.shape[0]
    codes = [c_ref.at[k] for k in range(4)]
    pairs = list(zip((c0_any, c1_any, c2_any, c3_any), codes)) + [(truth_hbm, truth_ref)]
    copies = [start_copy(src, dst, in_sem.at[k]) for k, (src, dst) in enumerate(pairs)]
    for copy in copies:
        copy.wait()
    decode(where_ref, codes, f_ref)
    collected = [f_ref[m][:nvar] for m in range(members)]
    truth = truth_ref[...]
    skill = sum(smooth_abs(f - truth) for f in collected)
    spread = jnp.zeros_like(skill)
    for m in range(members):
        for o in range(m + 1, members):
            spread = spread + smooth_abs(collected[m] - collected[o])
    score_ref[...] = skill * (1.0 / members) - (pair_factor(members) * 2.0) * spread


def backward_kernel(
    where_ref, c0_ref, c1_ref, c2_ref, c3_ref, truth_ref, var_ref, area_ref, dpt_ref,
    aggt_ref, hidt_ref, slope_ref, theirs_ref, sg_ref, grad_ref, f_ref, g_ref,
):
    members = f_ref.shape[0]
    nvar = truth_ref.shape[0]
    local, points, depth = slope_ref.shape
    half = depth // 2
    decode(where_ref, (c0_ref, c1_ref, c2_ref, c3_ref), f_ref)
    first = where_ref[1] * local
    truth = truth_ref[...]
    g_ref[96:] = jnp.zeros((VPAD - 96, points), F32)
    grads = []
    for m in range(local):
        own = f_ref[first + m][:nvar]
        mutual = sum(signum(own - f_ref[o][:nvar]) for o in range(members))
        g_ref[:nvar] = area_ref[...] * (
            signum(own - truth) * (1.0 / members) - (2.0 * pair_factor(members)) * mutual
        )
        grads.append((g_ref[...].T * var_ref[...]).astype(BF16))
    grad = jnp.concatenate(grads, axis=0)
    grad_ref[...] = grad
    theirs_ref[:, depth:] = dot(hidt_ref[half:], grad).astype(BF16)
    for j in range(depth // TILE):
        at = slice(j * TILE, (j + 1) * TILE)
        hg = dot(grad, dpt_ref[:, at])
        for m in range(local):
            rows = slice(m * points, (m + 1) * points)
            sg_ref[rows, at] = (hg[rows] * slope_ref[m, :, at]).astype(BF16)
        theirs_ref[:, at] = dot(aggt_ref[half:], sg_ref[:, at]).astype(BF16)


def mine_kernel(grad_ref, sg_ref, aggt_ref, hidt_ref, mine_ref):
    half, cols = mine_ref.shape
    depth = sg_ref.shape[1]
    mine_ref[:, depth:] = dot(hidt_ref[:half], grad_ref[...]).astype(BF16)
    for j in range(depth // TILE):
        at = slice(j * TILE, (j + 1) * TILE)
        mine_ref[:, at] = dot(aggt_ref[:half], sg_ref[:, at]).astype(BF16)


def merge_kernel(mine_ref, theirs_ref, after_any, out_hbm, out_ref, out_sem):
    rows = mine_ref.shape[0] // 4
    outs = []
    for k in range(4):
        at = slice(k * rows, (k + 1) * rows)
        out_ref[at] = (mine_ref[at].astype(F32) + theirs_ref[at].astype(F32)).astype(BF16)
        cut = pl.ds(k * rows, rows)
        outs.append(start_copy(out_ref.at[cut], out_hbm.at[cut], out_sem.at[k]))
    for copy in outs:
        copy.wait()


def rows_kernel(cft_ref, sg_ref, core_hbm, odd_hbm, core_ref, odd_ref, out_sem):
    local, _, depth = core_ref.shape
    points = cft_ref.shape[1] // 2
    high = cft_ref[HALO:, :points]
    low = cft_ref[HALO:, points:]
    outs = []
    for m in range(local):
        for j in range(depth // TILE):
            at = slice(j * TILE, (j + 1) * TILE)
            s = sg_ref[m * points : (m + 1) * points, at]
            g = (dot(high, s) + dot(low, s)).astype(BF16)
            core_ref[m, :, at] = g[:HALO]
            odd_ref[m, :, at] = g[HALO:]
        outs.append(start_copy(odd_ref.at[m], odd_hbm.at[m], out_sem.at[0, m]))
        outs.append(start_copy(core_ref.at[m], core_hbm.at[m], out_sem.at[1, m]))
    for copy in outs:
        copy.wait()


def plane_kernel(got_ref, out_hbm, out_ref, out_sem):
    per = out_hbm.shape[2]
    outs = []
    for z in range(out_hbm.shape[0]):
        at = slice(z * per, (z + 1) * per)
        total = got_ref[0, at].astype(F32)
        for k in range(1, got_ref.shape[0]):
            total = total + got_ref[k, at].astype(F32)
        out_ref[z] = total.astype(BF16)
        for e in range(out_hbm.shape[1]):
            outs.append(start_copy(out_ref.at[z], out_hbm.at[z, e], out_sem.at[z, e]))
    for copy in outs:
        copy.wait()


def final_kernel(got_ref, src_ref, out_ref, *, scaling):
    total = got_ref[0].astype(F32)
    for k in range(1, got_ref.shape[0]):
        total = total + got_ref[k].astype(F32)
    total = total * scaling
    depth = src_ref.shape[1]
    src_ref[...] = total[:, :depth]
    out_ref[...] = total[:, depth : depth + out_ref.shape[1]]


def latent_kernel(
    cft_hbm, sg_hbm, w_hbm, core_any, far_any, near_any, out_hbm,
    cft_ref, sg_ref, w_ref, core_ref, far_ref, near_ref, g_ref, out_ref, in_sem, out_sem,
):
    local, rows, depth = core_ref.shape
    points = cft_ref.shape[1] // 2
    steps = depth // TILE
    pairs = (
        (cft_hbm.at[pl.ds(0, HALO)], cft_ref), (sg_hbm, sg_ref), (core_any, core_ref),
        (far_any, far_ref), (near_any, near_ref), (w_hbm, w_ref),
    )
    copies = [start_copy(src, dst, in_sem.at[k]) for k, (src, dst) in enumerate(pairs)]
    for copy in copies[:5]:
        copy.wait()
    high = cft_ref[:, :points]
    low = cft_ref[:, points:]
    for m in range(local):
        for j in range(steps):
            at = slice(j * TILE, (j + 1) * TILE)
            s = sg_ref[m * points : (m + 1) * points, at]
            g = dot(high, s) + dot(low, s)
            for ref in (core_ref, far_ref, near_ref):
                g = g + ref[m, :, at].astype(F32)
            g_ref[m * HALO : (m + 1) * HALO, at] = g.astype(BF16)
    copies[5].wait()
    outs = []
    for j in range(steps):
        at = slice(j * TILE, (j + 1) * TILE)
        r = dot_nt(g_ref[...], w_ref[at, :]).astype(BF16)
        for m in range(local):
            out_ref[m, :, at] = r[m * HALO : (m + 1) * HALO]
        cols = pl.ds(j * TILE, TILE)
        outs.append(start_copy(out_ref.at[:, :, cols], out_hbm.at[:, :, cols], out_sem.at[j]))
    for copy in outs:
        copy.wait()


def shape(dims, dtype):
    return jax.ShapeDtypeStruct(dims, dtype)


def scratch(*arrays):
    return [pltpu.VMEM(a.shape, a.dtype) for a in arrays]


def sems(*dims):
    return pltpu.SemaphoreType.DMA(dims)


def call(
    kernel, name, out_shape, in_specs, out_specs, scratch_shapes, work, operands, limit=LIMIT
):
    return pl.pallas_call(
        kernel,
        out_shape=out_shape,
        in_specs=in_specs,
        out_specs=out_specs,
        scratch_shapes=scratch_shapes,
        compiler_params=params(limit),
        cost_estimate=cost(*work),
        name=name,
    )(*operands)


def call_prepare(where, edge_count, edge_src, edge_dst, edge_weight, latent, core_lat, weight):
    local, rows, depth = latent.shape
    window = rows + 2 * HALO
    points = edge_src.shape[0] * BLK
    cf = shape((points, 2 * window), BF16)
    cft = shape((window, 2 * points), BF16)
    return call(
        prepare_kernel,
        "prepare",
        (cf, cft, shape((points, 2 * HALO), BF16), shape((local, points, depth), F32)),
        smem(1) + hbm(5) + anywhere(1) + hbm(1),
        tuple(vmem(1) + hbm(1) + vmem(2)),
        [pltpu.SMEM(edge_count.shape, jnp.int32)]
        + scratch(edge_src, edge_dst, edge_weight)
        + [pltpu.VMEM((local * 2 * HALO, depth), BF16)]
        + scratch(weight, cft)
        + [sems(5 + 2 * local), pltpu.SemaphoreType.DMA],
        (3 * 10**9, 6 * 10**6),
        (where, edge_count, edge_src, edge_dst, edge_weight, latent, core_lat, weight),
        PREP,
    )


def call_forward(odd_lat, weight, cfo, part, dpt):
    local, points, depth = part.shape
    return call(
        forward_kernel,
        "forward",
        (
            shape(part.shape, F32),
            shape(part.shape, BF16),
            shape((local, VROWS, points), jnp.int16),
        ),
        vmem(5),
        tuple(vmem(3)),
        [],
        (2 * 10**9, 8 * 10**6),
        (odd_lat, weight, cfo, part, dpt),
    )


def call_factors(where, latent, core_lat, odd_lat, cf, summed, hidden):
    local, points, depth = summed.shape
    left = shape((depth, local * points), BF16)
    return call(
        factors_kernel,
        "factors",
        (left, left, shape(summed.shape, F32)),
        smem(1) + vmem(6),
        tuple(vmem(3)),
        [pltpu.VMEM((cf.shape[1] // 2, depth), BF16)],
        (3 * 10**9, 10 * 10**6),
        (where, latent, core_lat, odd_lat, cf, summed, hidden),
    )


def call_backward(where, codes, truth, var_row, area_row, dpt, aggt, hidt, slope):
    local, points, depth = slope.shape
    part = shape((depth // 2, depth + VPAD), BF16)
    return call(
        backward_kernel,
        "backward",
        (part, shape((local * points, depth), BF16), shape((local * points, VPAD), BF16)),
        smem(1) + vmem(len(codes) + 7),
        tuple(vmem(3)),
        [
            pltpu.VMEM((local * len(codes), VUSE, points), F32),
            pltpu.VMEM((VPAD, points), F32),
        ],
        (2 * 10**9, 5 * 10**6),
        (where, *codes, truth, var_row, area_row, dpt, aggt, hidt, slope),
    )


def call_mine(grad, summed_grad, aggt, hidt):
    return call(
        mine_kernel,
        "mine",
        shape((aggt.shape[0] // 2, summed_grad.shape[1] + VPAD), BF16),
        vmem(4),
        vmem(1)[0],
        [],
        (10**9, 4 * 10**6),
        (grad, summed_grad, aggt, hidt),
    )


def call_merge(mine, theirs, after):
    return call(
        merge_kernel,
        "merge",
        shape(mine.shape, BF16),
        vmem(2) + anywhere(1),
        hbm(1)[0],
        scratch(mine) + [sems(4)],
        (10**6, 4 * 10**6),
        (mine, theirs, after),
    )


def call_rows(cft, summed_grad, local):
    send = shape((local, HALO, summed_grad.shape[1]), BF16)
    return call(
        rows_kernel,
        "rows",
        (send, send),
        vmem(2),
        tuple(hbm(2)),
        scratch(send, send) + [sems(2, local)],
        (10**9, 3 * 10**6),
        (cft, summed_grad),
    )


def call_plane(got, ens):
    out_shape = shape((2, ens, got.shape[1] // 2, got.shape[2]), BF16)
    return call(
        plane_kernel,
        "plane",
        out_shape,
        vmem(1),
        hbm(1)[0],
        [pltpu.VMEM((2,) + out_shape.shape[2:], BF16), sems(2, ens)],
        (10**6, 10**6),
        (got,),
    )


def call_score(where, codes, truth):
    local, _, points = codes[0].shape
    return call(
        score_kernel,
        "score",
        shape(truth.shape, F32),
        smem(1) + anywhere(len(codes)) + hbm(1),
        vmem(1)[0],
        [pltpu.VMEM((len(codes),) + codes[0].shape, jnp.int16)]
        + scratch(truth)
        + [pltpu.VMEM((local * len(codes), VUSE, points), F32), sems(len(codes) + 1)],
        (10**7, 10**6),
        (where, *codes, truth),
        LARGE,
    )


def call_latent(cft, summed_grad, weight, core_grad, far_grad, near_grad):
    local, rows, depth = core_grad.shape
    return call(
        latent_kernel,
        "latent",
        shape(core_grad.shape, BF16),
        hbm(3) + anywhere(3),
        hbm(1)[0],
        [pltpu.VMEM((HALO, cft.shape[1]), BF16)]
        + scratch(summed_grad, weight, core_grad, far_grad, near_grad)
        + [pltpu.VMEM((local * rows, depth), BF16)]
        + scratch(core_grad)
        + [sems(6), sems(depth // TILE)],
        (10**9, 5 * 10**6),
        (cft, summed_grad, weight, core_grad, far_grad, near_grad),
        LARGE,
    )


def call_final(got, nvar, scaling):
    per = got.shape[1]
    return call(
        functools.partial(final_kernel, scaling=scaling),
        "final",
        (shape((per, got.shape[2] - VPAD), F32), shape((per, nvar), F32)),
        vmem(1),
        tuple(vmem(2)),
        [],
        (10**5, 4 * 10**5),
        (got,),
    )


def make_body(count):
    odd_pairs = [(i, (i + 1) % count if i % 2 else (i - 1) % count) for i in range(count)]
    far = [p for p in odd_pairs if abs(p[0] - p[1]) > 1 or p[0] // 32 != p[1] // 32]
    near = [p for p in odd_pairs if p not in far]
    swap = [(0, 1), (1, 0)]

    def body(
        latent, src_weight, decoder_projection, truth, area_weight, var_weight,
        edge_src, edge_dst, edge_weight, edge_count,
    ):
        local, rows, depth = latent.shape
        ens = lax.axis_size("ens")
        members = local * ens
        nvar = decoder_projection.shape[1]
        points = truth.shape[1]
        per = depth // count
        where = jnp.stack([lax.axis_index("core"), lax.axis_index("ens")]).astype(jnp.int32)

        odd_lat = lax.ppermute(latent, SPACE, odd_pairs).reshape(local * rows, depth)
        core_lat = lax.ppermute(latent, "core", swap)
        dpt = jnp.pad(decoder_projection.T, ((0, VPAD - nvar), (0, 0)))
        cf, cft, cfo, part = call_prepare(
            where, edge_count, edge_src, edge_dst, edge_weight, latent, core_lat, src_weight
        )
        var_row = jnp.pad(var_weight, (0, VPAD - nvar)).reshape(1, VPAD)
        area_row = area_weight.reshape(1, points)
        summed, hidden, coded = call_forward(odd_lat, src_weight, cfo, part, dpt)
        codes = [coded] + [
            lax.ppermute(coded, "ens", [(e, e ^ k) for e in range(ens)]) for k in range(1, ens)
        ]
        aggt, hidt, slope = call_factors(
            where, latent, core_lat, odd_lat, cf, summed, hidden
        )
        theirs, summed_grad, grad = call_backward(
            where, codes, truth, var_row, area_row, dpt, aggt, hidt, slope
        )
        theirs = lax.ppermute(theirs, "core", swap)
        mine = call_mine(grad, summed_grad, aggt, hidt)
        core_send, odd_send = call_rows(cft, summed_grad, local)
        near_grad = lax.ppermute(odd_send, SPACE, near)
        part = call_merge(mine, theirs, odd_send)
        part, odd_send, core_send = lax.optimization_barrier((part, odd_send, core_send))
        part = part.reshape(16, 2 * per, part.shape[1])
        got = lax.all_to_all(part, ("x", "y"), 0, 0, tiled=True)
        far_grad = lax.ppermute(odd_send, SPACE, far)
        core_grad = lax.ppermute(core_send, "core", swap)
        plane = call_plane(got, ens).reshape(2 * ens, per, got.shape[2])
        got = lax.all_to_all(plane, ("zhi", "ens"), 0, 0, tiled=True)
        score = call_score(where, codes, truth)
        grad_latent = call_latent(cft, summed_grad, src_weight, core_grad, far_grad, near_grad)
        scaling = 1.0 / math.sqrt(members * points * count)
        grad_src, grad_out = call_final(got, nvar, scaling)
        return score, grad_latent, grad_src, grad_out

    return body


def solution(mesh):
    fine = jax.sharding.Mesh(
        mesh.devices.reshape(mesh.devices.shape[0], 2, 4, 4, 2), ("ens",) + SPACE
    )
    return jax.shard_map(
        make_body(mesh.devices.shape[1]),
        mesh=fine,
        in_specs=(
            P("ens", SPACE, None), P(), P(), P(None, SPACE), P(SPACE), P(),
            P(SPACE, None), P(SPACE, None), P(SPACE, None), P(SPACE),
        ),
        out_specs=(P(None, SPACE), P("ens", SPACE, None), P(SPACE, None), P(SPACE, None)),
        check_vma=False,
    )
```

```python
import functools
import math

import jax
import jax.numpy as jnp
from jax import lax
from jax.experimental import pallas as pl
from jax.experimental.pallas import tpu as pltpu
from jax.sharding import PartitionSpec as P

HALO = 128
BLK = 128
ALPHA = 0.95
DELTA = 0.05
SPACE = ("zhi", "x", "y", "core")
QMAX = 32000.0
VPAD = 128
VROWS = 112
VUSE = 104
TILE = 256
GELU_C = math.sqrt(2.0 / math.pi)
MIB = 1 << 20
LIMIT = 24
PREP = 50
LARGE = 56
F32 = jnp.float32
BF16 = jnp.bfloat16


def dot(a, b):
    return jnp.dot(a, b, preferred_element_type=F32)


def dot_nt(a, b):
    return lax.dot_general(a, b, (((1,), (1,)), ((), ())), preferred_element_type=F32)


def smem(count):
    return [pl.BlockSpec(memory_space=pltpu.SMEM)] * count


def cost(flops, nbytes):
    return pl.CostEstimate(flops=flops, bytes_accessed=nbytes, transcendentals=0)


def params(mib):
    return pltpu.CompilerParams(vmem_limit_bytes=mib * MIB)


def hbm(count):
    return [pl.BlockSpec(memory_space=pltpu.HBM)] * count


def vmem(count):
    return [pl.BlockSpec(memory_space=pltpu.VMEM)] * count


def anywhere(count):
    return [pl.BlockSpec(memory_space=pl.ANY)] * count


def start_copy(src, dst, sem):
    copy = pltpu.make_async_copy(src, dst, sem)
    copy.start()
    return copy


def pair_factor(members):
    fair_eps = (1.0 - ALPHA) / members
    return (1.0 - fair_eps) / (2.0 * members * (members - 1))


def smooth_abs(distance):
    square = distance * distance + DELTA * DELTA
    return square * lax.rsqrt(square)


def signum(distance):
    return distance * lax.rsqrt(distance * distance + DELTA * DELTA)


def prepare_kernel(
    where_ref, count_hbm, src_hbm, dst_hbm, wt_hbm, lat_hbm, clat_hbm, w_hbm,
    cf_ref, cft_hbm, cfo_ref, part_ref,
    count_ref, src_ref, dst_ref, wt_ref, x_ref, w_ref, cft_ref, in_sem, out_sem,
):
    edges = [
        start_copy(src, dst, in_sem.at[k])
        for k, (src, dst) in enumerate(
            ((count_hbm, count_ref), (src_hbm, src_ref), (dst_hbm, dst_ref), (wt_hbm, wt_ref))
        )
    ]
    local = lat_hbm.shape[0]
    inputs = []
    for m in range(local):
        for k, ref in enumerate((lat_hbm, clat_hbm)):
            inputs.append(
                start_copy(
                    ref.at[m],
                    x_ref.at[pl.ds((2 * m + k) * HALO, HALO)],
                    in_sem.at[4 + 2 * m + k],
                )
            )
    inputs.append(start_copy(w_hbm, w_ref, in_sem.at[4 + 2 * local]))
    core = where_ref[0]
    slots = src_ref.shape[1]
    window = cf_ref.shape[1] // 2
    points = cf_ref.shape[0]
    for copy in edges:
        copy.wait()
    for b in range(src_ref.shape[0]):
        src = src_ref[b : b + 1, :]
        slot = lax.broadcasted_iota(jnp.int32, (1, slots), 1)
        wt = jnp.where(slot < count_ref[b], wt_ref[b : b + 1, :], 0.0)
        left = 2 * HALO - HALO * core
        right = HALO + HALO * core
        place = jnp.where(
            src < HALO,
            src + left,
            jnp.where(src < 2 * HALO, src - HALO, src - 2 * HALO + right),
        )
        rows = lax.broadcasted_iota(jnp.int32, (window, slots), 0)
        hot = jnp.where(rows == place, 1.0, 0.0).astype(BF16)
        pts = lax.broadcasted_iota(jnp.int32, (BLK, slots), 0)
        mat = jnp.where(pts == dst_ref[b : b + 1, :], wt, 0.0).astype(BF16)
        coef = dot_nt(mat, hot)
        high = coef.astype(BF16)
        low = (coef - high.astype(F32)).astype(BF16)
        at = slice(b * BLK, (b + 1) * BLK)
        cf_ref[at, :window] = high
        cf_ref[at, window:] = low
        cfo_ref[at, :HALO] = high[:, 2 * HALO :]
        cfo_ref[at, HALO:] = low[:, 2 * HALO :]
        coef_t = dot_nt(hot, mat)
        high_t = coef_t.astype(BF16)
        cft_ref[:, b * BLK : (b + 1) * BLK] = high_t
        cft_ref[:, points + b * BLK : points + (b + 1) * BLK] = (
            coef_t - high_t.astype(F32)
        ).astype(BF16)
    out = start_copy(cft_ref, cft_hbm, out_sem)
    for copy in inputs:
        copy.wait()
    x = x_ref[...]
    high = cf_ref[:, : 2 * HALO]
    low = cf_ref[:, window : window + 2 * HALO]
    for j in range(w_ref.shape[1] // TILE):
        at = slice(j * TILE, (j + 1) * TILE)
        p = dot(x, w_ref[:, at]).astype(BF16)
        for m in range(local):
            pm = p[2 * m * HALO : (2 * m + 2) * HALO]
            part_ref[m, :, at] = dot(high, pm) + dot(low, pm)
    out.wait()


def forward_kernel(
    odd_ref, w_ref, cfo_ref, part_ref, dpt_ref, summed_ref, hidden_ref, code_ref
):
    local, points, depth = part_ref.shape
    forecast = [jnp.zeros((VPAD, points), F32) for _ in range(local)]
    for j in range(depth // TILE):
        at = slice(j * TILE, (j + 1) * TILE)
        p = dot(odd_ref[...], w_ref[:, at]).astype(BF16)
        for m in range(local):
            pm = p[m * HALO : (m + 1) * HALO]
            s = part_ref[m, :, at] + dot(cfo_ref[...], jnp.concatenate([pm, pm], axis=0))
            summed_ref[m, :, at] = s
            t = jnp.tanh(s * (GELU_C + (GELU_C * 0.044715) * (s * s)))
            h = (0.5 * s * (1.0 + t)).astype(BF16)
            hidden_ref[m, :, at] = h
            forecast[m] = forecast[m] + dot_nt(dpt_ref[:, at], h)
    for m in range(local):
        f = forecast[m]
        largest = jnp.maximum(jnp.max(jnp.abs(f), axis=1, keepdims=True), 1e-30)
        power = jnp.ceil(jnp.log(largest) * (1.0 / math.log(2.0)) + 1e-3)
        power = jnp.broadcast_to(power, (VPAD, VPAD))
        q = f * (jnp.exp2(-power[:, :1]) * QMAX)
        q = jnp.where(q >= 0.0, q + 0.5, q - 0.5)
        row = jnp.concatenate([power.T[:8], jnp.zeros((8, points - VPAD), F32)], axis=1)
        row = jnp.where(row >= 0.0, row + 0.5, row - 0.5)
        code = jnp.concatenate([q[:VUSE], row], axis=0)
        code_ref[m] = code.astype(jnp.int32).astype(jnp.int16)


def factors_kernel(
    where_ref, lat_ref, clat_ref, olat_ref, cf_ref, summed_ref, hidden_ref,
    aggt_ref, hidt_ref, slope_ref, x_ref,
):
    core = where_ref[0]
    window = cf_ref.shape[1] // 2
    local, points, depth = summed_ref.shape
    high = cf_ref[:, :window]
    low = cf_ref[:, window:]
    for m in range(local):
        x_ref[:HALO] = lat_ref[m]
        x_ref[HALO : 2 * HALO] = clat_ref[m]
        x_ref[2 * HALO :] = olat_ref[m * HALO : (m + 1) * HALO]
        cols = slice(m * points, (m + 1) * points)
        for j in range(depth // TILE):
            at = slice(j * TILE, (j + 1) * TILE)
            x = x_ref[:, at]
            agg = (dot(high, x) + dot(low, x)).T.astype(BF16)
            hid = hidden_ref[m, :, at].astype(F32).T.astype(BF16)
            for k in range(TILE // 16):
                block = j * (TILE // 16) + k
                zhi, rest = divmod(block, 32)
                xy, c = divmod(rest, 2)
                to = lax.bitwise_xor(core, c) * (depth // 2) + (xy * 32 + zhi * 16)
                to = pl.ds(pl.multiple_of(to, 16), 16)
                aggt_ref[to, cols] = agg[k * 16 : (k + 1) * 16]
                hidt_ref[to, cols] = hid[k * 16 : (k + 1) * 16]
            s = summed_ref[m, :, at]
            t = jnp.tanh(s * (GELU_C + (GELU_C * 0.044715) * (s * s)))
            slope_ref[m, :, at] = 0.5 * (1.0 + t) + (0.5 * GELU_C) * s * (1.0 - t * t) * (
                1.0 + 3.0 * 0.044715 * (s * s)
            )


def decode(where_ref, code_refs, f_ref):
    local = code_refs[0].shape[0]
    rows = [
        ref[m, VROWS - 8 :, :].astype(jnp.int32).astype(F32)[:1, :VPAD]
        for ref in code_refs
        for m in range(local)
    ]
    rows.append(jnp.zeros((VPAD - len(rows), VPAD), F32))
    power = (jnp.exp2(jnp.concatenate(rows, axis=0)) * (1.0 / QMAX)).T
    for k, ref in enumerate(code_refs):
        first = lax.bitwise_xor(where_ref[1], k) * local
        for m in range(local):
            code = ref[m].astype(jnp.int32).astype(F32)[:VUSE]
            at = k * local + m
            f_ref[first + m] = code * power[:VUSE, at : at + 1]


def score_kernel(
    where_ref, c0_any, c1_any, c2_any, c3_any, truth_hbm, score_ref,
    c_ref, truth_ref, f_ref, in_sem,
):
    members = f_ref.shape[0]
    nvar = truth_ref.shape[0]
    codes = [c_ref.at[k] for k in range(4)]
    pairs = list(zip((c0_any, c1_any, c2_any, c3_any), codes)) + [(truth_hbm, truth_ref)]
    copies = [start_copy(src, dst, in_sem.at[k]) for k, (src, dst) in enumerate(pairs)]
    for copy in copies:
        copy.wait()
    decode(where_ref, codes, f_ref)
    collected = [f_ref[m][:nvar] for m in range(members)]
    truth = truth_ref[...]
    skill = sum(smooth_abs(f - truth) for f in collected)
    spread = jnp.zeros_like(skill)
    for m in range(members):
        for o in range(m + 1, members):
            spread = spread + smooth_abs(collected[m] - collected[o])
    score_ref[...] = skill * (1.0 / members) - (pair_factor(members) * 2.0) * spread


def backward_kernel(
    where_ref, c0_ref, c1_ref, c2_ref, c3_ref, truth_ref, var_ref, area_ref, dpt_ref,
    aggt_ref, hidt_ref, slope_ref, theirs_ref, sg_ref, grad_ref, f_ref, g_ref,
):
    members = f_ref.shape[0]
    nvar = truth_ref.shape[0]
    local, points, depth = slope_ref.shape
    half = depth // 2
    decode(where_ref, (c0_ref, c1_ref, c2_ref, c3_ref), f_ref)
    first = where_ref[1] * local
    truth = truth_ref[...]
    g_ref[96:] = jnp.zeros((VPAD - 96, points), F32)
    grads = []
    for m in range(local):
        own = f_ref[first + m][:nvar]
        mutual = sum(signum(own - f_ref[o][:nvar]) for o in range(members))
        g_ref[:nvar] = area_ref[...] * (
            signum(own - truth) * (1.0 / members) - (2.0 * pair_factor(members)) * mutual
        )
        grads.append((g_ref[...].T * var_ref[...]).astype(BF16))
    grad = jnp.concatenate(grads, axis=0)
    grad_ref[...] = grad
    theirs_ref[:, depth:] = dot(hidt_ref[half:], grad).astype(BF16)
    for j in range(depth // TILE):
        at = slice(j * TILE, (j + 1) * TILE)
        hg = dot(grad, dpt_ref[:, at])
        for m in range(local):
            rows = slice(m * points, (m + 1) * points)
            sg_ref[rows, at] = (hg[rows] * slope_ref[m, :, at]).astype(BF16)
        theirs_ref[:, at] = dot(aggt_ref[half:], sg_ref[:, at]).astype(BF16)


def mine_kernel(grad_ref, sg_ref, aggt_ref, hidt_ref, mine_ref):
    half, cols = mine_ref.shape
    depth = sg_ref.shape[1]
    mine_ref[:, depth:] = dot(hidt_ref[:half], grad_ref[...]).astype(BF16)
    for j in range(depth // TILE):
        at = slice(j * TILE, (j + 1) * TILE)
        mine_ref[:, at] = dot(aggt_ref[:half], sg_ref[:, at]).astype(BF16)


def merge_kernel(mine_ref, theirs_ref, after_any, out_hbm, out_ref, out_sem):
    rows = mine_ref.shape[0] // 4
    outs = []
    for k in range(4):
        at = slice(k * rows, (k + 1) * rows)
        out_ref[at] = (mine_ref[at].astype(F32) + theirs_ref[at].astype(F32)).astype(BF16)
        cut = pl.ds(k * rows, rows)
        outs.append(start_copy(out_ref.at[cut], out_hbm.at[cut], out_sem.at[k]))
    for copy in outs:
        copy.wait()


def rows_kernel(cft_ref, sg_ref, core_hbm, odd_hbm, core_ref, odd_ref, out_sem):
    local, _, depth = core_ref.shape
    points = cft_ref.shape[1] // 2
    high = cft_ref[HALO:, :points]
    low = cft_ref[HALO:, points:]
    outs = []
    for m in range(local):
        for j in range(depth // TILE):
            at = slice(j * TILE, (j + 1) * TILE)
            s = sg_ref[m * points : (m + 1) * points, at]
            g = (dot(high, s) + dot(low, s)).astype(BF16)
            core_ref[m, :, at] = g[:HALO]
            odd_ref[m, :, at] = g[HALO:]
        outs.append(start_copy(odd_ref.at[m], odd_hbm.at[m], out_sem.at[0, m]))
        outs.append(start_copy(core_ref.at[m], core_hbm.at[m], out_sem.at[1, m]))
    for copy in outs:
        copy.wait()


def plane_kernel(got_ref, out_hbm, out_ref, out_sem):
    per = out_hbm.shape[2]
    outs = []
    for z in range(out_hbm.shape[1]):
        at = slice(z * per, (z + 1) * per)
        total = got_ref[0, at].astype(F32)
        for k in range(1, got_ref.shape[0]):
            total = total + got_ref[k, at].astype(F32)
        out_ref[z] = total.astype(BF16)
        for e in range(out_hbm.shape[0]):
            outs.append(start_copy(out_ref.at[z], out_hbm.at[e, z], out_sem.at[z, e]))
    for copy in outs:
        copy.wait()


def final_kernel(got_ref, src_ref, out_ref, *, scaling):
    total = got_ref[0].astype(F32)
    for k in range(1, got_ref.shape[0]):
        total = total + got_ref[k].astype(F32)
    total = total * scaling
    depth = src_ref.shape[1]
    src_ref[...] = total[:, :depth]
    out_ref[...] = total[:, depth : depth + out_ref.shape[1]]


def latent_kernel(
    cft_hbm, sg_hbm, w_hbm, core_any, far_any, near_any, out_hbm,
    cft_ref, sg_ref, w_ref, core_ref, far_ref, near_ref, g_ref, out_ref, in_sem, out_sem,
):
    local, rows, depth = core_ref.shape
    points = cft_ref.shape[1] // 2
    steps = depth // TILE
    pairs = (
        (cft_hbm.at[pl.ds(0, HALO)], cft_ref), (sg_hbm, sg_ref), (core_any, core_ref),
        (far_any, far_ref), (near_any, near_ref), (w_hbm, w_ref),
    )
    copies = [start_copy(src, dst, in_sem.at[k]) for k, (src, dst) in enumerate(pairs)]
    for copy in copies[:5]:
        copy.wait()
    high = cft_ref[:, :points]
    low = cft_ref[:, points:]
    for m in range(local):
        for j in range(steps):
            at = slice(j * TILE, (j + 1) * TILE)
            s = sg_ref[m * points : (m + 1) * points, at]
            g = dot(high, s) + dot(low, s)
            for ref in (core_ref, far_ref, near_ref):
                g = g + ref[m, :, at].astype(F32)
            g_ref[m * HALO : (m + 1) * HALO, at] = g.astype(BF16)
    copies[5].wait()
    outs = []
    for j in range(steps):
        at = slice(j * TILE, (j + 1) * TILE)
        r = dot_nt(g_ref[...], w_ref[at, :]).astype(BF16)
        for m in range(local):
            out_ref[m, :, at] = r[m * HALO : (m + 1) * HALO]
        cols = pl.ds(j * TILE, TILE)
        outs.append(start_copy(out_ref.at[:, :, cols], out_hbm.at[:, :, cols], out_sem.at[j]))
    for copy in outs:
        copy.wait()


def shape(dims, dtype):
    return jax.ShapeDtypeStruct(dims, dtype)


def scratch(*arrays):
    return [pltpu.VMEM(a.shape, a.dtype) for a in arrays]


def sems(*dims):
    return pltpu.SemaphoreType.DMA(dims)


def call(
    kernel, name, out_shape, in_specs, out_specs, scratch_shapes, work, operands, limit=LIMIT
):
    return pl.pallas_call(
        kernel,
        out_shape=out_shape,
        in_specs=in_specs,
        out_specs=out_specs,
        scratch_shapes=scratch_shapes,
        compiler_params=params(limit),
        cost_estimate=cost(*work),
        name=name,
    )(*operands)


def call_prepare(where, edge_count, edge_src, edge_dst, edge_weight, latent, core_lat, weight):
    local, rows, depth = latent.shape
    window = rows + 2 * HALO
    points = edge_src.shape[0] * BLK
    cf = shape((points, 2 * window), BF16)
    cft = shape((window, 2 * points), BF16)
    return call(
        prepare_kernel,
        "prepare",
        (cf, cft, shape((points, 2 * HALO), BF16), shape((local, points, depth), F32)),
        smem(1) + hbm(5) + anywhere(1) + hbm(1),
        tuple(vmem(1) + hbm(1) + vmem(2)),
        [pltpu.SMEM(edge_count.shape, jnp.int32)]
        + scratch(edge_src, edge_dst, edge_weight)
        + [pltpu.VMEM((local * 2 * HALO, depth), BF16)]
        + scratch(weight, cft)
        + [sems(5 + 2 * local), pltpu.SemaphoreType.DMA],
        (3 * 10**9, 6 * 10**6),
        (where, edge_count, edge_src, edge_dst, edge_weight, latent, core_lat, weight),
        PREP,
    )


def call_forward(odd_lat, weight, cfo, part, dpt):
    local, points, depth = part.shape
    return call(
        forward_kernel,
        "forward",
        (
            shape(part.shape, F32),
            shape(part.shape, BF16),
            shape((local, VROWS, points), jnp.int16),
        ),
        vmem(5),
        tuple(vmem(3)),
        [],
        (2 * 10**9, 8 * 10**6),
        (odd_lat, weight, cfo, part, dpt),
    )


def call_factors(where, latent, core_lat, odd_lat, cf, summed, hidden):
    local, points, depth = summed.shape
    left = shape((depth, local * points), BF16)
    return call(
        factors_kernel,
        "factors",
        (left, left, shape(summed.shape, F32)),
        smem(1) + vmem(6),
        tuple(vmem(3)),
        [pltpu.VMEM((cf.shape[1] // 2, depth), BF16)],
        (3 * 10**9, 10 * 10**6),
        (where, latent, core_lat, odd_lat, cf, summed, hidden),
    )


def call_backward(where, codes, truth, var_row, area_row, dpt, aggt, hidt, slope):
    local, points, depth = slope.shape
    part = shape((depth // 2, depth + VPAD), BF16)
    return call(
        backward_kernel,
        "backward",
        (part, shape((local * points, depth), BF16), shape((local * points, VPAD), BF16)),
        smem(1) + vmem(len(codes) + 7),
        tuple(vmem(3)),
        [
            pltpu.VMEM((local * len(codes), VUSE, points), F32),
            pltpu.VMEM((VPAD, points), F32),
        ],
        (2 * 10**9, 5 * 10**6),
        (where, *codes, truth, var_row, area_row, dpt, aggt, hidt, slope),
    )


def call_mine(grad, summed_grad, aggt, hidt):
    return call(
        mine_kernel,
        "mine",
        shape((aggt.shape[0] // 2, summed_grad.shape[1] + VPAD), BF16),
        vmem(4),
        vmem(1)[0],
        [],
        (10**9, 4 * 10**6),
        (grad, summed_grad, aggt, hidt),
    )


def call_merge(mine, theirs, after):
    return call(
        merge_kernel,
        "merge",
        shape(mine.shape, BF16),
        vmem(2) + anywhere(1),
        hbm(1)[0],
        scratch(mine) + [sems(4)],
        (10**6, 4 * 10**6),
        (mine, theirs, after),
    )


def call_rows(cft, summed_grad, local):
    send = shape((local, HALO, summed_grad.shape[1]), BF16)
    return call(
        rows_kernel,
        "rows",
        (send, send),
        vmem(2),
        tuple(hbm(2)),
        scratch(send, send) + [sems(2, local)],
        (10**9, 3 * 10**6),
        (cft, summed_grad),
    )


def call_plane(got, ens):
    out_shape = shape((ens, 2, got.shape[1] // 2, got.shape[2]), BF16)
    return call(
        plane_kernel,
        "plane",
        out_shape,
        vmem(1),
        hbm(1)[0],
        [pltpu.VMEM((2,) + out_shape.shape[2:], BF16), sems(2, ens)],
        (10**6, 10**6),
        (got,),
    )


def call_score(where, codes, truth):
    local, _, points = codes[0].shape
    return call(
        score_kernel,
        "score",
        shape(truth.shape, F32),
        smem(1) + anywhere(len(codes)) + hbm(1),
        vmem(1)[0],
        [pltpu.VMEM((len(codes),) + codes[0].shape, jnp.int16)]
        + scratch(truth)
        + [pltpu.VMEM((local * len(codes), VUSE, points), F32), sems(len(codes) + 1)],
        (10**7, 10**6),
        (where, *codes, truth),
        LARGE,
    )


def call_latent(cft, summed_grad, weight, core_grad, far_grad, near_grad):
    local, rows, depth = core_grad.shape
    return call(
        latent_kernel,
        "latent",
        shape(core_grad.shape, BF16),
        hbm(3) + anywhere(3),
        hbm(1)[0],
        [pltpu.VMEM((HALO, cft.shape[1]), BF16)]
        + scratch(summed_grad, weight, core_grad, far_grad, near_grad)
        + [pltpu.VMEM((local * rows, depth), BF16)]
        + scratch(core_grad)
        + [sems(6), sems(depth // TILE)],
        (10**9, 5 * 10**6),
        (cft, summed_grad, weight, core_grad, far_grad, near_grad),
        LARGE,
    )


def call_final(got, nvar, scaling):
    per = got.shape[1]
    return call(
        functools.partial(final_kernel, scaling=scaling),
        "final",
        (shape((per, got.shape[2] - VPAD), F32), shape((per, nvar), F32)),
        vmem(1),
        tuple(vmem(2)),
        [],
        (10**5, 4 * 10**5),
        (got,),
    )


def make_body(count):
    odd_pairs = [(i, (i + 1) % count if i % 2 else (i - 1) % count) for i in range(count)]
    far = [p for p in odd_pairs if abs(p[0] - p[1]) > 1 or p[0] // 32 != p[1] // 32]
    near = [p for p in odd_pairs if p not in far]
    swap = [(0, 1), (1, 0)]

    def body(
        latent, src_weight, decoder_projection, truth, area_weight, var_weight,
        edge_src, edge_dst, edge_weight, edge_count,
    ):
        local, rows, depth = latent.shape
        ens = lax.axis_size("ens")
        members = local * ens
        nvar = decoder_projection.shape[1]
        points = truth.shape[1]
        per = depth // count
        where = jnp.stack([lax.axis_index("core"), lax.axis_index("ens")]).astype(jnp.int32)

        odd_lat = lax.ppermute(latent, SPACE, odd_pairs).reshape(local * rows, depth)
        core_lat = lax.ppermute(latent, "core", swap)
        dpt = jnp.pad(decoder_projection.T, ((0, VPAD - nvar), (0, 0)))
        cf, cft, cfo, part = call_prepare(
            where, edge_count, edge_src, edge_dst, edge_weight, latent, core_lat, src_weight
        )
        var_row = jnp.pad(var_weight, (0, VPAD - nvar)).reshape(1, VPAD)
        area_row = area_weight.reshape(1, points)
        summed, hidden, coded = call_forward(odd_lat, src_weight, cfo, part, dpt)
        codes = [coded] + [
            lax.ppermute(coded, "ens", [(e, e ^ k) for e in range(ens)]) for k in range(1, ens)
        ]
        aggt, hidt, slope = call_factors(
            where, latent, core_lat, odd_lat, cf, summed, hidden
        )
        theirs, summed_grad, grad = call_backward(
            where, codes, truth, var_row, area_row, dpt, aggt, hidt, slope
        )
        theirs = lax.ppermute(theirs, "core", swap)
        mine = call_mine(grad, summed_grad, aggt, hidt)
        core_send, odd_send = call_rows(cft, summed_grad, local)
        near_grad = lax.ppermute(odd_send, SPACE, near)
        part = call_merge(mine, theirs, odd_send)
        part, odd_send, core_send = lax.optimization_barrier((part, odd_send, core_send))
        part = part.reshape(16, 2 * per, part.shape[1])
        got = lax.all_to_all(part, ("x", "y"), 0, 0, tiled=True)
        far_grad = lax.ppermute(odd_send, SPACE, far)
        core_grad = lax.ppermute(core_send, "core", swap)
        plane = call_plane(got, ens).reshape(2 * ens, per, got.shape[2])
        got = lax.all_to_all(plane, ("ens", "zhi"), 0, 0, tiled=True)
        score = call_score(where, codes, truth)
        grad_latent = call_latent(cft, summed_grad, src_weight, core_grad, far_grad, near_grad)
        scaling = 1.0 / math.sqrt(members * points * count)
        grad_src, grad_out = call_final(got, nvar, scaling)
        return score, grad_latent, grad_src, grad_out

    return body


def solution(mesh):
    fine = jax.sharding.Mesh(
        mesh.devices.reshape(mesh.devices.shape[0], 2, 4, 4, 2), ("ens",) + SPACE
    )
    return jax.shard_map(
        make_body(mesh.devices.shape[1]),
        mesh=fine,
        in_specs=(
            P("ens", SPACE, None), P(), P(), P(None, SPACE), P(SPACE), P(),
            P(SPACE, None), P(SPACE, None), P(SPACE, None), P(SPACE),
        ),
        out_specs=(P(None, SPACE), P("ens", SPACE, None), P(SPACE, None), P(SPACE, None)),
        check_vma=False,
    )
```

```python
import functools
import math

import jax
import jax.numpy as jnp
from jax import lax
from jax.experimental import pallas as pl
from jax.experimental.pallas import tpu as pltpu
from jax.sharding import PartitionSpec as P

HALO = 128
BLK = 128
ALPHA = 0.95
DELTA = 0.05
SPACE = ("zhi", "x", "y", "core")
QMAX = 32000.0
VPAD = 128
VROWS = 112
VUSE = 104
TILE = 256
GELU_C = math.sqrt(2.0 / math.pi)
MIB = 1 << 20
LIMIT = 24
PREP = 50
LARGE = 56
F32 = jnp.float32
BF16 = jnp.bfloat16


def dot(a, b):
    return jnp.dot(a, b, preferred_element_type=F32)


def dot_nt(a, b):
    return lax.dot_general(a, b, (((1,), (1,)), ((), ())), preferred_element_type=F32)


def smem(count):
    return [pl.BlockSpec(memory_space=pltpu.SMEM)] * count


def cost(flops, nbytes):
    return pl.CostEstimate(flops=flops, bytes_accessed=nbytes, transcendentals=0)


def params(mib):
    return pltpu.CompilerParams(vmem_limit_bytes=mib * MIB)


def hbm(count):
    return [pl.BlockSpec(memory_space=pltpu.HBM)] * count


def vmem(count):
    return [pl.BlockSpec(memory_space=pltpu.VMEM)] * count


def anywhere(count):
    return [pl.BlockSpec(memory_space=pl.ANY)] * count


def start_copy(src, dst, sem):
    copy = pltpu.make_async_copy(src, dst, sem)
    copy.start()
    return copy


def pair_factor(members):
    fair_eps = (1.0 - ALPHA) / members
    return (1.0 - fair_eps) / (2.0 * members * (members - 1))


def smooth_abs(distance):
    square = distance * distance + DELTA * DELTA
    return square * lax.rsqrt(square)


def signum(distance):
    return distance * lax.rsqrt(distance * distance + DELTA * DELTA)


def prepare_kernel(
    where_ref, count_hbm, src_hbm, dst_hbm, wt_hbm, lat_hbm, clat_hbm, w_hbm,
    cf_ref, cft_hbm, cfo_ref, part_ref,
    count_ref, src_ref, dst_ref, wt_ref, x_ref, w_ref, cft_ref, in_sem, out_sem,
):
    edges = [
        start_copy(src, dst, in_sem.at[k])
        for k, (src, dst) in enumerate(
            ((count_hbm, count_ref), (src_hbm, src_ref), (dst_hbm, dst_ref), (wt_hbm, wt_ref))
        )
    ]
    local = lat_hbm.shape[0]
    inputs = []
    for m in range(local):
        for k, ref in enumerate((lat_hbm, clat_hbm)):
            inputs.append(
                start_copy(
                    ref.at[m],
                    x_ref.at[pl.ds((2 * m + k) * HALO, HALO)],
                    in_sem.at[4 + 2 * m + k],
                )
            )
    inputs.append(start_copy(w_hbm, w_ref, in_sem.at[4 + 2 * local]))
    core = where_ref[0]
    slots = src_ref.shape[1]
    window = cf_ref.shape[1] // 2
    points = cf_ref.shape[0]
    for copy in edges:
        copy.wait()
    for b in range(src_ref.shape[0]):
        src = src_ref[b : b + 1, :]
        slot = lax.broadcasted_iota(jnp.int32, (1, slots), 1)
        wt = jnp.where(slot < count_ref[b], wt_ref[b : b + 1, :], 0.0)
        left = 2 * HALO - HALO * core
        right = HALO + HALO * core
        place = jnp.where(
            src < HALO,
            src + left,
            jnp.where(src < 2 * HALO, src - HALO, src - 2 * HALO + right),
        )
        rows = lax.broadcasted_iota(jnp.int32, (window, slots), 0)
        hot = jnp.where(rows == place, 1.0, 0.0).astype(BF16)
        pts = lax.broadcasted_iota(jnp.int32, (BLK, slots), 0)
        mat = jnp.where(pts == dst_ref[b : b + 1, :], wt, 0.0).astype(BF16)
        coef = dot_nt(mat, hot)
        high = coef.astype(BF16)
        low = (coef - high.astype(F32)).astype(BF16)
        at = slice(b * BLK, (b + 1) * BLK)
        cf_ref[at, :window] = high
        cf_ref[at, window:] = low
        cfo_ref[at, :HALO] = high[:, 2 * HALO :]
        cfo_ref[at, HALO:] = low[:, 2 * HALO :]
        coef_t = dot_nt(hot, mat)
        high_t = coef_t.astype(BF16)
        cft_ref[:, b * BLK : (b + 1) * BLK] = high_t
        cft_ref[:, points + b * BLK : points + (b + 1) * BLK] = (
            coef_t - high_t.astype(F32)
        ).astype(BF16)
    out = start_copy(cft_ref, cft_hbm, out_sem)
    for copy in inputs:
        copy.wait()
    x = x_ref[...]
    high = cf_ref[:, : 2 * HALO]
    low = cf_ref[:, window : window + 2 * HALO]
    for j in range(w_ref.shape[1] // TILE):
        at = slice(j * TILE, (j + 1) * TILE)
        p = dot(x, w_ref[:, at]).astype(BF16)
        for m in range(local):
            pm = p[2 * m * HALO : (2 * m + 2) * HALO]
            part_ref[m, :, at] = dot(high, pm) + dot(low, pm)
    out.wait()


def forward_kernel(
    odd_ref, w_ref, cfo_ref, part_ref, dpt_ref, summed_ref, hidden_ref, code_ref
):
    local, points, depth = part_ref.shape
    forecast = [jnp.zeros((VPAD, points), F32) for _ in range(local)]
    for j in range(depth // TILE):
        at = slice(j * TILE, (j + 1) * TILE)
        p = dot(odd_ref[...], w_ref[:, at]).astype(BF16)
        for m in range(local):
            pm = p[m * HALO : (m + 1) * HALO]
            s = part_ref[m, :, at] + dot(cfo_ref[...], jnp.concatenate([pm, pm], axis=0))
            summed_ref[m, :, at] = s
            t = jnp.tanh(s * (GELU_C + (GELU_C * 0.044715) * (s * s)))
            h = (0.5 * s * (1.0 + t)).astype(BF16)
            hidden_ref[m, :, at] = h
            forecast[m] = forecast[m] + dot_nt(dpt_ref[:, at], h)
    for m in range(local):
        f = forecast[m]
        largest = jnp.maximum(jnp.max(jnp.abs(f), axis=1, keepdims=True), 1e-30)
        power = jnp.ceil(jnp.log(largest) * (1.0 / math.log(2.0)) + 1e-3)
        power = jnp.broadcast_to(power, (VPAD, VPAD))
        q = f * (jnp.exp2(-power[:, :1]) * QMAX)
        q = jnp.where(q >= 0.0, q + 0.5, q - 0.5)
        row = jnp.concatenate([power.T[:8], jnp.zeros((8, points - VPAD), F32)], axis=1)
        row = jnp.where(row >= 0.0, row + 0.5, row - 0.5)
        code = jnp.concatenate([q[:VUSE], row], axis=0)
        code_ref[m] = code.astype(jnp.int32).astype(jnp.int16)


def factors_kernel(
    where_ref, lat_ref, clat_ref, olat_ref, cf_ref, summed_ref, hidden_ref,
    aggt_ref, hidt_ref, slope_ref, x_ref,
):
    core = where_ref[0]
    window = cf_ref.shape[1] // 2
    local, points, depth = summed_ref.shape
    high = cf_ref[:, :window]
    low = cf_ref[:, window:]
    for m in range(local):
        x_ref[:HALO] = lat_ref[m]
        x_ref[HALO : 2 * HALO] = clat_ref[m]
        x_ref[2 * HALO :] = olat_ref[m * HALO : (m + 1) * HALO]
        cols = slice(m * points, (m + 1) * points)
        for j in range(depth // TILE):
            at = slice(j * TILE, (j + 1) * TILE)
            x = x_ref[:, at]
            agg = (dot(high, x) + dot(low, x)).T.astype(BF16)
            hid = hidden_ref[m, :, at].astype(F32).T.astype(BF16)
            for k in range(TILE // 16):
                block = j * (TILE // 16) + k
                zhi, rest = divmod(block, 32)
                xy, c = divmod(rest, 2)
                to = lax.bitwise_xor(core, c) * (depth // 2) + (xy * 32 + zhi * 16)
                to = pl.ds(pl.multiple_of(to, 16), 16)
                aggt_ref[to, cols] = agg[k * 16 : (k + 1) * 16]
                hidt_ref[to, cols] = hid[k * 16 : (k + 1) * 16]
            s = summed_ref[m, :, at]
            t = jnp.tanh(s * (GELU_C + (GELU_C * 0.044715) * (s * s)))
            slope_ref[m, :, at] = 0.5 * (1.0 + t) + (0.5 * GELU_C) * s * (1.0 - t * t) * (
                1.0 + 3.0 * 0.044715 * (s * s)
            )


def decode(where_ref, code_refs, f_ref):
    local = code_refs[0].shape[0]
    rows = [
        ref[m, VROWS - 16 :, :].astype(jnp.int32).astype(F32)[8:9, :VPAD]
        for ref in code_refs
        for m in range(local)
    ]
    rows.append(jnp.zeros((VPAD - len(rows), VPAD), F32))
    power = (jnp.exp2(jnp.concatenate(rows, axis=0)) * (1.0 / QMAX)).T
    for k, ref in enumerate(code_refs):
        first = lax.bitwise_xor(where_ref[1], k) * local
        for m in range(local):
            code = ref[m].astype(jnp.int32).astype(F32)[:VUSE]
            at = k * local + m
            f_ref[first + m] = code * power[:VUSE, at : at + 1]


def score_kernel(
    where_ref, c0_any, c1_any, c2_any, c3_any, truth_hbm, score_ref,
    c_ref, truth_ref, f_ref, in_sem,
):
    members = f_ref.shape[0]
    nvar = truth_ref.shape[0]
    codes = [c_ref.at[k] for k in range(4)]
    pairs = list(zip((c0_any, c1_any, c2_any, c3_any), codes)) + [(truth_hbm, truth_ref)]
    copies = [start_copy(src, dst, in_sem.at[k]) for k, (src, dst) in enumerate(pairs)]
    for copy in copies:
        copy.wait()
    decode(where_ref, codes, f_ref)
    collected = [f_ref[m][:nvar] for m in range(members)]
    truth = truth_ref[...]
    skill = sum(smooth_abs(f - truth) for f in collected)
    spread = jnp.zeros_like(skill)
    for m in range(members):
        for o in range(m + 1, members):
            spread = spread + smooth_abs(collected[m] - collected[o])
    score_ref[...] = skill * (1.0 / members) - (pair_factor(members) * 2.0) * spread


def backward_kernel(
    where_ref, c0_ref, c1_ref, c2_ref, c3_ref, truth_ref, var_ref, area_ref, dpt_ref,
    aggt_ref, hidt_ref, slope_ref, theirs_ref, sg_ref, grad_ref, f_ref, g_ref,
):
    members = f_ref.shape[0]
    nvar = truth_ref.shape[0]
    local, points, depth = slope_ref.shape
    half = depth // 2
    decode(where_ref, (c0_ref, c1_ref, c2_ref, c3_ref), f_ref)
    first = where_ref[1] * local
    truth = truth_ref[...]
    g_ref[96:] = jnp.zeros((VPAD - 96, points), F32)
    grads = []
    for m in range(local):
        own = f_ref[first + m][:nvar]
        mutual = sum(signum(own - f_ref[o][:nvar]) for o in range(members))
        g_ref[:nvar] = area_ref[...] * (
            signum(own - truth) * (1.0 / members) - (2.0 * pair_factor(members)) * mutual
        )
        grads.append((g_ref[...].T * var_ref[...]).astype(BF16))
    grad = jnp.concatenate(grads, axis=0)
    grad_ref[...] = grad
    theirs_ref[:, depth:] = dot(hidt_ref[half:], grad).astype(BF16)
    for j in range(depth // TILE):
        at = slice(j * TILE, (j + 1) * TILE)
        hg = dot(grad, dpt_ref[:, at])
        for m in range(local):
            rows = slice(m * points, (m + 1) * points)
            sg_ref[rows, at] = (hg[rows] * slope_ref[m, :, at]).astype(BF16)
        theirs_ref[:, at] = dot(aggt_ref[half:], sg_ref[:, at]).astype(BF16)


def mine_kernel(grad_ref, sg_ref, aggt_ref, hidt_ref, mine_ref):
    half, cols = mine_ref.shape
    depth = sg_ref.shape[1]
    mine_ref[:, depth:] = dot(hidt_ref[:half], grad_ref[...]).astype(BF16)
    for j in range(depth // TILE):
        at = slice(j * TILE, (j + 1) * TILE)
        mine_ref[:, at] = dot(aggt_ref[:half], sg_ref[:, at]).astype(BF16)


def merge_kernel(mine_ref, theirs_ref, after_any, out_hbm, out_ref, out_sem):
    rows = mine_ref.shape[0] // 4
    outs = []
    for k in range(4):
        at = slice(k * rows, (k + 1) * rows)
        out_ref[at] = (mine_ref[at].astype(F32) + theirs_ref[at].astype(F32)).astype(BF16)
        cut = pl.ds(k * rows, rows)
        outs.append(start_copy(out_ref.at[cut], out_hbm.at[cut], out_sem.at[k]))
    for copy in outs:
        copy.wait()


def rows_kernel(cft_ref, sg_ref, core_hbm, odd_hbm, core_ref, odd_ref, out_sem):
    local, _, depth = core_ref.shape
    points = cft_ref.shape[1] // 2
    high = cft_ref[HALO:, :points]
    low = cft_ref[HALO:, points:]
    outs = []
    for m in range(local):
        for j in range(depth // TILE):
            at = slice(j * TILE, (j + 1) * TILE)
            s = sg_ref[m * points : (m + 1) * points, at]
            g = (dot(high, s) + dot(low, s)).astype(BF16)
            core_ref[m, :, at] = g[:HALO]
            odd_ref[m, :, at] = g[HALO:]
        outs.append(start_copy(odd_ref.at[m], odd_hbm.at[m], out_sem.at[0, m]))
        outs.append(start_copy(core_ref.at[m], core_hbm.at[m], out_sem.at[1, m]))
    for copy in outs:
        copy.wait()


def plane_kernel(got_ref, out_hbm, out_ref, out_sem):
    per = out_hbm.shape[2]
    outs = []
    for z in range(out_hbm.shape[1]):
        at = slice(z * per, (z + 1) * per)
        total = got_ref[0, at].astype(F32)
        for k in range(1, got_ref.shape[0]):
            total = total + got_ref[k, at].astype(F32)
        out_ref[z] = total.astype(BF16)
        for e in range(out_hbm.shape[0]):
            outs.append(start_copy(out_ref.at[z], out_hbm.at[e, z], out_sem.at[z, e]))
    for copy in outs:
        copy.wait()


def final_kernel(got_ref, src_ref, out_ref, *, scaling):
    total = got_ref[0].astype(F32)
    for k in range(1, got_ref.shape[0]):
        total = total + got_ref[k].astype(F32)
    total = total * scaling
    depth = src_ref.shape[1]
    src_ref[...] = total[:, :depth]
    out_ref[...] = total[:, depth : depth + out_ref.shape[1]]


def latent_kernel(
    cft_hbm, sg_hbm, w_hbm, core_any, far_any, near_any, out_hbm,
    cft_ref, sg_ref, w_ref, core_ref, far_ref, near_ref, g_ref, out_ref, in_sem, out_sem,
):
    local, rows, depth = core_ref.shape
    points = cft_ref.shape[1] // 2
    steps = depth // TILE
    pairs = (
        (cft_hbm.at[pl.ds(0, HALO)], cft_ref), (sg_hbm, sg_ref), (core_any, core_ref),
        (far_any, far_ref), (near_any, near_ref), (w_hbm, w_ref),
    )
    copies = [start_copy(src, dst, in_sem.at[k]) for k, (src, dst) in enumerate(pairs)]
    for copy in copies[:5]:
        copy.wait()
    high = cft_ref[:, :points]
    low = cft_ref[:, points:]
    for m in range(local):
        for j in range(steps):
            at = slice(j * TILE, (j + 1) * TILE)
            s = sg_ref[m * points : (m + 1) * points, at]
            g = dot(high, s) + dot(low, s)
            for ref in (core_ref, far_ref, near_ref):
                g = g + ref[m, :, at].astype(F32)
            g_ref[m * HALO : (m + 1) * HALO, at] = g.astype(BF16)
    copies[5].wait()
    outs = []
    for j in range(steps):
        at = slice(j * TILE, (j + 1) * TILE)
        r = dot_nt(g_ref[...], w_ref[at, :]).astype(BF16)
        for m in range(local):
            out_ref[m, :, at] = r[m * HALO : (m + 1) * HALO]
        cols = pl.ds(j * TILE, TILE)
        outs.append(start_copy(out_ref.at[:, :, cols], out_hbm.at[:, :, cols], out_sem.at[j]))
    for copy in outs:
        copy.wait()


def shape(dims, dtype):
    return jax.ShapeDtypeStruct(dims, dtype)


def scratch(*arrays):
    return [pltpu.VMEM(a.shape, a.dtype) for a in arrays]


def sems(*dims):
    return pltpu.SemaphoreType.DMA(dims)


def call(
    kernel, name, out_shape, in_specs, out_specs, scratch_shapes, work, operands, limit=LIMIT
):
    return pl.pallas_call(
        kernel,
        out_shape=out_shape,
        in_specs=in_specs,
        out_specs=out_specs,
        scratch_shapes=scratch_shapes,
        compiler_params=params(limit),
        cost_estimate=cost(*work),
        name=name,
    )(*operands)


def call_prepare(where, edge_count, edge_src, edge_dst, edge_weight, latent, core_lat, weight):
    local, rows, depth = latent.shape
    window = rows + 2 * HALO
    points = edge_src.shape[0] * BLK
    cf = shape((points, 2 * window), BF16)
    cft = shape((window, 2 * points), BF16)
    return call(
        prepare_kernel,
        "prepare",
        (cf, cft, shape((points, 2 * HALO), BF16), shape((local, points, depth), F32)),
        smem(1) + hbm(5) + anywhere(1) + hbm(1),
        tuple(vmem(1) + hbm(1) + vmem(2)),
        [pltpu.SMEM(edge_count.shape, jnp.int32)]
        + scratch(edge_src, edge_dst, edge_weight)
        + [pltpu.VMEM((local * 2 * HALO, depth), BF16)]
        + scratch(weight, cft)
        + [sems(5 + 2 * local), pltpu.SemaphoreType.DMA],
        (3 * 10**9, 6 * 10**6),
        (where, edge_count, edge_src, edge_dst, edge_weight, latent, core_lat, weight),
        PREP,
    )


def call_forward(odd_lat, weight, cfo, part, dpt):
    local, points, depth = part.shape
    return call(
        forward_kernel,
        "forward",
        (
            shape(part.shape, F32),
            shape(part.shape, BF16),
            shape((local, VROWS, points), jnp.int16),
        ),
        vmem(5),
        tuple(vmem(3)),
        [],
        (2 * 10**9, 8 * 10**6),
        (odd_lat, weight, cfo, part, dpt),
    )


def call_factors(where, latent, core_lat, odd_lat, cf, summed, hidden):
    local, points, depth = summed.shape
    left = shape((depth, local * points), BF16)
    return call(
        factors_kernel,
        "factors",
        (left, left, shape(summed.shape, F32)),
        smem(1) + vmem(6),
        tuple(vmem(3)),
        [pltpu.VMEM((cf.shape[1] // 2, depth), BF16)],
        (3 * 10**9, 10 * 10**6),
        (where, latent, core_lat, odd_lat, cf, summed, hidden),
    )


def call_backward(where, codes, truth, var_row, area_row, dpt, aggt, hidt, slope):
    local, points, depth = slope.shape
    part = shape((depth // 2, depth + VPAD), BF16)
    return call(
        backward_kernel,
        "backward",
        (part, shape((local * points, depth), BF16), shape((local * points, VPAD), BF16)),
        smem(1) + vmem(len(codes) + 7),
        tuple(vmem(3)),
        [
            pltpu.VMEM((local * len(codes), VUSE, points), F32),
            pltpu.VMEM((VPAD, points), F32),
        ],
        (2 * 10**9, 5 * 10**6),
        (where, *codes, truth, var_row, area_row, dpt, aggt, hidt, slope),
    )


def call_mine(grad, summed_grad, aggt, hidt):
    return call(
        mine_kernel,
        "mine",
        shape((aggt.shape[0] // 2, summed_grad.shape[1] + VPAD), BF16),
        vmem(4),
        vmem(1)[0],
        [],
        (10**9, 4 * 10**6),
        (grad, summed_grad, aggt, hidt),
    )


def call_merge(mine, theirs, after):
    return call(
        merge_kernel,
        "merge",
        shape(mine.shape, BF16),
        vmem(2) + anywhere(1),
        hbm(1)[0],
        scratch(mine) + [sems(4)],
        (10**6, 4 * 10**6),
        (mine, theirs, after),
    )


def call_rows(cft, summed_grad, local):
    send = shape((local, HALO, summed_grad.shape[1]), BF16)
    return call(
        rows_kernel,
        "rows",
        (send, send),
        vmem(2),
        tuple(hbm(2)),
        scratch(send, send) + [sems(2, local)],
        (10**9, 3 * 10**6),
        (cft, summed_grad),
    )


def call_plane(got, ens):
    out_shape = shape((ens, 2, got.shape[1] // 2, got.shape[2]), BF16)
    return call(
        plane_kernel,
        "plane",
        out_shape,
        vmem(1),
        hbm(1)[0],
        [pltpu.VMEM((2,) + out_shape.shape[2:], BF16), sems(2, ens)],
        (10**6, 10**6),
        (got,),
    )


def call_score(where, codes, truth):
    local, _, points = codes[0].shape
    return call(
        score_kernel,
        "score",
        shape(truth.shape, F32),
        smem(1) + anywhere(len(codes)) + hbm(1),
        vmem(1)[0],
        [pltpu.VMEM((len(codes),) + codes[0].shape, jnp.int16)]
        + scratch(truth)
        + [pltpu.VMEM((local * len(codes), VUSE, points), F32), sems(len(codes) + 1)],
        (10**7, 10**6),
        (where, *codes, truth),
        LARGE,
    )


def call_latent(cft, summed_grad, weight, core_grad, far_grad, near_grad):
    local, rows, depth = core_grad.shape
    return call(
        latent_kernel,
        "latent",
        shape(core_grad.shape, BF16),
        hbm(3) + anywhere(3),
        hbm(1)[0],
        [pltpu.VMEM((HALO, cft.shape[1]), BF16)]
        + scratch(summed_grad, weight, core_grad, far_grad, near_grad)
        + [pltpu.VMEM((local * rows, depth), BF16)]
        + scratch(core_grad)
        + [sems(6), sems(depth // TILE)],
        (10**9, 5 * 10**6),
        (cft, summed_grad, weight, core_grad, far_grad, near_grad),
        LARGE,
    )


def call_final(got, nvar, scaling):
    per = got.shape[1]
    return call(
        functools.partial(final_kernel, scaling=scaling),
        "final",
        (shape((per, got.shape[2] - VPAD), F32), shape((per, nvar), F32)),
        vmem(1),
        tuple(vmem(2)),
        [],
        (10**5, 4 * 10**5),
        (got,),
    )


def make_body(count):
    odd_pairs = [(i, (i + 1) % count if i % 2 else (i - 1) % count) for i in range(count)]
    far = [p for p in odd_pairs if abs(p[0] - p[1]) > 1 or p[0] // 32 != p[1] // 32]
    near = [p for p in odd_pairs if p not in far]
    swap = [(0, 1), (1, 0)]

    def body(
        latent, src_weight, decoder_projection, truth, area_weight, var_weight,
        edge_src, edge_dst, edge_weight, edge_count,
    ):
        local, rows, depth = latent.shape
        ens = lax.axis_size("ens")
        members = local * ens
        nvar = decoder_projection.shape[1]
        points = truth.shape[1]
        per = depth // count
        where = jnp.stack([lax.axis_index("core"), lax.axis_index("ens")]).astype(jnp.int32)

        odd_lat = lax.ppermute(latent, SPACE, odd_pairs).reshape(local * rows, depth)
        core_lat = lax.ppermute(latent, "core", swap)
        dpt = jnp.pad(decoder_projection.T, ((0, VPAD - nvar), (0, 0)))
        cf, cft, cfo, part = call_prepare(
            where, edge_count, edge_src, edge_dst, edge_weight, latent, core_lat, src_weight
        )
        var_row = jnp.pad(var_weight, (0, VPAD - nvar)).reshape(1, VPAD)
        area_row = area_weight.reshape(1, points)
        summed, hidden, coded = call_forward(odd_lat, src_weight, cfo, part, dpt)
        codes = [coded] + [
            lax.ppermute(coded, "ens", [(e, e ^ k) for e in range(ens)]) for k in range(1, ens)
        ]
        aggt, hidt, slope = call_factors(
            where, latent, core_lat, odd_lat, cf, summed, hidden
        )
        theirs, summed_grad, grad = call_backward(
            where, codes, truth, var_row, area_row, dpt, aggt, hidt, slope
        )
        theirs = lax.ppermute(theirs, "core", swap)
        mine = call_mine(grad, summed_grad, aggt, hidt)
        core_send, odd_send = call_rows(cft, summed_grad, local)
        near_grad = lax.ppermute(odd_send, SPACE, near)
        part = call_merge(mine, theirs, odd_send)
        part, odd_send, core_send = lax.optimization_barrier((part, odd_send, core_send))
        part = part.reshape(16, 2 * per, part.shape[1])
        got = lax.all_to_all(part, ("x", "y"), 0, 0, tiled=True)
        far_grad = lax.ppermute(odd_send, SPACE, far)
        core_grad = lax.ppermute(core_send, "core", swap)
        plane = call_plane(got, ens).reshape(2 * ens, per, got.shape[2])
        got = lax.all_to_all(plane, ("ens", "zhi"), 0, 0, tiled=True)
        score = call_score(where, codes, truth)
        grad_latent = call_latent(cft, summed_grad, src_weight, core_grad, far_grad, near_grad)
        scaling = 1.0 / math.sqrt(members * points * count)
        grad_src, grad_out = call_final(got, nvar, scaling)
        return score, grad_latent, grad_src, grad_out

    return body


def solution(mesh):
    fine = jax.sharding.Mesh(
        mesh.devices.reshape(mesh.devices.shape[0], 2, 4, 4, 2), ("ens",) + SPACE
    )
    return jax.shard_map(
        make_body(mesh.devices.shape[1]),
        mesh=fine,
        in_specs=(
            P("ens", SPACE, None), P(), P(), P(None, SPACE), P(SPACE), P(),
            P(SPACE, None), P(SPACE, None), P(SPACE, None), P(SPACE),
        ),
        out_specs=(P(None, SPACE), P("ens", SPACE, None), P(SPACE, None), P(SPACE, None)),
        check_vma=False,
    )
```

```python
import functools
import math

import jax
import jax.numpy as jnp
from jax import lax
from jax.experimental import pallas as pl
from jax.experimental.pallas import tpu as pltpu
from jax.sharding import PartitionSpec as P

HALO = 128
BLK = 128
ALPHA = 0.95
DELTA = 0.05
SPACE = ("zhi", "x", "y", "core")
QMAX = 32000.0
VPAD = 128
VROWS = 112
VUSE = 104
TILE = 256
GELU_C = math.sqrt(2.0 / math.pi)
MIB = 1 << 20
LIMIT = 24
PREP = 50
LARGE = 56
F32 = jnp.float32
BF16 = jnp.bfloat16


def dot(a, b):
    return jnp.dot(a, b, preferred_element_type=F32)


def dot_nt(a, b):
    return lax.dot_general(a, b, (((1,), (1,)), ((), ())), preferred_element_type=F32)


def smem(count):
    return [pl.BlockSpec(memory_space=pltpu.SMEM)] * count


def cost(flops, nbytes):
    return pl.CostEstimate(flops=flops, bytes_accessed=nbytes, transcendentals=0)


def params(mib):
    return pltpu.CompilerParams(vmem_limit_bytes=mib * MIB)


def hbm(count):
    return [pl.BlockSpec(memory_space=pltpu.HBM)] * count


def vmem(count):
    return [pl.BlockSpec(memory_space=pltpu.VMEM)] * count


def anywhere(count):
    return [pl.BlockSpec(memory_space=pl.ANY)] * count


def start_copy(src, dst, sem):
    copy = pltpu.make_async_copy(src, dst, sem)
    copy.start()
    return copy


def pair_factor(members):
    fair_eps = (1.0 - ALPHA) / members
    return (1.0 - fair_eps) / (2.0 * members * (members - 1))


def smooth_abs(distance):
    square = distance * distance + DELTA * DELTA
    return square * lax.rsqrt(square)


def signum(distance):
    return distance * lax.rsqrt(distance * distance + DELTA * DELTA)


def prepare_kernel(
    where_ref, count_hbm, src_hbm, dst_hbm, wt_hbm, lat_hbm, clat_hbm, w_hbm,
    cf_ref, cft_hbm, cfo_ref, part_ref,
    count_ref, src_ref, dst_ref, wt_ref, x_ref, w_ref, cft_ref, in_sem, out_sem,
):
    edges = [
        start_copy(src, dst, in_sem.at[k])
        for k, (src, dst) in enumerate(
            ((count_hbm, count_ref), (src_hbm, src_ref), (dst_hbm, dst_ref), (wt_hbm, wt_ref))
        )
    ]
    local = lat_hbm.shape[0]
    inputs = []
    for m in range(local):
        for k, ref in enumerate((lat_hbm, clat_hbm)):
            inputs.append(
                start_copy(
                    ref.at[m],
                    x_ref.at[pl.ds((2 * m + k) * HALO, HALO)],
                    in_sem.at[4 + 2 * m + k],
                )
            )
    inputs.append(start_copy(w_hbm, w_ref, in_sem.at[4 + 2 * local]))
    core = where_ref[0]
    slots = src_ref.shape[1]
    window = cf_ref.shape[1] // 2
    points = cf_ref.shape[0]
    for copy in edges:
        copy.wait()
    for b in range(src_ref.shape[0]):
        src = src_ref[b : b + 1, :]
        slot = lax.broadcasted_iota(jnp.int32, (1, slots), 1)
        wt = jnp.where(slot < count_ref[b], wt_ref[b : b + 1, :], 0.0)
        left = 2 * HALO - HALO * core
        right = HALO + HALO * core
        place = jnp.where(
            src < HALO,
            src + left,
            jnp.where(src < 2 * HALO, src - HALO, src - 2 * HALO + right),
        )
        rows = lax.broadcasted_iota(jnp.int32, (window, slots), 0)
        hot = jnp.where(rows == place, 1.0, 0.0).astype(BF16)
        pts = lax.broadcasted_iota(jnp.int32, (BLK, slots), 0)
        mat = jnp.where(pts == dst_ref[b : b + 1, :], wt, 0.0).astype(BF16)
        coef = dot_nt(mat, hot)
        high = coef.astype(BF16)
        low = (coef - high.astype(F32)).astype(BF16)
        at = slice(b * BLK, (b + 1) * BLK)
        cf_ref[at, :window] = high
        cf_ref[at, window:] = low
        cfo_ref[at, :HALO] = high[:, 2 * HALO :]
        cfo_ref[at, HALO:] = low[:, 2 * HALO :]
        coef_t = dot_nt(hot, mat)
        high_t = coef_t.astype(BF16)
        cft_ref[:, b * BLK : (b + 1) * BLK] = high_t
        cft_ref[:, points + b * BLK : points + (b + 1) * BLK] = (
            coef_t - high_t.astype(F32)
        ).astype(BF16)
    out = start_copy(cft_ref, cft_hbm, out_sem)
    for copy in inputs:
        copy.wait()
    x = x_ref[...]
    high = cf_ref[:, : 2 * HALO]
    low = cf_ref[:, window : window + 2 * HALO]
    for j in range(w_ref.shape[1] // TILE):
        at = slice(j * TILE, (j + 1) * TILE)
        p = dot(x, w_ref[:, at]).astype(BF16)
        for m in range(local):
            pm = p[2 * m * HALO : (2 * m + 2) * HALO]
            part_ref[m, :, at] = dot(high, pm) + dot(low, pm)
    out.wait()


def forward_kernel(
    odd_ref, w_ref, cfo_ref, part_ref, dpt_ref, summed_ref, hidden_ref, code_ref
):
    local, points, depth = part_ref.shape
    forecast = [jnp.zeros((VPAD, points), F32) for _ in range(local)]
    for j in range(depth // TILE):
        at = slice(j * TILE, (j + 1) * TILE)
        p = dot(odd_ref[...], w_ref[:, at]).astype(BF16)
        for m in range(local):
            pm = p[m * HALO : (m + 1) * HALO]
            s = part_ref[m, :, at] + dot(cfo_ref[...], jnp.concatenate([pm, pm], axis=0))
            summed_ref[m, :, at] = s
            t = jnp.tanh(s * (GELU_C + (GELU_C * 0.044715) * (s * s)))
            h = (0.5 * s * (1.0 + t)).astype(BF16)
            hidden_ref[m, :, at] = h
            forecast[m] = forecast[m] + dot_nt(dpt_ref[:, at], h)
    for m in range(local):
        f = forecast[m]
        largest = jnp.maximum(jnp.max(jnp.abs(f), axis=1, keepdims=True), 1e-30)
        power = jnp.ceil(jnp.log(largest) * (1.0 / math.log(2.0)) + 1e-3)
        power = jnp.broadcast_to(power, (VPAD, VPAD))
        q = f * (jnp.exp2(-power[:, :1]) * QMAX)
        q = jnp.where(q >= 0.0, q + 0.5, q - 0.5)
        row = jnp.concatenate([power.T[:8], jnp.zeros((8, points - VPAD), F32)], axis=1)
        row = jnp.where(row >= 0.0, row + 0.5, row - 0.5)
        code = jnp.concatenate([q[:VUSE], row], axis=0)
        code_ref[m] = code.astype(jnp.int32).astype(jnp.int16)


def factors_kernel(
    where_ref, lat_ref, clat_ref, olat_ref, cf_ref, summed_ref, hidden_ref,
    aggt_ref, hidt_ref, slope_ref, x_ref,
):
    core = where_ref[0]
    window = cf_ref.shape[1] // 2
    local, points, depth = summed_ref.shape
    high = cf_ref[:, :window]
    low = cf_ref[:, window:]
    for m in range(local):
        x_ref[:HALO] = lat_ref[m]
        x_ref[HALO : 2 * HALO] = clat_ref[m]
        x_ref[2 * HALO :] = olat_ref[m * HALO : (m + 1) * HALO]
        cols = slice(m * points, (m + 1) * points)
        for j in range(depth // TILE):
            at = slice(j * TILE, (j + 1) * TILE)
            x = x_ref[:, at]
            agg = (dot(high, x) + dot(low, x)).T.astype(BF16)
            hid = hidden_ref[m, :, at].astype(F32).T.astype(BF16)
            for k in range(TILE // 16):
                block = j * (TILE // 16) + k
                zhi, rest = divmod(block, 32)
                xy, c = divmod(rest, 2)
                to = lax.bitwise_xor(core, c) * (depth // 2) + (xy * 32 + zhi * 16)
                to = pl.ds(pl.multiple_of(to, 16), 16)
                aggt_ref[to, cols] = agg[k * 16 : (k + 1) * 16]
                hidt_ref[to, cols] = hid[k * 16 : (k + 1) * 16]
            s = summed_ref[m, :, at]
            t = jnp.tanh(s * (GELU_C + (GELU_C * 0.044715) * (s * s)))
            slope_ref[m, :, at] = 0.5 * (1.0 + t) + (0.5 * GELU_C) * s * (1.0 - t * t) * (
                1.0 + 3.0 * 0.044715 * (s * s)
            )


def decode(where_ref, code_refs, f_ref):
    local = code_refs[0].shape[0]
    rows = [
        ref[m, VROWS - 16 :, :].astype(jnp.int32).astype(F32)[8:9, :VPAD]
        for ref in code_refs
        for m in range(local)
    ]
    rows.append(jnp.zeros((VPAD - len(rows), VPAD), F32))
    power = (jnp.exp2(jnp.concatenate(rows, axis=0)) * (1.0 / QMAX)).T
    for k, ref in enumerate(code_refs):
        first = lax.rem(where_ref[1] + k, len(code_refs)) * local
        for m in range(local):
            code = ref[m].astype(jnp.int32).astype(F32)[:VUSE]
            at = k * local + m
            f_ref[first + m] = code * power[:VUSE, at : at + 1]


def score_kernel(
    where_ref, c0_any, c1_any, c2_any, c3_any, truth_hbm, score_ref,
    c_ref, truth_ref, f_ref, in_sem,
):
    members = f_ref.shape[0]
    nvar = truth_ref.shape[0]
    codes = [c_ref.at[k] for k in range(4)]
    pairs = list(zip((c0_any, c1_any, c2_any, c3_any), codes)) + [(truth_hbm, truth_ref)]
    copies = [start_copy(src, dst, in_sem.at[k]) for k, (src, dst) in enumerate(pairs)]
    for copy in copies:
        copy.wait()
    decode(where_ref, codes, f_ref)
    collected = [f_ref[m][:nvar] for m in range(members)]
    truth = truth_ref[...]
    skill = sum(smooth_abs(f - truth) for f in collected)
    spread = jnp.zeros_like(skill)
    for m in range(members):
        for o in range(m + 1, members):
            spread = spread + smooth_abs(collected[m] - collected[o])
    score_ref[...] = skill * (1.0 / members) - (pair_factor(members) * 2.0) * spread


def backward_kernel(
    where_ref, c0_ref, c1_ref, c2_ref, c3_ref, truth_ref, var_ref, area_ref, dpt_ref,
    aggt_ref, hidt_ref, slope_ref, theirs_ref, sg_ref, grad_ref, f_ref, g_ref,
):
    members = f_ref.shape[0]
    nvar = truth_ref.shape[0]
    local, points, depth = slope_ref.shape
    half = depth // 2
    decode(where_ref, (c0_ref, c1_ref, c2_ref, c3_ref), f_ref)
    first = where_ref[1] * local
    truth = truth_ref[...]
    g_ref[96:] = jnp.zeros((VPAD - 96, points), F32)
    grads = []
    for m in range(local):
        own = f_ref[first + m][:nvar]
        mutual = sum(signum(own - f_ref[o][:nvar]) for o in range(members))
        g_ref[:nvar] = area_ref[...] * (
            signum(own - truth) * (1.0 / members) - (2.0 * pair_factor(members)) * mutual
        )
        grads.append((g_ref[...].T * var_ref[...]).astype(BF16))
    grad = jnp.concatenate(grads, axis=0)
    grad_ref[...] = grad
    theirs_ref[:, depth:] = dot(hidt_ref[half:], grad).astype(BF16)
    for j in range(depth // TILE):
        at = slice(j * TILE, (j + 1) * TILE)
        hg = dot(grad, dpt_ref[:, at])
        for m in range(local):
            rows = slice(m * points, (m + 1) * points)
            sg_ref[rows, at] = (hg[rows] * slope_ref[m, :, at]).astype(BF16)
        theirs_ref[:, at] = dot(aggt_ref[half:], sg_ref[:, at]).astype(BF16)


def mine_kernel(grad_ref, sg_ref, aggt_ref, hidt_ref, mine_ref):
    half, cols = mine_ref.shape
    depth = sg_ref.shape[1]
    mine_ref[:, depth:] = dot(hidt_ref[:half], grad_ref[...]).astype(BF16)
    for j in range(depth // TILE):
        at = slice(j * TILE, (j + 1) * TILE)
        mine_ref[:, at] = dot(aggt_ref[:half], sg_ref[:, at]).astype(BF16)


def merge_kernel(mine_ref, theirs_ref, after_any, out_hbm, out_ref, out_sem):
    rows = mine_ref.shape[0] // 4
    outs = []
    for k in range(4):
        at = slice(k * rows, (k + 1) * rows)
        out_ref[at] = (mine_ref[at].astype(F32) + theirs_ref[at].astype(F32)).astype(BF16)
        cut = pl.ds(k * rows, rows)
        outs.append(start_copy(out_ref.at[cut], out_hbm.at[cut], out_sem.at[k]))
    for copy in outs:
        copy.wait()


def rows_kernel(cft_ref, sg_ref, core_hbm, odd_hbm, core_ref, odd_ref, out_sem):
    local, _, depth = core_ref.shape
    points = cft_ref.shape[1] // 2
    high = cft_ref[HALO:, :points]
    low = cft_ref[HALO:, points:]
    outs = []
    for m in range(local):
        for j in range(depth // TILE):
            at = slice(j * TILE, (j + 1) * TILE)
            s = sg_ref[m * points : (m + 1) * points, at]
            g = (dot(high, s) + dot(low, s)).astype(BF16)
            core_ref[m, :, at] = g[:HALO]
            odd_ref[m, :, at] = g[HALO:]
        outs.append(start_copy(odd_ref.at[m], odd_hbm.at[m], out_sem.at[0, m]))
        outs.append(start_copy(core_ref.at[m], core_hbm.at[m], out_sem.at[1, m]))
    for copy in outs:
        copy.wait()


def plane_kernel(got_ref, out_hbm, out_ref, out_sem):
    per = out_hbm.shape[2]
    outs = []
    for z in range(out_hbm.shape[1]):
        at = slice(z * per, (z + 1) * per)
        total = got_ref[0, at].astype(F32)
        for k in range(1, got_ref.shape[0]):
            total = total + got_ref[k, at].astype(F32)
        out_ref[z] = total.astype(BF16)
        for e in range(out_hbm.shape[0]):
            outs.append(start_copy(out_ref.at[z], out_hbm.at[e, z], out_sem.at[z, e]))
    for copy in outs:
        copy.wait()


def final_kernel(got_ref, src_ref, out_ref, *, scaling):
    total = got_ref[0].astype(F32)
    for k in range(1, got_ref.shape[0]):
        total = total + got_ref[k].astype(F32)
    total = total * scaling
    depth = src_ref.shape[1]
    src_ref[...] = total[:, :depth]
    out_ref[...] = total[:, depth : depth + out_ref.shape[1]]


def latent_kernel(
    cft_hbm, sg_hbm, w_hbm, core_any, far_any, near_any, out_hbm,
    cft_ref, sg_ref, w_ref, core_ref, far_ref, near_ref, g_ref, out_ref, in_sem, out_sem,
):
    local, rows, depth = core_ref.shape
    points = cft_ref.shape[1] // 2
    steps = depth // TILE
    pairs = (
        (cft_hbm.at[pl.ds(0, HALO)], cft_ref), (sg_hbm, sg_ref), (core_any, core_ref),
        (far_any, far_ref), (near_any, near_ref), (w_hbm, w_ref),
    )
    copies = [start_copy(src, dst, in_sem.at[k]) for k, (src, dst) in enumerate(pairs)]
    for copy in copies[:5]:
        copy.wait()
    high = cft_ref[:, :points]
    low = cft_ref[:, points:]
    for m in range(local):
        for j in range(steps):
            at = slice(j * TILE, (j + 1) * TILE)
            s = sg_ref[m * points : (m + 1) * points, at]
            g = dot(high, s) + dot(low, s)
            for ref in (core_ref, far_ref, near_ref):
                g = g + ref[m, :, at].astype(F32)
            g_ref[m * HALO : (m + 1) * HALO, at] = g.astype(BF16)
    copies[5].wait()
    outs = []
    for j in range(steps):
        at = slice(j * TILE, (j + 1) * TILE)
        r = dot_nt(g_ref[...], w_ref[at, :]).astype(BF16)
        for m in range(local):
            out_ref[m, :, at] = r[m * HALO : (m + 1) * HALO]
        cols = pl.ds(j * TILE, TILE)
        outs.append(start_copy(out_ref.at[:, :, cols], out_hbm.at[:, :, cols], out_sem.at[j]))
    for copy in outs:
        copy.wait()


def shape(dims, dtype):
    return jax.ShapeDtypeStruct(dims, dtype)


def scratch(*arrays):
    return [pltpu.VMEM(a.shape, a.dtype) for a in arrays]


def sems(*dims):
    return pltpu.SemaphoreType.DMA(dims)


def call(
    kernel, name, out_shape, in_specs, out_specs, scratch_shapes, work, operands, limit=LIMIT
):
    return pl.pallas_call(
        kernel,
        out_shape=out_shape,
        in_specs=in_specs,
        out_specs=out_specs,
        scratch_shapes=scratch_shapes,
        compiler_params=params(limit),
        cost_estimate=cost(*work),
        name=name,
    )(*operands)


def call_prepare(where, edge_count, edge_src, edge_dst, edge_weight, latent, core_lat, weight):
    local, rows, depth = latent.shape
    window = rows + 2 * HALO
    points = edge_src.shape[0] * BLK
    cf = shape((points, 2 * window), BF16)
    cft = shape((window, 2 * points), BF16)
    return call(
        prepare_kernel,
        "prepare",
        (cf, cft, shape((points, 2 * HALO), BF16), shape((local, points, depth), F32)),
        smem(1) + hbm(5) + anywhere(1) + hbm(1),
        tuple(vmem(1) + hbm(1) + vmem(2)),
        [pltpu.SMEM(edge_count.shape, jnp.int32)]
        + scratch(edge_src, edge_dst, edge_weight)
        + [pltpu.VMEM((local * 2 * HALO, depth), BF16)]
        + scratch(weight, cft)
        + [sems(5 + 2 * local), pltpu.SemaphoreType.DMA],
        (3 * 10**9, 6 * 10**6),
        (where, edge_count, edge_src, edge_dst, edge_weight, latent, core_lat, weight),
        PREP,
    )


def call_forward(odd_lat, weight, cfo, part, dpt):
    local, points, depth = part.shape
    return call(
        forward_kernel,
        "forward",
        (
            shape(part.shape, F32),
            shape(part.shape, BF16),
            shape((local, VROWS, points), jnp.int16),
        ),
        vmem(5),
        tuple(vmem(3)),
        [],
        (2 * 10**9, 8 * 10**6),
        (odd_lat, weight, cfo, part, dpt),
    )


def call_factors(where, latent, core_lat, odd_lat, cf, summed, hidden):
    local, points, depth = summed.shape
    left = shape((depth, local * points), BF16)
    return call(
        factors_kernel,
        "factors",
        (left, left, shape(summed.shape, F32)),
        smem(1) + vmem(6),
        tuple(vmem(3)),
        [pltpu.VMEM((cf.shape[1] // 2, depth), BF16)],
        (3 * 10**9, 10 * 10**6),
        (where, latent, core_lat, odd_lat, cf, summed, hidden),
    )


def call_backward(where, codes, truth, var_row, area_row, dpt, aggt, hidt, slope):
    local, points, depth = slope.shape
    part = shape((depth // 2, depth + VPAD), BF16)
    return call(
        backward_kernel,
        "backward",
        (part, shape((local * points, depth), BF16), shape((local * points, VPAD), BF16)),
        smem(1) + vmem(len(codes) + 7),
        tuple(vmem(3)),
        [
            pltpu.VMEM((local * len(codes), VUSE, points), F32),
            pltpu.VMEM((VPAD, points), F32),
        ],
        (2 * 10**9, 5 * 10**6),
        (where, *codes, truth, var_row, area_row, dpt, aggt, hidt, slope),
    )


def call_mine(grad, summed_grad, aggt, hidt):
    return call(
        mine_kernel,
        "mine",
        shape((aggt.shape[0] // 2, summed_grad.shape[1] + VPAD), BF16),
        vmem(4),
        vmem(1)[0],
        [],
        (10**9, 4 * 10**6),
        (grad, summed_grad, aggt, hidt),
    )


def call_merge(mine, theirs, after):
    return call(
        merge_kernel,
        "merge",
        shape(mine.shape, BF16),
        vmem(2) + anywhere(1),
        hbm(1)[0],
        scratch(mine) + [sems(4)],
        (10**6, 4 * 10**6),
        (mine, theirs, after),
    )


def call_rows(cft, summed_grad, local):
    send = shape((local, HALO, summed_grad.shape[1]), BF16)
    return call(
        rows_kernel,
        "rows",
        (send, send),
        vmem(2),
        tuple(hbm(2)),
        scratch(send, send) + [sems(2, local)],
        (10**9, 3 * 10**6),
        (cft, summed_grad),
    )


def call_plane(got, ens):
    out_shape = shape((ens, 2, got.shape[1] // 2, got.shape[2]), BF16)
    return call(
        plane_kernel,
        "plane",
        out_shape,
        vmem(1),
        hbm(1)[0],
        [pltpu.VMEM((2,) + out_shape.shape[2:], BF16), sems(2, ens)],
        (10**6, 10**6),
        (got,),
    )


def call_score(where, codes, truth):
    local, _, points = codes[0].shape
    return call(
        score_kernel,
        "score",
        shape(truth.shape, F32),
        smem(1) + anywhere(len(codes)) + hbm(1),
        vmem(1)[0],
        [pltpu.VMEM((len(codes),) + codes[0].shape, jnp.int16)]
        + scratch(truth)
        + [pltpu.VMEM((local * len(codes), VUSE, points), F32), sems(len(codes) + 1)],
        (10**7, 10**6),
        (where, *codes, truth),
        LARGE,
    )


def call_latent(cft, summed_grad, weight, core_grad, far_grad, near_grad):
    local, rows, depth = core_grad.shape
    return call(
        latent_kernel,
        "latent",
        shape(core_grad.shape, BF16),
        hbm(3) + anywhere(3),
        hbm(1)[0],
        [pltpu.VMEM((HALO, cft.shape[1]), BF16)]
        + scratch(summed_grad, weight, core_grad, far_grad, near_grad)
        + [pltpu.VMEM((local * rows, depth), BF16)]
        + scratch(core_grad)
        + [sems(6), sems(depth // TILE)],
        (10**9, 5 * 10**6),
        (cft, summed_grad, weight, core_grad, far_grad, near_grad),
        LARGE,
    )


def call_final(got, nvar, scaling):
    per = got.shape[1]
    return call(
        functools.partial(final_kernel, scaling=scaling),
        "final",
        (shape((per, got.shape[2] - VPAD), F32), shape((per, nvar), F32)),
        vmem(1),
        tuple(vmem(2)),
        [],
        (10**5, 4 * 10**5),
        (got,),
    )


def make_body(count):
    odd_pairs = [(i, (i + 1) % count if i % 2 else (i - 1) % count) for i in range(count)]
    far = [p for p in odd_pairs if abs(p[0] - p[1]) > 1 or p[0] // 32 != p[1] // 32]
    near = [p for p in odd_pairs if p not in far]
    swap = [(0, 1), (1, 0)]

    def body(
        latent, src_weight, decoder_projection, truth, area_weight, var_weight,
        edge_src, edge_dst, edge_weight, edge_count,
    ):
        local, rows, depth = latent.shape
        ens = lax.axis_size("ens")
        members = local * ens
        nvar = decoder_projection.shape[1]
        points = truth.shape[1]
        per = depth // count
        where = jnp.stack([lax.axis_index("core"), lax.axis_index("ens")]).astype(jnp.int32)

        odd_lat = lax.ppermute(latent, SPACE, odd_pairs).reshape(local * rows, depth)
        core_lat = lax.ppermute(latent, "core", swap)
        dpt = jnp.pad(decoder_projection.T, ((0, VPAD - nvar), (0, 0)))
        cf, cft, cfo, part = call_prepare(
            where, edge_count, edge_src, edge_dst, edge_weight, latent, core_lat, src_weight
        )
        var_row = jnp.pad(var_weight, (0, VPAD - nvar)).reshape(1, VPAD)
        area_row = area_weight.reshape(1, points)
        summed, hidden, coded = call_forward(odd_lat, src_weight, cfo, part, dpt)
        codes = [coded] + [
            lax.ppermute(coded, "ens", [((e + k) % ens, e) for e in range(ens)])
            for k in range(1, ens)
        ]
        aggt, hidt, slope = call_factors(
            where, latent, core_lat, odd_lat, cf, summed, hidden
        )
        theirs, summed_grad, grad = call_backward(
            where, codes, truth, var_row, area_row, dpt, aggt, hidt, slope
        )
        theirs = lax.ppermute(theirs, "core", swap)
        mine = call_mine(grad, summed_grad, aggt, hidt)
        core_send, odd_send = call_rows(cft, summed_grad, local)
        near_grad = lax.ppermute(odd_send, SPACE, near)
        part = call_merge(mine, theirs, odd_send)
        part, odd_send, core_send = lax.optimization_barrier((part, odd_send, core_send))
        part = part.reshape(16, 2 * per, part.shape[1])
        got = lax.all_to_all(part, ("x", "y"), 0, 0, tiled=True)
        far_grad = lax.ppermute(odd_send, SPACE, far)
        core_grad = lax.ppermute(core_send, "core", swap)
        plane = call_plane(got, ens).reshape(2 * ens, per, got.shape[2])
        got = lax.all_to_all(plane, ("ens", "zhi"), 0, 0, tiled=True)
        score = call_score(where, codes, truth)
        grad_latent = call_latent(cft, summed_grad, src_weight, core_grad, far_grad, near_grad)
        scaling = 1.0 / math.sqrt(members * points * count)
        grad_src, grad_out = call_final(got, nvar, scaling)
        return score, grad_latent, grad_src, grad_out

    return body


def solution(mesh):
    fine = jax.sharding.Mesh(
        mesh.devices.reshape(mesh.devices.shape[0], 2, 4, 4, 2), ("ens",) + SPACE
    )
    return jax.shard_map(
        make_body(mesh.devices.shape[1]),
        mesh=fine,
        in_specs=(
            P("ens", SPACE, None), P(), P(), P(None, SPACE), P(SPACE), P(),
            P(SPACE, None), P(SPACE, None), P(SPACE, None), P(SPACE),
        ),
        out_specs=(P(None, SPACE), P("ens", SPACE, None), P(SPACE, None), P(SPACE, None)),
        check_vma=False,
    )
```

```python
import functools
import math

import jax
import jax.numpy as jnp
from jax import lax
from jax.experimental import pallas as pl
from jax.experimental.pallas import tpu as pltpu
from jax.sharding import PartitionSpec as P

HALO = 128
BLK = 128
ALPHA = 0.95
DELTA = 0.05
SPACE = ("zhi", "x", "y", "core")
QMAX = 32000.0
VPAD = 128
VROWS = 112
VUSE = 104
TILE = 256
GELU_C = math.sqrt(2.0 / math.pi)
MIB = 1 << 20
LIMIT = 24
PREP = 50
LARGE = 56
F32 = jnp.float32
BF16 = jnp.bfloat16


def dot(a, b):
    return jnp.dot(a, b, preferred_element_type=F32)


def dot_nt(a, b):
    return lax.dot_general(a, b, (((1,), (1,)), ((), ())), preferred_element_type=F32)


def smem(count):
    return [pl.BlockSpec(memory_space=pltpu.SMEM)] * count


def cost(flops, nbytes):
    return pl.CostEstimate(flops=flops, bytes_accessed=nbytes, transcendentals=0)


def params(mib):
    return pltpu.CompilerParams(vmem_limit_bytes=mib * MIB)


def hbm(count):
    return [pl.BlockSpec(memory_space=pltpu.HBM)] * count


def vmem(count):
    return [pl.BlockSpec(memory_space=pltpu.VMEM)] * count


def anywhere(count):
    return [pl.BlockSpec(memory_space=pl.ANY)] * count


def start_copy(src, dst, sem):
    copy = pltpu.make_async_copy(src, dst, sem)
    copy.start()
    return copy


def pair_factor(members):
    fair_eps = (1.0 - ALPHA) / members
    return (1.0 - fair_eps) / (2.0 * members * (members - 1))


def smooth_abs(distance):
    square = distance * distance + DELTA * DELTA
    return square * lax.rsqrt(square)


def signum(distance):
    return distance * lax.rsqrt(distance * distance + DELTA * DELTA)


def prepare_kernel(
    where_ref, count_hbm, src_hbm, dst_hbm, wt_hbm, lat_hbm, clat_hbm, w_hbm,
    cf_ref, cft_hbm, cfo_ref, part_ref,
    count_ref, src_ref, dst_ref, wt_ref, x_ref, w_ref, cft_ref, in_sem, out_sem,
):
    edges = [
        start_copy(src, dst, in_sem.at[k])
        for k, (src, dst) in enumerate(
            ((count_hbm, count_ref), (src_hbm, src_ref), (dst_hbm, dst_ref), (wt_hbm, wt_ref))
        )
    ]
    local = lat_hbm.shape[0]
    inputs = []
    for m in range(local):
        for k, ref in enumerate((lat_hbm, clat_hbm)):
            inputs.append(
                start_copy(
                    ref.at[m],
                    x_ref.at[pl.ds((2 * m + k) * HALO, HALO)],
                    in_sem.at[4 + 2 * m + k],
                )
            )
    inputs.append(start_copy(w_hbm, w_ref, in_sem.at[4 + 2 * local]))
    core = where_ref[0]
    slots = src_ref.shape[1]
    window = cf_ref.shape[1] // 2
    points = cf_ref.shape[0]
    for copy in edges:
        copy.wait()
    for b in range(src_ref.shape[0]):
        src = src_ref[b : b + 1, :]
        slot = lax.broadcasted_iota(jnp.int32, (1, slots), 1)
        wt = jnp.where(slot < count_ref[b], wt_ref[b : b + 1, :], 0.0)
        left = 2 * HALO - HALO * core
        right = HALO + HALO * core
        place = jnp.where(
            src < HALO,
            src + left,
            jnp.where(src < 2 * HALO, src - HALO, src - 2 * HALO + right),
        )
        rows = lax.broadcasted_iota(jnp.int32, (window, slots), 0)
        hot = jnp.where(rows == place, 1.0, 0.0).astype(BF16)
        pts = lax.broadcasted_iota(jnp.int32, (BLK, slots), 0)
        mat = jnp.where(pts == dst_ref[b : b + 1, :], wt, 0.0).astype(BF16)
        coef = dot_nt(mat, hot)
        high = coef.astype(BF16)
        low = (coef - high.astype(F32)).astype(BF16)
        at = slice(b * BLK, (b + 1) * BLK)
        cf_ref[at, :window] = high
        cf_ref[at, window:] = low
        cfo_ref[at, :HALO] = high[:, 2 * HALO :]
        cfo_ref[at, HALO:] = low[:, 2 * HALO :]
        coef_t = dot_nt(hot, mat)
        high_t = coef_t.astype(BF16)
        cft_ref[:, b * BLK : (b + 1) * BLK] = high_t
        cft_ref[:, points + b * BLK : points + (b + 1) * BLK] = (
            coef_t - high_t.astype(F32)
        ).astype(BF16)
    out = start_copy(cft_ref, cft_hbm, out_sem)
    for copy in inputs:
        copy.wait()
    x = x_ref[...]
    high = cf_ref[:, : 2 * HALO]
    low = cf_ref[:, window : window + 2 * HALO]
    for j in range(w_ref.shape[1] // TILE):
        at = slice(j * TILE, (j + 1) * TILE)
        p = dot(x, w_ref[:, at]).astype(BF16)
        for m in range(local):
            pm = p[2 * m * HALO : (2 * m + 2) * HALO]
            part_ref[m, :, at] = dot(high, pm) + dot(low, pm)
    out.wait()


def forward_kernel(
    odd_ref, w_ref, cfo_ref, part_ref, dpt_ref, summed_ref, hidden_ref, code_ref
):
    local, points, depth = part_ref.shape
    forecast = [jnp.zeros((VPAD, points), F32) for _ in range(local)]
    for j in range(depth // TILE):
        at = slice(j * TILE, (j + 1) * TILE)
        p = dot(odd_ref[...], w_ref[:, at]).astype(BF16)
        for m in range(local):
            pm = p[m * HALO : (m + 1) * HALO]
            s = part_ref[m, :, at] + dot(cfo_ref[...], jnp.concatenate([pm, pm], axis=0))
            summed_ref[m, :, at] = s
            t = jnp.tanh(s * (GELU_C + (GELU_C * 0.044715) * (s * s)))
            h = (0.5 * s * (1.0 + t)).astype(BF16)
            hidden_ref[m, :, at] = h
            forecast[m] = forecast[m] + dot_nt(dpt_ref[:, at], h)
    for m in range(local):
        f = forecast[m]
        largest = jnp.maximum(jnp.max(jnp.abs(f), axis=1, keepdims=True), 1e-30)
        power = jnp.ceil(jnp.log(largest) * (1.0 / math.log(2.0)) + 1e-3)
        power = jnp.broadcast_to(power, (VPAD, VPAD))
        q = f * (jnp.exp2(-power[:, :1]) * QMAX)
        q = jnp.where(q >= 0.0, q + 0.5, q - 0.5)
        row = jnp.concatenate([power.T[:8], jnp.zeros((8, points - VPAD), F32)], axis=1)
        row = jnp.where(row >= 0.0, row + 0.5, row - 0.5)
        code = jnp.concatenate([q[:VUSE], row], axis=0)
        code_ref[m] = code.astype(jnp.int32).astype(jnp.int16)


def factors_kernel(
    where_ref, lat_ref, clat_ref, olat_ref, cf_ref, summed_ref, hidden_ref,
    aggt_ref, hidt_ref, slope_ref, x_ref,
):
    core = where_ref[0]
    window = cf_ref.shape[1] // 2
    local, points, depth = summed_ref.shape
    high = cf_ref[:, :window]
    low = cf_ref[:, window:]
    for m in range(local):
        x_ref[:HALO] = lat_ref[m]
        x_ref[HALO : 2 * HALO] = clat_ref[m]
        x_ref[2 * HALO :] = olat_ref[m * HALO : (m + 1) * HALO]
        cols = slice(m * points, (m + 1) * points)
        for j in range(depth // TILE):
            at = slice(j * TILE, (j + 1) * TILE)
            x = x_ref[:, at]
            agg = (dot(high, x) + dot(low, x)).T.astype(BF16)
            hid = hidden_ref[m, :, at].astype(F32).T.astype(BF16)
            for k in range(TILE // 16):
                block = j * (TILE // 16) + k
                zhi, rest = divmod(block, 32)
                xy, c = divmod(rest, 2)
                to = lax.bitwise_xor(core, c) * (depth // 2) + (xy * 32 + zhi * 16)
                to = pl.ds(pl.multiple_of(to, 16), 16)
                aggt_ref[to, cols] = agg[k * 16 : (k + 1) * 16]
                hidt_ref[to, cols] = hid[k * 16 : (k + 1) * 16]
            s = summed_ref[m, :, at]
            t = jnp.tanh(s * (GELU_C + (GELU_C * 0.044715) * (s * s)))
            slope_ref[m, :, at] = 0.5 * (1.0 + t) + (0.5 * GELU_C) * s * (1.0 - t * t) * (
                1.0 + 3.0 * 0.044715 * (s * s)
            )


def decode(where_ref, code_refs, f_ref):
    local = code_refs[0].shape[0]
    rows = [
        ref[m, VROWS - 16 :, :].astype(jnp.int32).astype(F32)[8:9, :VPAD]
        for ref in code_refs
        for m in range(local)
    ]
    rows.append(jnp.zeros((VPAD - len(rows), VPAD), F32))
    power = (jnp.exp2(jnp.concatenate(rows, axis=0)) * (1.0 / QMAX)).T
    for k, ref in enumerate(code_refs):
        first = lax.rem(where_ref[1] + k, len(code_refs)) * local
        for m in range(local):
            code = ref[m].astype(jnp.int32).astype(F32)[:VUSE]
            at = k * local + m
            f_ref[first + m] = code * power[:VUSE, at : at + 1]


def score_kernel(
    where_ref, c0_any, c1_any, c2_any, c3_any, truth_hbm, score_ref,
    c_ref, truth_ref, f_ref, in_sem,
):
    members = f_ref.shape[0]
    nvar = truth_ref.shape[0]
    codes = [c_ref.at[k] for k in range(4)]
    pairs = list(zip((c0_any, c1_any, c2_any, c3_any), codes)) + [(truth_hbm, truth_ref)]
    copies = [start_copy(src, dst, in_sem.at[k]) for k, (src, dst) in enumerate(pairs)]
    for copy in copies:
        copy.wait()
    decode(where_ref, codes, f_ref)
    collected = [f_ref[m][:nvar] for m in range(members)]
    truth = truth_ref[...]
    skill = sum(smooth_abs(f - truth) for f in collected)
    spread = jnp.zeros_like(skill)
    for m in range(members):
        for o in range(m + 1, members):
            spread = spread + smooth_abs(collected[m] - collected[o])
    score_ref[...] = skill * (1.0 / members) - (pair_factor(members) * 2.0) * spread


def backward_kernel(
    where_ref, c0_ref, c1_ref, c2_ref, c3_ref, truth_ref, var_ref, area_ref, dpt_ref,
    aggt_ref, hidt_ref, slope_ref, theirs_ref, sg_ref, grad_ref, f_ref, g_ref,
):
    members = f_ref.shape[0]
    nvar = truth_ref.shape[0]
    local, points, depth = slope_ref.shape
    half = depth // 2
    decode(where_ref, (c0_ref, c1_ref, c2_ref, c3_ref), f_ref)
    first = where_ref[1] * local
    truth = truth_ref[...]
    g_ref[96:] = jnp.zeros((VPAD - 96, points), F32)
    grads = []
    for m in range(local):
        own = f_ref[first + m][:nvar]
        mutual = sum(signum(own - f_ref[o][:nvar]) for o in range(members))
        g_ref[:nvar] = area_ref[...] * (
            signum(own - truth) * (1.0 / members) - (2.0 * pair_factor(members)) * mutual
        )
        grads.append((g_ref[...].T * var_ref[...]).astype(BF16))
    grad = jnp.concatenate(grads, axis=0)
    grad_ref[...] = grad
    theirs_ref[:, depth:] = dot(hidt_ref[half:], grad).astype(BF16)
    for j in range(depth // TILE):
        at = slice(j * TILE, (j + 1) * TILE)
        hg = dot(grad, dpt_ref[:, at])
        for m in range(local):
            rows = slice(m * points, (m + 1) * points)
            sg_ref[rows, at] = (hg[rows] * slope_ref[m, :, at]).astype(BF16)
        theirs_ref[:, at] = dot(aggt_ref[half:], sg_ref[:, at]).astype(BF16)


def mine_kernel(grad_ref, sg_ref, aggt_ref, hidt_ref, mine_ref):
    half, cols = mine_ref.shape
    depth = sg_ref.shape[1]
    mine_ref[:, depth:] = dot(hidt_ref[:half], grad_ref[...]).astype(BF16)
    for j in range(depth // TILE):
        at = slice(j * TILE, (j + 1) * TILE)
        mine_ref[:, at] = dot(aggt_ref[:half], sg_ref[:, at]).astype(BF16)


def merge_kernel(mine_ref, theirs_ref, after_any, out_hbm, out_ref, out_sem):
    rows = mine_ref.shape[0] // 4
    outs = []
    for k in range(4):
        at = slice(k * rows, (k + 1) * rows)
        out_ref[at] = (mine_ref[at].astype(F32) + theirs_ref[at].astype(F32)).astype(BF16)
        cut = pl.ds(k * rows, rows)
        outs.append(start_copy(out_ref.at[cut], out_hbm.at[cut], out_sem.at[k]))
    for copy in outs:
        copy.wait()


def rows_kernel(cft_ref, sg_ref, core_hbm, odd_hbm, core_ref, odd_ref, out_sem):
    local, _, depth = core_ref.shape
    points = cft_ref.shape[1] // 2
    high = cft_ref[HALO:, :points]
    low = cft_ref[HALO:, points:]
    outs = []
    for m in range(local):
        for j in range(depth // TILE):
            at = slice(j * TILE, (j + 1) * TILE)
            s = sg_ref[m * points : (m + 1) * points, at]
            g = (dot(high, s) + dot(low, s)).astype(BF16)
            core_ref[m, :, at] = g[:HALO]
            odd_ref[m, :, at] = g[HALO:]
        outs.append(start_copy(odd_ref.at[m], odd_hbm.at[m], out_sem.at[0, m]))
        outs.append(start_copy(core_ref.at[m], core_hbm.at[m], out_sem.at[1, m]))
    for copy in outs:
        copy.wait()


def plane_kernel(got_ref, out_hbm, out_ref, out_sem):
    per = out_hbm.shape[2]
    outs = []
    for z in range(out_hbm.shape[1]):
        at = slice(z * per, (z + 1) * per)
        total = got_ref[0, at].astype(F32)
        for k in range(1, got_ref.shape[0]):
            total = total + got_ref[k, at].astype(F32)
        out_ref[z] = total.astype(BF16)
        for e in range(out_hbm.shape[0]):
            outs.append(start_copy(out_ref.at[z], out_hbm.at[e, z], out_sem.at[z, e]))
    for copy in outs:
        copy.wait()


def final_kernel(got_ref, src_ref, out_ref, *, scaling):
    total = got_ref[0].astype(F32)
    for k in range(1, got_ref.shape[0]):
        total = total + got_ref[k].astype(F32)
    total = total * scaling
    depth = src_ref.shape[1]
    src_ref[...] = total[:, :depth]
    out_ref[...] = total[:, depth : depth + out_ref.shape[1]]


def latent_kernel(
    cft_hbm, sg_hbm, w_hbm, core_any, far_any, near_any, out_hbm,
    cft_ref, sg_ref, w_ref, core_ref, far_ref, near_ref, g_ref, out_ref, in_sem, out_sem,
):
    local, rows, depth = core_ref.shape
    points = cft_ref.shape[1] // 2
    steps = depth // TILE
    pairs = (
        (cft_hbm.at[pl.ds(0, HALO)], cft_ref), (sg_hbm, sg_ref), (core_any, core_ref),
        (far_any, far_ref), (near_any, near_ref), (w_hbm, w_ref),
    )
    copies = [start_copy(src, dst, in_sem.at[k]) for k, (src, dst) in enumerate(pairs)]
    for copy in copies[:5]:
        copy.wait()
    high = cft_ref[:, :points]
    low = cft_ref[:, points:]
    for m in range(local):
        for j in range(steps):
            at = slice(j * TILE, (j + 1) * TILE)
            s = sg_ref[m * points : (m + 1) * points, at]
            g = dot(high, s) + dot(low, s)
            for ref in (core_ref, far_ref, near_ref):
                g = g + ref[m, :, at].astype(F32)
            g_ref[m * HALO : (m + 1) * HALO, at] = g.astype(BF16)
    copies[5].wait()
    outs = []
    for j in range(steps):
        at = slice(j * TILE, (j + 1) * TILE)
        r = dot_nt(g_ref[...], w_ref[at, :]).astype(BF16)
        for m in range(local):
            out_ref[m, :, at] = r[m * HALO : (m + 1) * HALO]
        cols = pl.ds(j * TILE, TILE)
        outs.append(start_copy(out_ref.at[:, :, cols], out_hbm.at[:, :, cols], out_sem.at[j]))
    for copy in outs:
        copy.wait()


def shape(dims, dtype):
    return jax.ShapeDtypeStruct(dims, dtype)


def scratch(*arrays):
    return [pltpu.VMEM(a.shape, a.dtype) for a in arrays]


def sems(*dims):
    return pltpu.SemaphoreType.DMA(dims)


def call(
    kernel, name, out_shape, in_specs, out_specs, scratch_shapes, work, operands, limit=LIMIT
):
    return pl.pallas_call(
        kernel,
        out_shape=out_shape,
        in_specs=in_specs,
        out_specs=out_specs,
        scratch_shapes=scratch_shapes,
        compiler_params=params(limit),
        cost_estimate=cost(*work),
        name=name,
    )(*operands)


def call_prepare(where, edge_count, edge_src, edge_dst, edge_weight, latent, core_lat, weight):
    local, rows, depth = latent.shape
    window = rows + 2 * HALO
    points = edge_src.shape[0] * BLK
    cf = shape((points, 2 * window), BF16)
    cft = shape((window, 2 * points), BF16)
    return call(
        prepare_kernel,
        "prepare",
        (cf, cft, shape((points, 2 * HALO), BF16), shape((local, points, depth), F32)),
        smem(1) + hbm(5) + anywhere(1) + hbm(1),
        tuple(vmem(1) + hbm(1) + vmem(2)),
        [pltpu.SMEM(edge_count.shape, jnp.int32)]
        + scratch(edge_src, edge_dst, edge_weight)
        + [pltpu.VMEM((local * 2 * HALO, depth), BF16)]
        + scratch(weight, cft)
        + [sems(5 + 2 * local), pltpu.SemaphoreType.DMA],
        (3 * 10**9, 6 * 10**6),
        (where, edge_count, edge_src, edge_dst, edge_weight, latent, core_lat, weight),
        PREP,
    )


def call_forward(odd_lat, weight, cfo, part, dpt):
    local, points, depth = part.shape
    return call(
        forward_kernel,
        "forward",
        (
            shape(part.shape, F32),
            shape(part.shape, BF16),
            shape((local, VROWS, points), jnp.int16),
        ),
        vmem(5),
        tuple(vmem(3)),
        [],
        (2 * 10**9, 8 * 10**6),
        (odd_lat, weight, cfo, part, dpt),
    )


def call_factors(where, latent, core_lat, odd_lat, cf, summed, hidden):
    local, points, depth = summed.shape
    left = shape((depth, local * points), BF16)
    return call(
        factors_kernel,
        "factors",
        (left, left, shape(summed.shape, F32)),
        smem(1) + vmem(6),
        tuple(vmem(3)),
        [pltpu.VMEM((cf.shape[1] // 2, depth), BF16)],
        (3 * 10**9, 10 * 10**6),
        (where, latent, core_lat, odd_lat, cf, summed, hidden),
    )


def call_backward(where, codes, truth, var_row, area_row, dpt, aggt, hidt, slope):
    local, points, depth = slope.shape
    part = shape((depth // 2, depth + VPAD), BF16)
    return call(
        backward_kernel,
        "backward",
        (part, shape((local * points, depth), BF16), shape((local * points, VPAD), BF16)),
        smem(1) + vmem(len(codes) + 7),
        tuple(vmem(3)),
        [
            pltpu.VMEM((local * len(codes), VUSE, points), F32),
            pltpu.VMEM((VPAD, points), F32),
        ],
        (2 * 10**9, 5 * 10**6),
        (where, *codes, truth, var_row, area_row, dpt, aggt, hidt, slope),
    )


def call_mine(grad, summed_grad, aggt, hidt):
    return call(
        mine_kernel,
        "mine",
        shape((aggt.shape[0] // 2, summed_grad.shape[1] + VPAD), BF16),
        vmem(4),
        vmem(1)[0],
        [],
        (10**9, 4 * 10**6),
        (grad, summed_grad, aggt, hidt),
    )


def call_merge(mine, theirs, after):
    return call(
        merge_kernel,
        "merge",
        shape(mine.shape, BF16),
        vmem(2) + anywhere(1),
        hbm(1)[0],
        scratch(mine) + [sems(4)],
        (10**6, 4 * 10**6),
        (mine, theirs, after),
    )


def call_rows(cft, summed_grad, local):
    send = shape((local, HALO, summed_grad.shape[1]), BF16)
    return call(
        rows_kernel,
        "rows",
        (send, send),
        vmem(2),
        tuple(hbm(2)),
        scratch(send, send) + [sems(2, local)],
        (10**9, 3 * 10**6),
        (cft, summed_grad),
    )


def call_plane(got, ens):
    out_shape = shape((ens, 2, got.shape[1] // 2, got.shape[2]), BF16)
    return call(
        plane_kernel,
        "plane",
        out_shape,
        vmem(1),
        hbm(1)[0],
        [pltpu.VMEM((2,) + out_shape.shape[2:], BF16), sems(2, ens)],
        (10**6, 10**6),
        (got,),
    )


def call_score(where, codes, truth):
    local, _, points = codes[0].shape
    return call(
        score_kernel,
        "score",
        shape(truth.shape, F32),
        smem(1) + anywhere(len(codes)) + hbm(1),
        vmem(1)[0],
        [pltpu.VMEM((len(codes),) + codes[0].shape, jnp.int16)]
        + scratch(truth)
        + [pltpu.VMEM((local * len(codes), VUSE, points), F32), sems(len(codes) + 1)],
        (10**7, 10**6),
        (where, *codes, truth),
        LARGE,
    )


def call_latent(cft, summed_grad, weight, core_grad, far_grad, near_grad):
    local, rows, depth = core_grad.shape
    return call(
        latent_kernel,
        "latent",
        shape(core_grad.shape, BF16),
        hbm(3) + anywhere(3),
        hbm(1)[0],
        [pltpu.VMEM((HALO, cft.shape[1]), BF16)]
        + scratch(summed_grad, weight, core_grad, far_grad, near_grad)
        + [pltpu.VMEM((local * rows, depth), BF16)]
        + scratch(core_grad)
        + [sems(6), sems(depth // TILE)],
        (10**9, 5 * 10**6),
        (cft, summed_grad, weight, core_grad, far_grad, near_grad),
        LARGE,
    )


def call_final(got, nvar, scaling):
    per = got.shape[1]
    return call(
        functools.partial(final_kernel, scaling=scaling),
        "final",
        (shape((per, got.shape[2] - VPAD), F32), shape((per, nvar), F32)),
        vmem(1),
        tuple(vmem(2)),
        [],
        (10**5, 4 * 10**5),
        (got,),
    )


def make_body(count):
    odd_pairs = [(i, (i + 1) % count if i % 2 else (i - 1) % count) for i in range(count)]
    far = [p for p in odd_pairs if abs(p[0] - p[1]) > 1 or p[0] // 32 != p[1] // 32]
    near = [p for p in odd_pairs if p not in far]
    swap = [(0, 1), (1, 0)]

    def body(
        latent, src_weight, decoder_projection, truth, area_weight, var_weight,
        edge_src, edge_dst, edge_weight, edge_count,
    ):
        local, rows, depth = latent.shape
        ens = lax.axis_size("ens")
        members = local * ens
        nvar = decoder_projection.shape[1]
        points = truth.shape[1]
        per = depth // count
        where = jnp.stack([lax.axis_index("core"), lax.axis_index("ens")]).astype(jnp.int32)

        odd_lat = lax.ppermute(latent, SPACE, odd_pairs).reshape(local * rows, depth)
        core_lat = lax.ppermute(latent, "core", swap)
        dpt = jnp.pad(decoder_projection.T, ((0, VPAD - nvar), (0, 0)))
        cf, cft, cfo, part = call_prepare(
            where, edge_count, edge_src, edge_dst, edge_weight, latent, core_lat, src_weight
        )
        var_row = jnp.pad(var_weight, (0, VPAD - nvar)).reshape(1, VPAD)
        area_row = area_weight.reshape(1, points)
        summed, hidden, coded = call_forward(odd_lat, src_weight, cfo, part, dpt)
        order = sorted(range(1, ens), key=lambda k: -min(k, ens - k))
        moved = {
            k: lax.ppermute(coded, "ens", [((e + k) % ens, e) for e in range(ens)])
            for k in order
        }
        codes = [coded] + [moved[k] for k in range(1, ens)]
        aggt, hidt, slope = call_factors(
            where, latent, core_lat, odd_lat, cf, summed, hidden
        )
        theirs, summed_grad, grad = call_backward(
            where, codes, truth, var_row, area_row, dpt, aggt, hidt, slope
        )
        theirs = lax.ppermute(theirs, "core", swap)
        mine = call_mine(grad, summed_grad, aggt, hidt)
        core_send, odd_send = call_rows(cft, summed_grad, local)
        near_grad = lax.ppermute(odd_send, SPACE, near)
        part = call_merge(mine, theirs, odd_send)
        part, odd_send, core_send = lax.optimization_barrier((part, odd_send, core_send))
        part = part.reshape(16, 2 * per, part.shape[1])
        got = lax.all_to_all(part, ("x", "y"), 0, 0, tiled=True)
        far_grad = lax.ppermute(odd_send, SPACE, far)
        core_grad = lax.ppermute(core_send, "core", swap)
        plane = call_plane(got, ens).reshape(2 * ens, per, got.shape[2])
        got = lax.all_to_all(plane, ("ens", "zhi"), 0, 0, tiled=True)
        score = call_score(where, codes, truth)
        grad_latent = call_latent(cft, summed_grad, src_weight, core_grad, far_grad, near_grad)
        scaling = 1.0 / math.sqrt(members * points * count)
        grad_src, grad_out = call_final(got, nvar, scaling)
        return score, grad_latent, grad_src, grad_out

    return body


def solution(mesh):
    fine = jax.sharding.Mesh(
        mesh.devices.reshape(mesh.devices.shape[0], 2, 4, 4, 2), ("ens",) + SPACE
    )
    return jax.shard_map(
        make_body(mesh.devices.shape[1]),
        mesh=fine,
        in_specs=(
            P("ens", SPACE, None), P(), P(), P(None, SPACE), P(SPACE), P(),
            P(SPACE, None), P(SPACE, None), P(SPACE, None), P(SPACE),
        ),
        out_specs=(P(None, SPACE), P("ens", SPACE, None), P(SPACE, None), P(SPACE, None)),
        check_vma=False,
    )
```
